32 devices in a mesh: groups: 2 (over x), tensor: 8 (over z, y), batch: 2 (over core).
Axes of the slice: x: 2, y: 2, z: 4, core: 2. Of those that a mesh axis runs over, the one named last changes fastest.
Arguments:
- token_ids: int32 [4, 256], P(None, ('groups', 'batch')), parts along dimension 1, may hold values from 0 to 511
- embed: bfloat16 [512, 8192], P(None, 'tensor')
- norm_gain: bfloat16 [8192], P('tensor'), may hold values from 0.099609375 to 1.8984375
- w_in: bfloat16 [8192, 24576], P(None, 'tensor'), may hold values from -0.0625 to 0.0625
- filters: bfloat16 [8192, 128], P('tensor'), may hold values from -0.59765625 to 0.59765625
- w_out: bfloat16 [8192, 8192], P('tensor'), may hold values from -0.09375 to 0.09375
- cache_rows: bfloat16 [256, 127, 8192], P(('groups', 'tensor', 'batch')), parts along dimension 0, may hold values from -6 to 6
- owner: int32 [256], P('groups'), parts along dimension 0, may hold values from 0 to 127, as said below
- lengths: int32 [256], P(('groups', 'batch')), parts along dimension 0, may hold values from 8 to 255
Outputs:
- block_out: bfloat16 [4, 256, 8192], P(None, ('groups', 'batch'), 'tensor'), parts along dimension 1
The draws below stay inside these ranges and needn't reach their ends.
There are 2 independent parts, one for each index of `groups`. The reference program is written for one: setup_inputs(seed, part) draws one part's arguments, and reference() takes and returns one part's arrays. A program takes and returns all parts, laid end to end along the dimension named above; an argument that names none is the same for every part. Nothing has to cross between parts.
Inputs may be any that keep to these rules, and one draw needn't show every extreme that they name: owner names every sequence exactly once; the prefill rows come in aligned blocks of 8 rows, and block k holds only sequences k % 2 * 64 to k % 2 * 64 + 63.
All inputs are finite; a program needn't handle non-finite values.
Results may differ from the reference program's by a relative error of at most 0.0046.
Values may be sent and summed in bfloat16 or wider, within the bound.
No kernel may reach another device: no remote copies, remote signals or barrier semaphores. Data moves between devices by JAX's collectives and lax.ppermute only.
A program may use at most 256 MiB of HBM per device.

```python
import jax
import jax.numpy as jnp
from jax import lax

D = 8192
VOCAB = 512
TAPS = 128
STEPS = 4
SEQ_DEV = 64
SEQS = 128
N_TENSOR = 8
N_BATCH = 2


def draw_embed(key, part):
    key = jax.random.fold_in(key, 11)
    key_base = jax.random.fold_in(key, 1)
    key_cols = jax.random.fold_in(key, 2)
    key_rows = jax.random.fold_in(key, 3)
    ramp = jnp.arange(D, dtype=jnp.float32) / D
    column_scale = jnp.exp(1.0986 * ramp + jax.random.uniform(key_cols, (D,), minval=-1.0, maxval=1.0))
    row_scale = jnp.exp(jax.random.uniform(key_rows, (VOCAB, 1), minval=-1.0, maxval=1.0))
    base = jax.random.normal(key_base, (VOCAB, D))
    return (0.5 * base * column_scale * row_scale).astype(jnp.bfloat16)


def draw_owner(key, part):
    key = jax.random.fold_in(key, 5)
    half_keys = jax.random.split(key, N_BATCH)
    orders = jax.vmap(lambda single: jax.random.permutation(single, SEQ_DEV))(half_keys)
    block_rows = SEQ_DEV // N_TENSOR
    row_index = jnp.arange(SEQ_DEV * N_BATCH, dtype=jnp.int32)
    half_index = row_index // block_rows % N_BATCH
    position = row_index // (block_rows * N_BATCH) * block_rows + row_index % block_rows
    return (half_index * SEQ_DEV + orders[half_index, position]).astype(jnp.int32)


def with_ends(array, rng, low, high):
    extent = array.shape
    index_at = [jax.random.randint(jax.random.fold_in(rng, axis), (), 0, extent[axis]) for axis in range(len(extent))]
    array = array.at[tuple(index_at)].set(low)
    longest = extent.index(max(extent))
    index_at[longest] = (index_at[longest] + 1) % extent[longest]
    return array.at[tuple(index_at)].set(high)


def spiked(drawn, own_key, source, target, parts, factor):
    def block_of(dim):
        return (jnp.arange(drawn.shape[dim]) // (drawn.shape[dim] // parts)).reshape((-1,) + (1,) * (drawn.ndim - 1 - dim))

    one_side = jax.random.permutation(own_key, parts)[block_of(target)]
    other_side = (block_of(target) + parts // 2) % parts
    return jnp.where((block_of(source) == one_side) | (block_of(source) == other_side), factor * drawn, drawn)


def shard_levels(stream_key, extent, cuts, least, high):
    def one(dim, blocks):
        heights = jax.random.uniform(jax.random.fold_in(jax.random.fold_in(stream_key, 6), dim), (blocks,), jnp.float32, least / len(cuts), high / len(cuts))
        return jnp.repeat(jnp.exp(heights), extent[dim] // blocks).reshape((-1,) + (1,) * (len(extent) - dim - 1))

    loudness = one(*cuts[0])
    for cut in cuts[1:]:
        loudness = loudness * one(*cut)
    return loudness


def scatter_about(own_key, dims, scale, limit, cuts=(), held_as=jnp.bfloat16):
    gain = shard_levels(own_key, dims, cuts, -0.22, 0.18) if cuts else 1.0
    values = jax.random.normal(own_key, dims, jnp.float32) * scale * gain
    return jnp.minimum(jnp.maximum(values, -limit), limit).astype(held_as)


def gaussian_with(stream_key, shape, scale, most, cuts, heavy, kind=jnp.bfloat16):
    result = scale * jax.random.normal(stream_key, shape, jnp.float32)
    if cuts:
        result = result * shard_levels(stream_key, shape, cuts, -0.22, 0.18)
    return jnp.clip(spiked(result, jax.random.fold_in(stream_key, 3), *heavy), -most, most).astype(kind)


def setup_inputs(seed: int = 0, part: int = 0) -> dict:
    keys = jax.random.split(jax.random.key(seed), 10)
    part_splits = jax.random.split(jax.random.fold_in(keys[9], part), 10)
    token_ids = with_ends(jax.random.randint(part_splits[0], (STEPS, SEQS), 0, VOCAB), jax.random.fold_in(part_splits[0], 1), 0, VOCAB - 1).astype(jnp.int32)
    embed = draw_embed(jax.random.fold_in(keys[9], 71), part)
    norm_gain = jnp.clip(1.0 + 0.18 * jax.random.normal(keys[2], (D,), jnp.float32), 0.099609375, 1.8984375).astype(jnp.bfloat16)
    w_in = scatter_about(keys[3], (D, 3 * D), D ** -0.5, 0.0625, ((1, 8),))
    filters = scatter_about(keys[4], (D, TAPS), 0.1, 0.59765625, ((0, 8),))
    w_out = gaussian_with(keys[5], (D, D), D ** -0.5, 0.09375, ((0, 8),), (0, 1, 8, 2.0))
    cache_rows = scatter_about(part_splits[6], (SEQS, TAPS - 1, D), 1.0, 6.0, ((0, 16),))
    owner = draw_owner(jax.random.fold_in(jax.random.fold_in(keys[9], part), 71), part)
    lengths = with_ends(jax.random.randint(part_splits[8], (SEQS,), 8, 256), jax.random.fold_in(part_splits[8], 1), 8, 255).astype(jnp.int32)
    return {"token_ids": token_ids, "embed": embed, "norm_gain": norm_gain, "w_in": w_in, "filters": filters, "w_out": w_out, "cache_rows": cache_rows, "owner": owner, "lengths": lengths}


EPSILON = 1e-05

def shifted_taps(filters, count):
    width = filters.shape[1]
    padded = jnp.concatenate([filters.astype(jnp.float32), jnp.zeros((filters.shape[0], count), jnp.float32)], axis=1)
    return jnp.stack([padded[:, offset + 1:offset + width].T for offset in range(count)])

def reference(token_ids, embed, norm_gain, w_in, filters, w_out, cache_rows, owner, lengths):
    placed = jnp.zeros((SEQS,), jnp.int32).at[owner].set(jnp.arange(SEQS, dtype=jnp.int32))
    tap_table = shifted_taps(filters, STEPS)
    lag_index = jnp.arange(TAPS - 1, dtype=jnp.int32)

    def one_sequence(inputs):
        row_index, seq_length = inputs
        cached = lax.dynamic_index_in_dim(cache_rows, row_index, 0, keepdims=False)
        masked = jnp.where((lag_index < seq_length)[:, None], cached.astype(jnp.float32), 0.0)
        return jnp.einsum('mc,tmc->tc', masked, tap_table, precision=lax.Precision.HIGHEST)
    history = lax.map(one_sequence, (placed, lengths))
    channels = D // N_TENSOR
    tap_values = filters.astype(jnp.float32)
    gain_values = norm_gain.astype(jnp.float32)
    recent = []
    outputs = []
    for position in range(STEPS):
        stream = embed[token_ids[position]].astype(jnp.float32)
        inv_rms = lax.rsqrt(lax.optimization_barrier(jnp.sum(stream * stream, axis=1)) / D + EPSILON)
        normed = (stream * inv_rms[:, None] * gain_values).astype(jnp.bfloat16)
        projected = jnp.dot(normed, w_in, preferred_element_type=jnp.float32).reshape(SEQS, N_TENSOR, 3, channels)
        queries = projected[:, :, 0].reshape(SEQS, D)
        keys_part = projected[:, :, 1].reshape(SEQS, D)
        values_part = projected[:, :, 2].reshape(SEQS, D)
        recent.append((keys_part * values_part).astype(jnp.bfloat16))
        filtered = history[:, position]
        for lag_back in range(position + 1):
            filtered = filtered + tap_values[:, lag_back] * recent[position - lag_back].astype(jnp.float32)
        gated_rows = (queries * filtered).astype(jnp.bfloat16)
        summed = jnp.dot(gated_rows, w_out, preferred_element_type=jnp.float32)
        outputs.append((stream + summed).astype(jnp.bfloat16))
    return jnp.stack(outputs)
```

```python
import functools

import jax
import jax.numpy as jnp
from jax import lax
from jax.experimental import pallas as pl
from jax.experimental.pallas import tpu as pltpu
from jax.sharding import PartitionSpec as P

D = 8192
EPSILON = 1e-05
LANES = 128
SUBLANES = 8
PACKED = 16
VMEM_LIMIT = 56 * 1024 * 1024


def history_kernel(steps, lags, row_lengths, taps_ref, cache_ref, out_ref, taps_scr):
    rows, _, channels = cache_ref.shape
    width = taps_scr.shape[0] - PACKED
    taps_scr[pl.ds(0, width), :] = taps_ref[0, pl.ds(0, width), :].astype(jnp.float32)
    taps_scr[pl.ds(width, PACKED), :] = jnp.zeros((PACKED, channels), jnp.float32)
    lag_index = lax.broadcasted_iota(jnp.int32, (PACKED, LANES), 0)

    def one_chunk(chunk, carry):
        at = pl.ds(pl.multiple_of(chunk * LANES, LANES), LANES)
        sums = [[jnp.zeros((SUBLANES, LANES), jnp.float32) for _ in range(rows)] for _ in range(steps)]
        for first in range(0, lags, PACKED):
            taps = [taps_scr[pl.ds(first + 1 + step, PACKED), at] for step in range(steps)]
            count = min(PACKED, lags - first)
            for row in range(rows):
                values = cache_ref[row, pl.ds(first, count), at].astype(jnp.float32)
                if count < PACKED:
                    values = jnp.concatenate(
                        [values, jnp.zeros((PACKED - count, LANES), jnp.float32)], axis=0
                    )
                values = jnp.where(lag_index < row_lengths[row] - first, values, 0.0)
                for step in range(steps):
                    terms = values * taps[step]
                    sums[step][row] += terms[:SUBLANES] + terms[SUBLANES:]
        for step in range(steps):
            totals = [jnp.sum(sums[step][row], axis=0, keepdims=True) for row in range(rows)]
            out_ref[0, step, :, at] = jnp.concatenate(totals, axis=0).astype(out_ref.dtype)
        return carry

    lax.fori_loop(0, channels // LANES, one_chunk, 0)


def history_terms(cache_rows, taps_all, row_lengths, steps):
    rows, lags, width = cache_rows.shape
    owners, tap_rows, channels = taps_all.shape
    return pl.pallas_call(
        functools.partial(history_kernel, steps, lags),
        grid_spec=pltpu.PrefetchScalarGridSpec(
            num_scalar_prefetch=1,
            grid=(owners,),
            in_specs=[
                pl.BlockSpec((1, tap_rows, channels), lambda block, _: (block, 0, 0)),
                pl.BlockSpec((rows, lags, channels), lambda block, _: (0, 0, block)),
            ],
            out_specs=pl.BlockSpec((1, steps, rows, channels), lambda block, _: (block, 0, 0, 0)),
            scratch_shapes=[pltpu.VMEM((lags + 1 + PACKED, channels), jnp.float32)],
        ),
        out_shape=jax.ShapeDtypeStruct((owners, steps, rows, channels), jnp.bfloat16),
        compiler_params=pltpu.CompilerParams(vmem_limit_bytes=VMEM_LIMIT),
        cost_estimate=pl.CostEstimate(
            flops=2 * steps * rows * lags * width,
            bytes_accessed=2 * rows * lags * width,
            transcendentals=0,
        ),
        name="history_terms",
    )(row_lengths, taps_all, cache_rows)


def gate_kernel(steps, shards, x_ref, wq_ref, wk_ref, wv_ref, taps_ref, hist_ref, out_ref, acc):
    part = pl.program_id(1)
    channels = x_ref.shape[2]

    @pl.when(part == 0)
    def _():
        acc[...] = jnp.zeros_like(acc)

    for index, w_ref in enumerate((wq_ref, wk_ref, wv_ref)):
        total = acc[index]
        for shard in range(shards):
            total += jnp.dot(
                x_ref[part * shards + shard],
                w_ref[pl.ds(shard * channels, channels), :],
                preferred_element_type=jnp.float32,
            )
        acc[index] = total

    @pl.when(part == pl.num_programs(1) - 1)
    def _():
        seqs = out_ref.shape[0] // steps
        recent = (acc[1] * acc[2]).astype(jnp.bfloat16)
        for step in range(steps):
            at = pl.ds(step * seqs, seqs)
            filtered = hist_ref[at, :]
            for back in range(step + 1):
                older = recent[(step - back) * seqs : (step - back + 1) * seqs]
                filtered += taps_ref[pl.ds(back, 1), :].astype(jnp.float32) * older.astype(jnp.float32)
            out_ref[at, :] = (acc[0, at, :] * filtered).astype(jnp.bfloat16)


def gated_rows(normed, w_in, taps, history, steps):
    owners, rows, channels = normed.shape
    block = min(256, channels)
    blocks = channels // block
    shards = max(1, min(owners, 2048 // channels))
    weights = [
        pl.BlockSpec((shards * channels, block), functools.partial(lambda first, c, k: (k, first + c), index * blocks))
        for index in range(3)
    ]
    return pl.pallas_call(
        functools.partial(gate_kernel, steps, shards),
        grid=(blocks, owners // shards),
        in_specs=[
            pl.BlockSpec((owners, rows, channels), lambda c, k: (0, 0, 0)),
            *weights,
            pl.BlockSpec((PACKED, block), lambda c, k: (0, c)),
            pl.BlockSpec((rows, block), lambda c, k: (0, c)),
        ],
        out_specs=pl.BlockSpec((rows, block), lambda c, k: (0, c)),
        out_shape=jax.ShapeDtypeStruct((rows, channels), jnp.bfloat16),
        scratch_shapes=[pltpu.VMEM((3, rows, block), jnp.float32)],
        compiler_params=pltpu.CompilerParams(vmem_limit_bytes=VMEM_LIMIT),
        cost_estimate=pl.CostEstimate(
            flops=2 * rows * w_in.shape[0] * w_in.shape[1],
            bytes_accessed=2 * w_in.shape[0] * w_in.shape[1],
            transcendentals=0,
        ),
        name="gated_rows",
    )(normed, w_in, w_in, w_in, taps, history)


def share_kernel(x_ref, w_ref, out_ref):
    out_ref[0] = jnp.dot(x_ref[...], w_ref[...], preferred_element_type=jnp.float32).astype(
        out_ref.dtype
    )


def output_shares(gated, w_out, owners):
    rows, channels = gated.shape
    block = w_out.shape[1] // owners
    return pl.pallas_call(
        share_kernel,
        grid=(owners,),
        in_specs=[
            pl.BlockSpec((rows, channels), lambda n: (0, 0)),
            pl.BlockSpec((channels, block), lambda n: (0, n)),
        ],
        out_specs=pl.BlockSpec((1, rows, block), lambda n: (n, 0, 0)),
        out_shape=jax.ShapeDtypeStruct((owners, rows, block), jnp.bfloat16),
        compiler_params=pltpu.CompilerParams(vmem_limit_bytes=VMEM_LIMIT),
        cost_estimate=pl.CostEstimate(
            flops=2 * rows * channels * w_out.shape[1],
            bytes_accessed=2 * channels * w_out.shape[1],
            transcendentals=0,
        ),
        name="output_shares",
    )(gated, w_out)


def per_device(token_ids, embed, norm_gain, w_in, filters, w_out, cache_rows, owner, lengths):
    steps, seqs = token_ids.shape
    vocab, channels = embed.shape
    rows = cache_rows.shape[0]
    taps = filters.shape[1]
    owners = lax.axis_size("tensor")
    halves = lax.axis_size("batch")
    mine = lax.axis_index("tensor")
    half = lax.axis_index("batch")

    small = jnp.concatenate(
        [filters.T, norm_gain[None, :], jnp.zeros((PACKED - 1, channels), jnp.bfloat16)], axis=0
    )
    small_all = lax.all_gather(small, "tensor")

    onehot = token_ids.reshape(-1)[:, None] == jnp.arange(vocab, dtype=jnp.int32)[None, :]
    stream = jnp.dot(onehot.astype(jnp.bfloat16), embed, preferred_element_type=jnp.float32)
    stream_all = lax.all_gather(stream.astype(jnp.bfloat16), "tensor")

    owner_grid = owner.reshape(owners, halves, rows)
    arrived = lax.dynamic_index_in_dim(owner_grid, half, 1, keepdims=False) - half * seqs
    own = lax.dynamic_index_in_dim(arrived, mine, 0, keepdims=False)
    seq_index = jnp.arange(seqs, dtype=jnp.int32)
    row_lengths = jnp.sum(jnp.where(own[:, None] == seq_index[None, :], lengths[None, :], 0), axis=1)

    history = history_terms(cache_rows, small_all, row_lengths, steps)
    history = lax.all_to_all(history, "tensor", 0, 0, tiled=True)
    step_index = jnp.arange(steps, dtype=jnp.int32)
    place = (
        (step_index[:, None, None, None, None] == step_index[None, None, None, :, None])
        & (seq_index[None, :, None, None, None] == arrived[None, None, :, None, :])
    ).reshape(steps * seqs, owners * steps * rows)
    history = jnp.dot(
        place.astype(jnp.bfloat16),
        history.reshape(owners * steps * rows, channels),
        preferred_element_type=jnp.float32,
    )

    wide = stream_all.astype(jnp.float32)
    inv_rms = lax.rsqrt(jnp.sum(wide * wide, axis=(0, 2)) / D + EPSILON)
    gain = small_all[:, taps, :].astype(jnp.float32)
    normed = (wide * inv_rms[None, :, None] * gain[:, None, :]).astype(jnp.bfloat16)

    gated = gated_rows(normed, w_in, small, history, steps)
    shares = lax.all_to_all(output_shares(gated, w_out, owners), "tensor", 0, 0, tiled=True)
    summed = jnp.sum(shares.astype(jnp.float32), axis=0)
    return (stream + summed).astype(jnp.bfloat16).reshape(steps, seqs, channels)


def solution(mesh):
    in_specs = (
        P(None, ("groups", "batch")),
        P(None, "tensor"),
        P("tensor"),
        P(None, "tensor"),
        P("tensor", None),
        P("tensor", None),
        P(("groups", "tensor", "batch"), None, None),
        P("groups"),
        P(("groups", "batch")),
    )
    out_specs = P(None, ("groups", "batch"), "tensor")
    return jax.shard_map(
        per_device, mesh=mesh, in_specs=in_specs, out_specs=out_specs, check_vma=False
    )
```

```python
import functools

import jax
import jax.numpy as jnp
from jax import lax
from jax.experimental import pallas as pl
from jax.experimental.pallas import tpu as pltpu
from jax.sharding import PartitionSpec as P

D = 8192
EPSILON = 1e-05
LANES = 128
PACKED = 16
INNER = 2
RING_MOST = 8
VMEM_LIMIT = 28 * 1024 * 1024


def place_of(mine, owners):
    return mine // INNER, mine % INNER, owners // INNER


def moved(array, outer_by, flip):
    owners = lax.axis_size("tensor")
    outer_size = owners // INNER
    pairs = []
    for source in range(owners):
        outer, inner = source // INNER, source % INNER
        pairs.append((source, (outer + outer_by) % outer_size * INNER + (inner ^ flip)))
    return lax.ppermute(array, "tensor", pairs)


def spread(block):
    outer_size = lax.axis_size("tensor") // INNER
    blocks = []
    held = block
    for step in range(outer_size):
        if step:
            held = moved(held, 1, 0)
        blocks.append((held, moved(held, 0, 1)))
    return blocks


def history_kernel(steps, spot, lengths_ref, near_ref, far_ref, cache_ref, near_out, far_out, taps_scr):
    lags, rows, channels = cache_ref.shape
    part = pl.program_id(0)
    parts = pl.num_programs(0) // 2
    width = min(4 * LANES, channels)
    at_part = pl.ds(pl.multiple_of(part % parts * channels, channels), channels)

    @pl.when(part < parts)
    def _():
        taps_scr[...] = near_ref[pl.ds(0, lags + 1), at_part].astype(jnp.float32)

    @pl.when(part >= parts)
    def _():
        taps_scr[...] = far_ref[pl.ds(0, lags + 1), at_part].astype(jnp.float32)

    lengths = jnp.concatenate([lengths_ref[...]] * (width // LANES), axis=1)

    def one_chunk(chunk, carry):
        at = pl.ds(pl.multiple_of(chunk * width, width), width)
        taps = [
            jnp.broadcast_to(taps_scr[pl.ds(1 + step, 1), at], (rows, width)) for step in range(steps)
        ]
        sums = [jnp.zeros((rows, width), jnp.float32) for _ in range(steps)]
        for lag in range(lags):
            values = jnp.where(lengths > lag, cache_ref[lag, :, at].astype(jnp.float32), 0.0)
            for step in range(min(steps, lags - lag)):
                sums[step] += values * taps[step]
            taps = taps[1:]
            if lag + 1 + steps <= lags:
                taps.append(
                    jnp.broadcast_to(taps_scr[pl.ds(lag + 1 + steps, 1), at], (rows, width))
                )

        @pl.when(part < parts)
        def _():
            for step in range(steps):
                near_out[step, :, at] = sums[step].astype(near_out.dtype)

        @pl.when(part >= parts)
        def _():
            for step in range(steps):
                far_out[step, :, at] = sums[step].astype(far_out.dtype)

        return carry

    lax.fori_loop(0, channels // width, one_chunk, 0)


def history_terms(cache, near, far, lengths, spot, steps):
    lags, rows, _ = cache.shape
    tap_rows, channels = near.shape
    parts = 2 if channels >= 8 * LANES else 1
    block = channels // parts

    def cache_at(part, spot):
        inner = (spot[1] + part // parts) % INNER
        return 0, 0, (spot[0] * INNER + inner) * parts + part % parts

    return pl.pallas_call(
        functools.partial(history_kernel, steps),
        grid_spec=pltpu.PrefetchScalarGridSpec(
            num_scalar_prefetch=1,
            grid=(2 * parts,),
            in_specs=[
                pl.BlockSpec((rows, LANES), lambda part, _: (0, 0)),
                pl.BlockSpec((tap_rows, channels), lambda part, _: (0, 0)),
                pl.BlockSpec((tap_rows, channels), lambda part, _: (0, 0)),
                pl.BlockSpec((lags, rows, block), cache_at),
            ],
            out_specs=[
                pl.BlockSpec((steps, rows, block), lambda part, _: (0, 0, jnp.minimum(part, parts - 1))),
                pl.BlockSpec((steps, rows, block), lambda part, _: (0, 0, jnp.maximum(part - parts, 0))),
            ],
            scratch_shapes=[pltpu.VMEM((lags + 1, block), jnp.float32)],
        ),
        out_shape=[jax.ShapeDtypeStruct((steps, rows, channels), jnp.bfloat16)] * 2,
        compiler_params=pltpu.CompilerParams(vmem_limit_bytes=VMEM_LIMIT),
        cost_estimate=pl.CostEstimate(
            flops=4 * steps * rows * lags * channels,
            bytes_accessed=4 * rows * lags * channels,
            transcendentals=0,
        ),
        name="history_terms",
    )(spot, lengths, near, far, cache)


def project_kernel(steps, first, last, *refs):
    refs = list(refs)
    spot, near, far, near_gain, far_gain, inv_ref, wq_ref, wk_ref, wv_ref = refs[:9]
    del refs[:9]
    earlier = None if first else refs.pop(0)
    taps_ref, hist_ref = (refs.pop(0), refs.pop(0)) if last else (None, None)
    out_ref, normed = refs
    rows, channels = near.shape

    @pl.when(pl.program_id(0) == 0)
    def _():
        inv_rms = inv_ref[:, :1]
        for flip, x_ref, gain_ref in ((0, near, near_gain), (1, far, far_gain)):
            gain = gain_ref[pl.ds(0, 1), :].astype(jnp.float32)
            scaled = x_ref[...].astype(jnp.float32) * inv_rms * gain
            normed[(spot[1] + flip) % INNER] = scaled.astype(jnp.bfloat16)

    totals = []
    for index, w_ref in enumerate((wq_ref, wk_ref, wv_ref)):
        total = None if first else earlier[index]
        for inner in range(INNER):
            term = jnp.dot(
                normed[inner],
                w_ref[pl.ds(inner * channels, channels), :],
                preferred_element_type=jnp.float32,
            )
            total = term if total is None else total + term
        totals.append(total)
    if not last:
        for index in range(3):
            out_ref[index] = totals[index]
        return
    seqs = rows // steps
    queries = totals[0]
    recent = (totals[1] * totals[2]).astype(jnp.bfloat16).astype(jnp.float32)
    for step in range(steps):
        filtered = hist_ref[pl.ds(step * seqs, seqs), :]
        for back in range(step + 1):
            older = recent[(step - back) * seqs : (step - back + 1) * seqs]
            filtered += taps_ref[pl.ds(back, 1), :].astype(jnp.float32) * older
        out_ref[pl.ds(step * seqs, seqs), :] = (
            queries[step * seqs : (step + 1) * seqs] * filtered
        ).astype(jnp.bfloat16)


def projected(spot, pair, gains, inv_rms, w_in, earlier, taps=None, history=None, steps=1):
    near, far = pair
    rows, channels = near.shape
    block = min(256, channels)
    blocks = channels // block
    first, last = earlier is None, history is not None
    tap_rows = gains[0].shape[0]
    in_specs = [
        pl.BlockSpec((rows, channels), lambda c, _: (0, 0)),
        pl.BlockSpec((rows, channels), lambda c, _: (0, 0)),
        pl.BlockSpec((PACKED, channels), lambda c, _: (tap_rows // PACKED - 1, 0)),
        pl.BlockSpec((PACKED, channels), lambda c, _: (tap_rows // PACKED - 1, 0)),
        pl.BlockSpec((rows, LANES), lambda c, _: (0, 0)),
    ]
    for index in range(3):
        in_specs.append(
            pl.BlockSpec(
                (INNER * channels, block),
                functools.partial(lambda start, c, spot: (spot[0], start + c), index * blocks),
            )
        )
    args = [near, far, *gains, inv_rms, w_in, w_in, w_in]
    total_spec = pl.BlockSpec((3, rows, block), lambda c, _: (0, 0, c))
    if not first:
        in_specs.append(total_spec)
        args.append(earlier)
    if last:
        in_specs += [
            pl.BlockSpec((PACKED, block), lambda c, _: (0, c)),
            pl.BlockSpec((rows, block), lambda c, _: (0, c)),
        ]
        args += [taps, history]
        out_spec = pl.BlockSpec((rows, block), lambda c, _: (0, c))
        out_shape = jax.ShapeDtypeStruct((rows, channels), jnp.bfloat16)
    else:
        out_spec = total_spec
        out_shape = jax.ShapeDtypeStruct((3, rows, channels), jnp.float32)
    return pl.pallas_call(
        functools.partial(project_kernel, steps, first, last),
        grid_spec=pltpu.PrefetchScalarGridSpec(
            num_scalar_prefetch=1,
            grid=(blocks,),
            in_specs=in_specs,
            out_specs=out_spec,
            scratch_shapes=[pltpu.VMEM((INNER, rows, channels), jnp.bfloat16)],
        ),
        out_shape=out_shape,
        compiler_params=pltpu.CompilerParams(vmem_limit_bytes=VMEM_LIMIT),
        cost_estimate=pl.CostEstimate(
            flops=2 * rows * INNER * channels * 3 * channels,
            bytes_accessed=2 * INNER * channels * 3 * channels,
            transcendentals=0,
        ),
        name="gated_rows" if last else "projected_part",
    )(spot, *args)


def share_kernel(spot, x_ref, w_ref, *refs):
    share = jnp.dot(x_ref[...], w_ref[...], preferred_element_type=jnp.float32)
    if len(refs) > 1:
        share += refs[0][...].astype(jnp.float32)
    refs[-1][...] = share.astype(refs[-1].dtype)


def output_share(spot, gated, w_out, owners, arrived=None):
    rows, channels = gated.shape
    wide = w_out.shape[1] // owners
    block = min(512, wide)
    blocks = wide // block
    specs = [
        pl.BlockSpec((rows, channels), lambda c, _: (0, 0)),
        pl.BlockSpec((channels, block), lambda c, spot: (0, spot[0] * blocks + c)),
    ]
    args = [gated, w_out]
    if arrived is not None:
        specs.append(pl.BlockSpec((rows, block), lambda c, _: (0, c)))
        args.append(arrived)
    return pl.pallas_call(
        share_kernel,
        grid_spec=pltpu.PrefetchScalarGridSpec(
            num_scalar_prefetch=1,
            grid=(blocks,),
            in_specs=specs,
            out_specs=pl.BlockSpec((rows, block), lambda c, _: (0, c)),
        ),
        out_shape=jax.ShapeDtypeStruct((rows, wide), jnp.bfloat16),
        compiler_params=pltpu.CompilerParams(vmem_limit_bytes=VMEM_LIMIT),
        cost_estimate=pl.CostEstimate(
            flops=2 * rows * channels * wide,
            bytes_accessed=2 * channels * wide,
            transcendentals=0,
        ),
        name="output_share",
    )(spot, *args)


def split_sums(values, channels):
    parts = []
    rest = values
    for _ in range(3):
        part = lax.reduce_precision(rest, 8, 7)
        parts.append(part.astype(jnp.bfloat16))
        rest = rest - part
    flat = jnp.concatenate(parts)
    count = -(-flat.shape[0] // channels)
    return jnp.pad(flat, (0, count * channels - flat.shape[0])).reshape(count, channels)


def per_device(token_ids, embed, norm_gain, w_in, filters, w_out, cache_rows, owner, lengths):
    steps, seqs = token_ids.shape
    vocab, channels = embed.shape
    rows = cache_rows.shape[0]
    taps = filters.shape[1]
    tokens = steps * seqs
    owners = lax.axis_size("tensor")
    halves = lax.axis_size("batch")
    mine = lax.axis_index("tensor")
    half = lax.axis_index("batch")
    outer, inner, outer_size = place_of(mine, owners)

    onehot = token_ids.reshape(-1)[:, None] == jnp.arange(vocab, dtype=jnp.int32)[None, :]
    stream = jnp.dot(onehot.astype(jnp.bfloat16), embed, preferred_element_type=jnp.float32)
    squares = split_sums(jnp.sum(stream * stream, axis=1), channels)
    filler = -(taps + 1 + squares.shape[0]) % PACKED
    small = jnp.concatenate(
        [filters.T, norm_gain[None, :], squares, jnp.zeros((filler, channels), jnp.bfloat16)], axis=0
    )
    smalls = spread(small)
    streams = spread(stream.astype(jnp.bfloat16))

    def spot_at(back):
        return jnp.stack([(outer + back) % outer_size, inner]).astype(jnp.int32)

    owner_grid = owner.reshape(owners, halves, rows)
    arrived = lax.dynamic_index_in_dim(owner_grid, half, 1, keepdims=False) - half * seqs
    seq_index = jnp.arange(seqs, dtype=jnp.int32)
    own = lax.dynamic_index_in_dim(arrived, mine, 0, keepdims=False)
    row_lengths = jnp.sum(jnp.where(own[:, None] == seq_index[None, :], lengths[None, :], 0), axis=1)
    row_lengths = jnp.broadcast_to(row_lengths[:, None], (rows, LANES))
    cache = cache_rows.transpose(1, 0, 2)

    pieces = []
    piece_owner = []
    for back, (near, far) in enumerate(smalls):
        terms = history_terms(cache, near, far, row_lengths, spot_at(-back), steps)
        for flip, piece in enumerate(terms):
            pieces.append(moved(piece, -back, flip) if back or flip else piece)
            piece_owner.append((outer + back) % outer_size * INNER + (inner + flip) % INNER)
    from_whom = jnp.stack(piece_owner)
    sent_rows = jnp.sum(
        jnp.where(
            (from_whom[:, None] == jnp.arange(owners)[None, :])[:, :, None], arrived[None], 0
        ),
        axis=1,
    )
    step_index = jnp.arange(steps, dtype=jnp.int32)
    place = (
        (step_index[:, None, None, None, None] == step_index[None, None, None, :, None])
        & (seq_index[None, :, None, None, None] == sent_rows[None, None, :, None, :])
    ).reshape(tokens, owners * steps * rows)
    history = jnp.dot(
        place.astype(jnp.bfloat16),
        jnp.concatenate(pieces, axis=0).reshape(owners * steps * rows, channels),
        preferred_element_type=jnp.float32,
    )

    total = 0.0
    for near, far in smalls:
        for block in (near, far):
            flat = block[taps + 1 : taps + 1 + squares.shape[0]].reshape(-1)[: 3 * tokens]
            total = total + jnp.sum(flat.astype(jnp.float32).reshape(3, tokens), axis=0)
    inv_rms = lax.rsqrt(total / D + EPSILON)
    inv_rms = jnp.broadcast_to(inv_rms[:, None], (tokens, LANES))

    sums = None
    for back in range(outer_size):
        ends = dict(taps=small, history=history, steps=steps) if back == outer_size - 1 else {}
        sums = projected(spot_at(-back), streams[back], smalls[back], inv_rms, w_in, sums, **ends)
    gated = sums

    def spot_to(ahead, flip):
        return ((outer + ahead) % outer_size * INNER + (inner + flip) % INNER)[None].astype(jnp.int32)

    order = sorted(range(outer_size), key=lambda ahead: (ahead == 0, -min(ahead, outer_size - ahead)))
    across = {
        ahead: moved(output_share(spot_to(ahead, 1), gated, w_out, owners), 0, 1) for ahead in order
    }
    out = stream
    for ahead in order:
        share = output_share(spot_to(ahead, 0), gated, w_out, owners, across[ahead])
        out = out + (moved(share, ahead, 0) if ahead else share).astype(jnp.float32)
    return out.astype(jnp.bfloat16).reshape(steps, seqs, channels)


def solution(mesh):
    in_specs = (
        P(None, ("groups", "batch")),
        P(None, "tensor"),
        P("tensor"),
        P(None, "tensor"),
        P("tensor", None),
        P("tensor", None),
        P(("groups", "tensor", "batch"), None, None),
        P("groups"),
        P(("groups", "batch")),
    )
    out_specs = P(None, ("groups", "batch"), "tensor")
    return jax.shard_map(
        per_device, mesh=mesh, in_specs=in_specs, out_specs=out_specs, check_vma=False
    )
```

```python
import functools

import jax
import jax.numpy as jnp
from jax import lax
from jax.experimental import pallas as pl
from jax.experimental.pallas import tpu as pltpu
from jax.sharding import PartitionSpec as P

D = 8192
EPSILON = 1e-05
LANES = 128
PACKED = 16
INNER = 2
VMEM_LIMIT = 28 * 1024 * 1024
LARGE_LIMIT = 46 * 1024 * 1024


def place_of(mine, owners):
    return mine // INNER, mine % INNER, owners // INNER


def moved(array, outer_by, flip):
    owners = lax.axis_size("tensor")
    outer_size = owners // INNER
    pairs = []
    for source in range(owners):
        outer, inner = source // INNER, source % INNER
        pairs.append((source, (outer + outer_by) % outer_size * INNER + (inner ^ flip)))
    return lax.ppermute(array, "tensor", pairs)


def spread(block):
    outer_size = lax.axis_size("tensor") // INNER
    blocks = []
    held = block
    for step in range(outer_size):
        if step:
            held = moved(held, 1, 0)
        blocks.append((held, moved(held, 0, 1)))
    return blocks


def history_kernel(steps, spot, lengths_ref, *refs):
    *tap_refs, cache_ref, out_ref, taps_scr = refs
    lags, rows, channels = cache_ref.shape
    width = min(4 * LANES, channels)
    for index, tap_ref in enumerate(tap_refs):

        @pl.when(pl.program_id(1) == index)
        def _():
            taps_scr[...] = tap_ref[0].astype(jnp.float32)

    lengths = jnp.concatenate([lengths_ref[...]] * (width // LANES), axis=1)

    def one_chunk(chunk, carry):
        at = pl.ds(pl.multiple_of(chunk * width, width), width)
        taps = [
            jnp.broadcast_to(taps_scr[pl.ds(1 + step, 1), at], (rows, width)) for step in range(steps)
        ]
        sums = [jnp.zeros((rows, width), jnp.float32) for _ in range(steps)]
        for lag in range(lags):
            values = jnp.where(lengths > lag, cache_ref[lag, :, at].astype(jnp.float32), 0.0)
            for step in range(min(steps, lags - lag)):
                sums[step] += values * taps[step]
            taps = taps[1:]
            if lag + 1 + steps <= lags:
                taps.append(
                    jnp.broadcast_to(taps_scr[pl.ds(lag + 1 + steps, 1), at], (rows, width))
                )
        for step in range(steps):
            out_ref[0, step, :, at] = sums[step].astype(out_ref.dtype)
        return carry

    lax.fori_loop(0, channels // width, one_chunk, 0)


def history_terms(cache, tap_parts, spot, lengths, steps):
    lags, rows, width = cache.shape
    owners, tap_rows, channels = tap_parts[0].shape
    count = len(tap_parts)
    per_owner = width // owners // channels
    tap_spec = pl.BlockSpec((1, tap_rows, channels), lambda n, part, _: (n, 0, 0))
    return pl.pallas_call(
        functools.partial(history_kernel, steps),
        grid_spec=pltpu.PrefetchScalarGridSpec(
            num_scalar_prefetch=1,
            grid=(owners, count),
            in_specs=[
                pl.BlockSpec((rows, LANES), lambda n, part, _: (0, 0)),
                *[tap_spec] * count,
                pl.BlockSpec(
                    (lags, rows, channels),
                    lambda n, part, spot: (0, 0, n * per_owner + spot[0] + (spot[1] + part) % count),
                ),
            ],
            out_specs=pl.BlockSpec(
                (1, steps, rows, channels), lambda n, part, spot: (n, 0, 0, (spot[1] + part) % count)
            ),
            scratch_shapes=[pltpu.VMEM((tap_rows, channels), jnp.float32)],
        ),
        out_shape=jax.ShapeDtypeStruct((owners, steps, rows, count * channels), jnp.bfloat16),
        compiler_params=pltpu.CompilerParams(vmem_limit_bytes=LARGE_LIMIT),
        cost_estimate=pl.CostEstimate(
            flops=2 * steps * rows * lags * owners * count * channels,
            bytes_accessed=2 * rows * lags * owners * count * channels,
            transcendentals=0,
        ),
        name="history_terms",
    )(spot, lengths, *tap_parts, cache)


def project_kernel(steps, first, last, spot, near, far, gain_ref, inv_ref, w_ref, *refs):
    refs = list(refs)
    if not first:
        refs.pop(0)
    taps_ref, hist_ref = (refs.pop(0), refs.pop(0)) if last else (None, None)
    total_ref = refs.pop(0)
    gated_ref = refs.pop(0) if last else None
    (normed,) = refs
    rows, channels = near.shape
    depth, width = w_ref.shape
    block = min(512, channels)
    part = pl.program_id(0)
    parts = channels // depth
    inner = part // parts
    at = pl.ds(pl.multiple_of(part % parts * depth, depth), depth)
    scale = inv_ref[:, :1]
    gain = gain_ref[pl.ds(spot[0] * INNER + inner, 1), at]

    @pl.when(inner == spot[1])
    def _():
        normed[...] = (near[:, at].astype(jnp.float32) * scale * gain).astype(jnp.bfloat16)

    @pl.when(inner != spot[1])
    def _():
        normed[...] = (far[:, at].astype(jnp.float32) * scale * gain).astype(jnp.bfloat16)

    if first:

        @pl.when(part == 0)
        def _():
            total_ref[...] = jnp.zeros_like(total_ref)

    for start in range(0, width, block):
        columns = pl.ds(start, block)
        total_ref[:, columns] += jnp.dot(
            normed[...], w_ref[:, columns], preferred_element_type=jnp.float32
        )
    if not last:
        return

    @pl.when(part == pl.num_programs(0) - 1)
    def _():
        seqs = rows // steps
        for start in range(0, channels, LANES):
            columns = pl.ds(start, LANES)
            keys = total_ref[:, pl.ds(channels + start, LANES)]
            values = total_ref[:, pl.ds(2 * channels + start, LANES)]
            recent = (keys * values).astype(jnp.bfloat16).astype(jnp.float32)
            for step in range(steps):
                at_step = pl.ds(step * seqs, seqs)
                filtered = hist_ref[at_step, columns]
                for back in range(step + 1):
                    older = recent[(step - back) * seqs : (step - back + 1) * seqs]
                    filtered += taps_ref[pl.ds(back, 1), columns] * older
                gated_ref[at_step, columns] = (total_ref[at_step, columns] * filtered).astype(
                    jnp.bfloat16
                )


def projected(spot, pair, gains, inv_rms, w_in, earlier, taps=None, history=None, steps=1):
    near, far = pair
    rows, channels = near.shape
    first, last = earlier is None, history is not None
    depth = min(512, channels)
    parts = INNER * channels // depth

    def whole(shape):
        return pl.BlockSpec(shape, lambda part, _: (0,) * len(shape))

    in_place = pl.BlockSpec(memory_space=pltpu.VMEM)
    in_specs = [
        whole((rows, channels)),
        whole((rows, channels)),
        whole(gains.shape),
        whole((rows, LANES)),
        pl.BlockSpec((depth, w_in.shape[1]), lambda part, spot: (spot[0] * parts + part, 0)),
    ]
    args = [near, far, gains, inv_rms, w_in]
    aliases = {}
    if not first:
        in_specs.append(in_place)
        aliases = {len(args) + 1: 0}
        args.append(earlier)
    out_specs = [in_place]
    out_shape = [jax.ShapeDtypeStruct((rows, 3 * channels), jnp.float32)]
    if last:
        in_specs += [whole(taps.shape), whole((rows, channels))]
        args += [taps, history]
        out_specs.append(whole((rows, channels)))
        out_shape.append(jax.ShapeDtypeStruct((rows, channels), jnp.bfloat16))
    return pl.pallas_call(
        functools.partial(project_kernel, steps, first, last),
        grid_spec=pltpu.PrefetchScalarGridSpec(
            num_scalar_prefetch=1,
            grid=(parts,),
            in_specs=in_specs,
            out_specs=out_specs,
            scratch_shapes=[pltpu.VMEM((rows, depth), jnp.bfloat16)],
        ),
        out_shape=out_shape,
        input_output_aliases=aliases,
        compiler_params=pltpu.CompilerParams(vmem_limit_bytes=VMEM_LIMIT),
        cost_estimate=pl.CostEstimate(
            flops=2 * rows * INNER * channels * 3 * channels,
            bytes_accessed=2 * INNER * channels * 3 * channels,
            transcendentals=0,
        ),
        name="gated_rows" if last else "projected_part",
    )(spot, *args)[-1]


def share_kernel(spot, x_ref, w_ref, *refs):
    share = jnp.dot(x_ref[...], w_ref[...], preferred_element_type=jnp.float32)
    if len(refs) > 1:
        share += refs[0][...].astype(jnp.float32)
    refs[-1][...] = share.astype(refs[-1].dtype)


def output_share(spot, gated, w_out, owners, arrived=None):
    rows, channels = gated.shape
    wide = w_out.shape[1] // owners
    block = min(512, wide)
    blocks = wide // block
    specs = [
        pl.BlockSpec((rows, channels), lambda c, _: (0, 0)),
        pl.BlockSpec((channels, block), lambda c, spot: (0, spot[0] * blocks + c)),
    ]
    args = [gated, w_out]
    if arrived is not None:
        specs.append(pl.BlockSpec((rows, block), lambda c, _: (0, c)))
        args.append(arrived)
    return pl.pallas_call(
        share_kernel,
        grid_spec=pltpu.PrefetchScalarGridSpec(
            num_scalar_prefetch=1,
            grid=(blocks,),
            in_specs=specs,
            out_specs=pl.BlockSpec((rows, block), lambda c, _: (0, c)),
        ),
        out_shape=jax.ShapeDtypeStruct((rows, wide), jnp.bfloat16),
        compiler_params=pltpu.CompilerParams(vmem_limit_bytes=VMEM_LIMIT),
        cost_estimate=pl.CostEstimate(
            flops=2 * rows * channels * wide,
            bytes_accessed=2 * channels * wide,
            transcendentals=0,
        ),
        name="output_share",
    )(spot, *args)


def gathered_taps(filters):
    owners = lax.axis_size("tensor")
    channels = filters.shape[0]
    groups, halves = lax.axis_size("groups"), lax.axis_size("batch")
    group, half = lax.axis_index("groups"), lax.axis_index("batch")
    if groups != 2 or halves != 2 or channels % (4 * LANES):
        return [(0, 0, [lax.all_gather(filters.T, "tensor")])]
    quarter = channels // 4
    own = lax.dynamic_slice_in_dim(filters, (group * 2 + half) * quarter, quarter, 0).T
    own = jnp.broadcast_to(own[None], (owners, *own.shape))
    own = lax.all_to_all(own, "tensor", 0, 0, tiled=True)
    swap = [(0, 1), (1, 0)]
    across = lax.ppermute(own, "groups", swap)
    return [
        (group * 2, half, [own, lax.ppermute(own, "batch", swap)]),
        ((1 - group) * 2, half, [across, lax.ppermute(across, "batch", swap)]),
    ]


def per_device(token_ids, embed, norm_gain, w_in, filters, w_out, cache_rows, owner, lengths):
    steps, seqs = token_ids.shape
    vocab, channels = embed.shape
    rows = cache_rows.shape[0]
    tokens = steps * seqs
    owners = lax.axis_size("tensor")
    halves = lax.axis_size("batch")
    mine = lax.axis_index("tensor")
    half = lax.axis_index("batch")
    outer, inner, outer_size = place_of(mine, owners)

    onehot = token_ids.reshape(-1)[:, None] == jnp.arange(vocab, dtype=jnp.int32)[None, :]
    stream = jnp.dot(onehot.astype(jnp.bfloat16), embed, preferred_element_type=jnp.float32)
    streams = spread(stream.astype(jnp.bfloat16))

    tiny = jnp.concatenate([norm_gain.astype(jnp.float32), jnp.sum(stream * stream, axis=1)])
    tiny = tiny.reshape(-1, LANES)
    tiny = lax.all_to_all(
        jnp.broadcast_to(tiny[None], (owners, *tiny.shape)), "tensor", 0, 0, tiled=True
    )
    gain_rows = channels // LANES
    gains = tiny[:, :gain_rows].reshape(owners, channels)
    inv_rms = lax.rsqrt(jnp.sum(tiny[:, gain_rows:], axis=0).reshape(tokens) / D + EPSILON)
    inv_rms = jnp.broadcast_to(inv_rms[:, None], (tokens, LANES))

    owner_grid = owner.reshape(owners, halves, rows)
    arrived = lax.dynamic_index_in_dim(owner_grid, half, 1, keepdims=False) - half * seqs
    seq_index = jnp.arange(seqs, dtype=jnp.int32)
    own = lax.dynamic_index_in_dim(arrived, mine, 0, keepdims=False)
    row_lengths = jnp.sum(jnp.where(own[:, None] == seq_index[None, :], lengths[None, :], 0), axis=1)
    row_lengths = jnp.broadcast_to(row_lengths[:, None], (rows, LANES))
    step_index = jnp.arange(steps, dtype=jnp.int32)
    place = (
        (step_index[:, None, None, None, None] == step_index[None, None, None, :, None])
        & (seq_index[None, :, None, None, None] == arrived[None, None, :, None, :])
    ).reshape(tokens, owners * steps * rows)
    place = place.astype(jnp.bfloat16)

    cache = cache_rows.transpose(1, 0, 2)
    histories = []
    for first, listed, tap_parts in gathered_taps(filters):
        spot = jnp.stack([jnp.int32(first), jnp.int32(listed)])
        terms = history_terms(cache, tap_parts, spot, row_lengths, steps)
        terms = lax.all_to_all(terms, "tensor", 0, 0, tiled=True)
        histories.append(
            jnp.dot(
                place,
                terms.reshape(owners * steps * rows, terms.shape[3]),
                preferred_element_type=jnp.float32,
            )
        )
    history = jnp.concatenate(histories, axis=1)
    if len(histories) == 2:
        swapped = jnp.concatenate(histories[::-1], axis=1)
        history = jnp.where(lax.axis_index("groups") == 0, history, swapped)

    def spot_at(back):
        return jnp.stack([(outer + back) % outer_size, inner]).astype(jnp.int32)

    sums = None
    near_taps = filters[:, : 2 * steps].T.astype(jnp.float32)
    for back in range(outer_size):
        ends = dict(taps=near_taps, history=history, steps=steps) if back == outer_size - 1 else {}
        sums = projected(spot_at(-back), streams[back], gains, inv_rms, w_in, sums, **ends)
    gated = sums

    def spot_to(ahead, flip):
        return ((outer + ahead) % outer_size * INNER + (inner + flip) % INNER)[None].astype(jnp.int32)

    order = sorted(range(outer_size), key=lambda ahead: (ahead == 0, -min(ahead, outer_size - ahead)))
    across = {
        ahead: moved(output_share(spot_to(ahead, 1), gated, w_out, owners), 0, 1) for ahead in order
    }
    out = stream
    for ahead in order:
        share = output_share(spot_to(ahead, 0), gated, w_out, owners, across[ahead])
        out = out + (moved(share, ahead, 0) if ahead else share).astype(jnp.float32)
    return out.astype(jnp.bfloat16).reshape(steps, seqs, channels)


def solution(mesh):
    in_specs = (
        P(None, ("groups", "batch")),
        P(None, "tensor"),
        P("tensor"),
        P(None, "tensor"),
        P("tensor", None),
        P("tensor", None),
        P(("groups", "tensor", "batch"), None, None),
        P("groups"),
        P(("groups", "batch")),
    )
    out_specs = P(None, ("groups", "batch"), "tensor")
    return jax.shard_map(
        per_device, mesh=mesh, in_specs=in_specs, out_specs=out_specs, check_vma=False
    )
```

```python
import functools

import jax
import jax.numpy as jnp
from jax import lax
from jax.experimental import pallas as pl
from jax.experimental.pallas import tpu as pltpu
from jax.sharding import PartitionSpec as P

D = 8192
EPSILON = 1e-05
LANES = 128
PACKED = 16
INNER = 2
VMEM_LIMIT = 28 * 1024 * 1024
LARGE_LIMIT = 46 * 1024 * 1024


def place_of(mine, owners):
    return mine // INNER, mine % INNER, owners // INNER


def moved(array, outer_by, flip):
    owners = lax.axis_size("tensor")
    outer_size = owners // INNER
    pairs = []
    for source in range(owners):
        outer, inner = source // INNER, source % INNER
        pairs.append((source, (outer + outer_by) % outer_size * INNER + (inner ^ flip)))
    return lax.ppermute(array, "tensor", pairs)


def spread(block):
    outer_size = lax.axis_size("tensor") // INNER
    blocks = []
    held = block
    for step in range(outer_size):
        if step:
            held = moved(held, 1, 0)
        blocks.append((held, moved(held, 0, 1)))
    return blocks


def history_kernel(steps, spot, lengths_ref, *refs):
    *tap_refs, cache_ref, out_ref, taps_scr = refs
    lags, rows, channels = cache_ref.shape
    width = min(4 * LANES, channels)
    for index, tap_ref in enumerate(tap_refs):

        @pl.when(pl.program_id(1) == index)
        def _():
            taps_scr[...] = tap_ref[0].astype(jnp.float32).T

    lengths = jnp.concatenate([lengths_ref[...]] * (width // LANES), axis=1)

    def one_chunk(chunk, carry):
        at = pl.ds(pl.multiple_of(chunk * width, width), width)
        taps = [
            jnp.broadcast_to(taps_scr[pl.ds(1 + step, 1), at], (rows, width)) for step in range(steps)
        ]
        sums = [jnp.zeros((rows, width), jnp.float32) for _ in range(steps)]
        for lag in range(lags):
            values = jnp.where(lengths > lag, cache_ref[lag, :, at].astype(jnp.float32), 0.0)
            for step in range(min(steps, lags - lag)):
                sums[step] += values * taps[step]
            taps = taps[1:]
            if lag + 1 + steps <= lags:
                taps.append(
                    jnp.broadcast_to(taps_scr[pl.ds(lag + 1 + steps, 1), at], (rows, width))
                )
        for step in range(steps):
            out_ref[0, step, :, at] = sums[step].astype(out_ref.dtype)
        return carry

    lax.fori_loop(0, channels // width, one_chunk, 0)


def history_terms(cache, tap_parts, spot, lengths, steps):
    lags, rows, width = cache.shape
    owners, channels, tap_rows = tap_parts[0].shape
    count = len(tap_parts)
    tap_spec = pl.BlockSpec((1, channels, tap_rows), lambda n, part, _: (n, 0, 0))
    return pl.pallas_call(
        functools.partial(history_kernel, steps),
        grid_spec=pltpu.PrefetchScalarGridSpec(
            num_scalar_prefetch=1,
            grid=(owners, count),
            in_specs=[
                pl.BlockSpec((rows, LANES), lambda n, part, _: (0, 0)),
                *[tap_spec] * count,
                pl.BlockSpec(
                    (lags, rows, channels),
                    lambda n, part, spot: (0, 0, n * count + (spot[0] + part) % count),
                ),
            ],
            out_specs=pl.BlockSpec(
                (1, steps, rows, channels), lambda n, part, spot: (n, 0, 0, (spot[0] + part) % count)
            ),
            scratch_shapes=[pltpu.VMEM((tap_rows, channels), jnp.float32)],
        ),
        out_shape=jax.ShapeDtypeStruct((owners, steps, rows, count * channels), jnp.bfloat16),
        compiler_params=pltpu.CompilerParams(vmem_limit_bytes=LARGE_LIMIT),
        cost_estimate=pl.CostEstimate(
            flops=2 * steps * rows * lags * owners * count * channels,
            bytes_accessed=2 * rows * lags * owners * count * channels,
            transcendentals=0,
        ),
        name="history_terms",
    )(spot, lengths, *tap_parts, cache)


def project_kernel(steps, first, last, spot, near, far, gain_ref, inv_ref, w_ref, *refs):
    refs = list(refs)
    earlier = None if first else refs.pop(0)
    taps_ref, place_ref, terms_ref = (refs.pop(0) for _ in range(3)) if last else (None,) * 3
    out_ref, normed = refs[:2]
    rows, channels = near.shape
    step_at = pl.program_id(0)

    @pl.when(step_at == 0)
    def _():
        scale = inv_ref[:, :1]
        for flip, x_ref in ((0, near), (1, far)):
            inner = (spot[1] + flip) % INNER
            gain = gain_ref[pl.ds(spot[0] * INNER + inner, 1), :]
            normed[:, pl.ds(pl.multiple_of(inner * channels, channels), channels)] = (
                x_ref[...].astype(jnp.float32) * scale * gain
            ).astype(jnp.bfloat16)

    total = jnp.dot(normed[...], w_ref[...], preferred_element_type=jnp.float32)
    if not first:
        total += earlier[...]
    if not last:
        out_ref[...] = total
        return
    parts = refs[2]
    which = step_at % 3
    parts[which] = total

    @pl.when(which == 2)
    def _():
        seqs = rows // steps
        history = jnp.dot(place_ref[...], terms_ref[...], preferred_element_type=jnp.float32)
        recent = (parts[1] * parts[2]).astype(jnp.bfloat16).astype(jnp.float32)
        for step in range(steps):
            at = slice(step * seqs, (step + 1) * seqs)
            filtered = history[at]
            for back in range(step + 1):
                older = recent[(step - back) * seqs : (step - back + 1) * seqs]
                filtered += taps_ref[pl.ds(back, 1), :] * older
            out_ref[at, :] = (parts[0, at, :] * filtered).astype(jnp.bfloat16)


def projected(spot, pair, gains, inv_rms, w_in, earlier, taps=None, place=None, terms=None, steps=1):
    near, far = pair
    rows, channels = near.shape
    block = min(256, channels)
    blocks = channels // block
    first, last = earlier is None, terms is not None

    def whole(shape):
        return pl.BlockSpec(shape, lambda i, _: (0,) * len(shape))

    def column(i):
        return i % 3 * blocks + i // 3

    in_specs = [
        whole((rows, channels)),
        whole((rows, channels)),
        whole(gains.shape),
        whole((rows, LANES)),
        pl.BlockSpec((INNER * channels, block), lambda i, spot: (spot[0], column(i))),
    ]
    args = [near, far, gains, inv_rms, w_in]
    total_spec = pl.BlockSpec((rows, block), lambda i, _: (0, column(i)))
    if not first:
        in_specs.append(total_spec)
        args.append(earlier)
    scratch = [pltpu.VMEM((rows, INNER * channels), jnp.bfloat16)]
    if last:
        in_specs += [
            pl.BlockSpec((taps.shape[0], block), lambda i, _: (0, i // 3)),
            whole(place.shape),
            pl.BlockSpec((terms.shape[0], block), lambda i, _: (0, i // 3)),
        ]
        args += [taps, place, terms]
        scratch.append(pltpu.VMEM((3, rows, block), jnp.float32))
        out_spec = pl.BlockSpec((rows, block), lambda i, _: (0, i // 3))
        out_shape = jax.ShapeDtypeStruct((rows, channels), jnp.bfloat16)
    else:
        out_spec = total_spec
        out_shape = jax.ShapeDtypeStruct((rows, 3 * channels), jnp.float32)
    return pl.pallas_call(
        functools.partial(project_kernel, steps, first, last),
        grid_spec=pltpu.PrefetchScalarGridSpec(
            num_scalar_prefetch=1,
            grid=(3 * blocks,),
            in_specs=in_specs,
            out_specs=out_spec,
            scratch_shapes=scratch,
        ),
        out_shape=out_shape,
        compiler_params=pltpu.CompilerParams(vmem_limit_bytes=VMEM_LIMIT),
        cost_estimate=pl.CostEstimate(
            flops=2 * rows * INNER * channels * 3 * channels,
            bytes_accessed=2 * INNER * channels * 3 * channels,
            transcendentals=0,
        ),
        name="gated_rows" if last else "projected_part",
    )(spot, *args)


def share_kernel(spot, x_ref, w_ref, *refs):
    share = jnp.dot(x_ref[...], w_ref[...], preferred_element_type=jnp.float32)
    if len(refs) > 1:
        share += refs[0][...].astype(jnp.float32)
    refs[-1][...] = share.astype(refs[-1].dtype)


def output_share(spot, gated, w_out, owners, arrived=None):
    rows, channels = gated.shape
    wide = w_out.shape[1] // owners
    block = min(512, wide)
    blocks = wide // block
    specs = [
        pl.BlockSpec((rows, channels), lambda c, _: (0, 0)),
        pl.BlockSpec((channels, block), lambda c, spot: (0, spot[0] * blocks + c)),
    ]
    args = [gated, w_out]
    if arrived is not None:
        specs.append(pl.BlockSpec((rows, block), lambda c, _: (0, c)))
        args.append(arrived)
    return pl.pallas_call(
        share_kernel,
        grid_spec=pltpu.PrefetchScalarGridSpec(
            num_scalar_prefetch=1,
            grid=(blocks,),
            in_specs=specs,
            out_specs=pl.BlockSpec((rows, block), lambda c, _: (0, c)),
        ),
        out_shape=jax.ShapeDtypeStruct((rows, wide), jnp.bfloat16),
        compiler_params=pltpu.CompilerParams(vmem_limit_bytes=LARGE_LIMIT),
        cost_estimate=pl.CostEstimate(
            flops=2 * rows * channels * wide,
            bytes_accessed=2 * channels * wide,
            transcendentals=0,
        ),
        name="output_share",
    )(spot, *args)


def gathered_taps(filters):
    channels = filters.shape[0]
    if not halved(channels):
        return lax.all_gather(filters, "tensor")
    wide = channels // 2
    own = lax.dynamic_slice_in_dim(filters, lax.axis_index("batch") * wide, wide, 0)
    return lax.all_gather(own, "tensor")


def halved(channels):
    return lax.axis_size("batch") == 2 and channels % (2 * LANES) == 0


def after(array, earlier):
    return lax.optimization_barrier((array, earlier))[0]


def per_device(token_ids, embed, norm_gain, w_in, filters, w_out, cache_rows, owner, lengths):
    steps, seqs = token_ids.shape
    vocab, channels = embed.shape
    rows = cache_rows.shape[0]
    tokens = steps * seqs
    owners = lax.axis_size("tensor")
    halves = lax.axis_size("batch")
    mine = lax.axis_index("tensor")
    half = lax.axis_index("batch")
    outer, inner, outer_size = place_of(mine, owners)

    onehot = token_ids.reshape(-1)[:, None] == jnp.arange(vocab, dtype=jnp.int32)[None, :]
    stream = jnp.dot(onehot.astype(jnp.bfloat16), embed, preferred_element_type=jnp.float32)
    streams = spread(stream.astype(jnp.bfloat16))

    tiny = jnp.concatenate([norm_gain.astype(jnp.float32), jnp.sum(stream * stream, axis=1)])
    tiny = tiny.reshape(-1, LANES)
    tiny = lax.all_to_all(
        jnp.broadcast_to(tiny[None], (owners, *tiny.shape)), "tensor", 0, 0, tiled=True
    )
    gain_rows = channels // LANES
    gains = tiny[:, :gain_rows].reshape(owners, channels)
    inv_rms = lax.rsqrt(jnp.sum(tiny[:, gain_rows:], axis=0).reshape(tokens) / D + EPSILON)
    inv_rms = jnp.broadcast_to(inv_rms[:, None], (tokens, LANES))

    owner_grid = owner.reshape(owners, halves, rows)
    arrived = lax.dynamic_index_in_dim(owner_grid, half, 1, keepdims=False) - half * seqs
    seq_index = jnp.arange(seqs, dtype=jnp.int32)
    own = lax.dynamic_index_in_dim(arrived, mine, 0, keepdims=False)
    row_lengths = jnp.sum(jnp.where(own[:, None] == seq_index[None, :], lengths[None, :], 0), axis=1)
    row_lengths = jnp.broadcast_to(row_lengths[:, None], (rows, LANES))
    step_index = jnp.arange(steps, dtype=jnp.int32)
    place = (
        (step_index[:, None, None, None, None] == step_index[None, None, None, :, None])
        & (seq_index[None, :, None, None, None] == arrived[None, None, :, None, :])
    ).reshape(tokens, owners * steps * rows)
    place = place.astype(jnp.bfloat16)

    cache = cache_rows.transpose(1, 0, 2)
    own_taps = gathered_taps(filters)

    def spot_at(back):
        return jnp.stack([(outer + back) % outer_size, inner]).astype(jnp.int32)

    near_taps = filters[:, : 2 * steps].T.astype(jnp.float32)
    sums = None
    for back in range(outer_size - 1):
        sums = projected(spot_at(-back), streams[back], gains, inv_rms, w_in, sums)
        if back == outer_size // 2 - 1:
            own_taps = after(own_taps, sums)
    tap_parts = [own_taps]
    listed = jnp.int32(0)
    if halved(channels):
        tap_parts.append(lax.ppermute(own_taps, "batch", [(0, 1), (1, 0)]))
        listed = half
    terms = history_terms(cache, tap_parts, listed[None], row_lengths, steps)
    terms = lax.all_to_all(terms, "tensor", 0, 0, tiled=True)
    gated = projected(
        spot_at(1 - outer_size),
        streams[outer_size - 1],
        gains,
        inv_rms,
        w_in,
        sums,
        taps=near_taps,
        place=place,
        terms=terms.reshape(owners * steps * rows, channels),
        steps=steps,
    )

    def spot_to(ahead, flip):
        return ((outer + ahead) % outer_size * INNER + (inner + flip) % INNER)[None].astype(jnp.int32)

    order = sorted(range(outer_size), key=lambda ahead: (ahead == 0, -min(ahead, outer_size - ahead)))
    across = {
        ahead: moved(output_share(spot_to(ahead, 1), gated, w_out, owners), 0, 1) for ahead in order
    }
    out = stream
    for ahead in order:
        share = output_share(spot_to(ahead, 0), gated, w_out, owners, across[ahead])
        out = out + (moved(share, ahead, 0) if ahead else share).astype(jnp.float32)
    return out.astype(jnp.bfloat16).reshape(steps, seqs, channels)


def solution(mesh):
    in_specs = (
        P(None, ("groups", "batch")),
        P(None, "tensor"),
        P("tensor"),
        P(None, "tensor"),
        P("tensor", None),
        P("tensor", None),
        P(("groups", "tensor", "batch"), None, None),
        P("groups"),
        P(("groups", "batch")),
    )
    out_specs = P(None, ("groups", "batch"), "tensor")
    return jax.shard_map(
        per_device, mesh=mesh, in_specs=in_specs, out_specs=out_specs, check_vma=False
    )
```

```python
import functools

import jax
import jax.numpy as jnp
from jax import lax
from jax.experimental import pallas as pl
from jax.experimental.pallas import tpu as pltpu
from jax.sharding import PartitionSpec as P

D = 8192
EPSILON = 1e-05
LANES = 128
PACKED = 16
INNER = 2
DEPTH = 4
VMEM_LIMIT = 16 * 1024 * 1024
IN_SMEM = pl.BlockSpec(memory_space=pltpu.SMEM)
IN_VMEM = pl.BlockSpec(memory_space=pltpu.VMEM)
IN_HBM = pl.BlockSpec(memory_space=pltpu.HBM)


def moved(array, outer_by, flip):
    owners = lax.axis_size("tensor")
    outer_size = owners // INNER
    pairs = []
    for source in range(owners):
        outer, inner = source // INNER, source % INNER
        pairs.append((source, (outer + outer_by) % outer_size * INNER + (inner ^ flip)))
    return lax.ppermute(array, "tensor", pairs)


def spread(block):
    outer_size = lax.axis_size("tensor") // INNER
    blocks = []
    held = block
    for step in range(outer_size):
        if step:
            held = moved(held, 1, 0)
        blocks.append((held, moved(held, 0, 1)))
    return blocks


def kernel_call(kernel, name, spot, operands, outputs, aliases, scratch, flops, moved_bytes):
    specs, args = zip(*operands)
    args = [
        pltpu.with_memory_space_constraint(arg, pltpu.HBM) if spec is IN_HBM else arg
        for spec, arg in operands
    ]
    out_specs, out_shape = zip(*outputs)
    return pl.pallas_call(
        kernel,
        in_specs=[IN_SMEM, *specs],
        out_specs=list(out_specs),
        out_shape=list(out_shape),
        input_output_aliases=aliases,
        scratch_shapes=scratch,
        compiler_params=pltpu.CompilerParams(vmem_limit_bytes=VMEM_LIMIT),
        cost_estimate=pl.CostEstimate(flops=flops, bytes_accessed=moved_bytes, transcendentals=0),
        name=name,
    )(spot, *args)


def history_kernel(steps, first, spot, lengths_ref, near_ref, far_ref, cache_hbm, *refs):
    terms_ref, held, taps_scr, sems = refs if first else refs[1:]
    if not first:
        terms_ref[...] = refs[0][...]
    _, lags, rows, width = held.shape
    channels = near_ref.shape[1]
    parts = channels // width
    lengths = jnp.concatenate([lengths_ref[...]] * (width // LANES), axis=1)

    def owner_of(flip):
        return spot[0] * INNER + (spot[1] + flip) % INNER

    def fetch(index):
        start = (owner_of(index // parts) * parts + index % parts) * width
        columns = pl.ds(pl.multiple_of(start, width), width)
        return pltpu.make_async_copy(cache_hbm.at[:, :, columns], held.at[index], sems.at[index])

    for index in range(2 * parts):
        fetch(index).start()

    def one_part(index, carry):
        fetch(index).wait()
        flip = index // parts
        at = pl.ds(pl.multiple_of(index % parts * width, width), width)

        @pl.when(flip == 0)
        def _():
            taps_scr[...] = near_ref[pl.ds(0, lags + 1), at].astype(jnp.float32)

        @pl.when(flip == 1)
        def _():
            taps_scr[...] = far_ref[pl.ds(0, lags + 1), at].astype(jnp.float32)

        def tap(lag):
            return jnp.broadcast_to(taps_scr[pl.ds(lag, 1), :], (rows, width))

        taps = [tap(1 + step) for step in range(steps)]
        sums = [jnp.zeros((rows, width), jnp.float32) for _ in range(steps)]
        for lag in range(lags):
            values = jnp.where(lengths > lag, held[index, lag].astype(jnp.float32), 0.0)
            for step in range(min(steps, lags - lag)):
                sums[step] += values * taps[step]
            taps = taps[1:]
            if lag + 1 + steps <= lags:
                taps.append(tap(lag + 1 + steps))
        for step in range(steps):
            terms_ref[owner_of(flip), step, :, at] = sums[step].astype(terms_ref.dtype)
        return carry

    lax.fori_loop(0, 2 * parts, one_part, 0)


def history_terms(cache, near, far, lengths, spot, steps, earlier):
    lags, rows, total = cache.shape
    channels = near.shape[1]
    width = min(4 * LANES, channels)
    count = 2 * channels // width
    operands = [(IN_VMEM, lengths), (IN_VMEM, near), (IN_VMEM, far), (IN_HBM, cache)]
    aliases = {}
    if earlier is not None:
        aliases = {len(operands) + 1: 0}
        operands.append((IN_VMEM, earlier))
    shape = (total // channels, steps, rows, channels)
    return kernel_call(
        functools.partial(history_kernel, steps, earlier is None),
        "history_terms",
        spot,
        operands,
        [(IN_VMEM, jax.ShapeDtypeStruct(shape, jnp.bfloat16))],
        aliases,
        [
            pltpu.VMEM((count, lags, rows, width), jnp.bfloat16),
            pltpu.VMEM((lags + 1, width), jnp.float32),
            pltpu.SemaphoreType.DMA((count,)),
        ],
        2400 * steps * rows * lags * channels // 2,
        4 * rows * lags * channels,
    )[0]


def project_kernel(steps, first, last, gain_at, spot, near, far, near_gain, far_gain, inv_ref, w_hbm, *refs):
    refs = list(refs)
    earlier = None if first else refs.pop(0)
    taps_ref, place_ref, terms_ref = (refs.pop(0) for _ in range(3)) if last else (None,) * 3
    total_ref = refs.pop(0)
    gated_ref = refs.pop(0) if last else None
    normed, held, sems = refs
    rows, channels = near.shape
    slots, depth, block = held.shape
    chunks = 3 * channels // block
    in_rows = pl.ds(pl.multiple_of(spot[0] * depth, depth), depth)

    def fetch(chunk):
        columns = pl.ds(pl.multiple_of(chunk * block, block), block)
        slot = lax.rem(chunk, slots)
        return pltpu.make_async_copy(w_hbm.at[in_rows, columns], held.at[slot], sems.at[slot])

    for chunk in range(min(slots, chunks)):
        fetch(chunk).start()

    scale = inv_ref[:, :1]
    for flip, x_ref, gain_ref in ((0, near, near_gain), (1, far, far_gain)):
        inner = (spot[1] + flip) % INNER
        gain = gain_ref[pl.ds(gain_at, PACKED), :].astype(jnp.float32)[:1]
        normed[:, pl.ds(pl.multiple_of(inner * channels, channels), channels)] = (
            x_ref[...].astype(jnp.float32) * scale * gain
        ).astype(jnp.bfloat16)

    def one_chunk(chunk, carry):
        fetch(chunk).wait()
        columns = pl.ds(pl.multiple_of(chunk * block, block), block)
        term = jnp.dot(
            normed[...], held[lax.rem(chunk, slots)], preferred_element_type=jnp.float32
        )
        if first:
            total_ref[:, columns] = term
        else:
            total_ref[:, columns] = earlier[:, columns] + term

        @pl.when(chunk + slots < chunks)
        def _():
            fetch(chunk + slots).start()

        return carry

    lax.fori_loop(0, chunks, one_chunk, 0)
    if not last:
        return
    seqs = rows // steps

    def one_gate(chunk, carry):
        start = pl.multiple_of(chunk * block, block)
        at = pl.ds(start, block)
        history = jnp.dot(place_ref[...], terms_ref[:, at], preferred_element_type=jnp.float32)
        keys = total_ref[:, pl.ds(pl.multiple_of(channels + start, block), block)]
        values = total_ref[:, pl.ds(pl.multiple_of(2 * channels + start, block), block)]
        recent = (keys * values).astype(jnp.bfloat16).astype(jnp.float32)
        for step in range(steps):
            rows_at = pl.ds(step * seqs, seqs)
            filtered = history[step * seqs : (step + 1) * seqs]
            for back in range(step + 1):
                older = recent[(step - back) * seqs : (step - back + 1) * seqs]
                filtered += taps_ref[pl.ds(back, 1), at] * older
            gated_ref[rows_at, at] = (total_ref[rows_at, at] * filtered).astype(jnp.bfloat16)
        return carry

    lax.fori_loop(0, channels // block, one_gate, 0)


def projected(spot, pair, gains, gain_at, inv_rms, w_in, earlier, ends=None):
    near, far = pair
    rows, channels = near.shape
    block = min(256, channels)
    first, last = earlier is None, ends is not None
    operands = [(IN_VMEM, array) for array in (near, far, *gains, inv_rms)] + [(IN_HBM, w_in)]
    aliases = {}
    if not first:
        aliases = {len(operands) + 1: 0}
        operands.append((IN_VMEM, earlier))
    outputs = [(IN_VMEM, jax.ShapeDtypeStruct((rows, 3 * channels), jnp.float32))]
    steps = 1
    if last:
        steps, *arrays = ends
        operands += [(IN_VMEM, array) for array in arrays]
        outputs.append((IN_VMEM, jax.ShapeDtypeStruct((rows, channels), jnp.bfloat16)))
    return kernel_call(
        functools.partial(project_kernel, steps, first, last, gain_at),
        "gated_rows" if last else "projected_part",
        spot,
        operands,
        outputs,
        aliases,
        [
            pltpu.VMEM((rows, INNER * channels), jnp.bfloat16),
            pltpu.VMEM((DEPTH, INNER * channels, block), jnp.bfloat16),
            pltpu.SemaphoreType.DMA((DEPTH,)),
        ],
        4 * rows * INNER * channels * 3 * channels,
        4 * INNER * channels * 3 * channels,
    )[-1]


def share_kernel(spot, x_ref, w_hbm, *refs):
    *arrived, out_ref, held, sems = refs
    chunks, _, block = held.shape

    def fetch(chunk):
        start = pl.multiple_of((spot[0] * chunks + chunk) * block, block)
        return pltpu.make_async_copy(w_hbm.at[:, pl.ds(start, block)], held.at[chunk], sems.at[chunk])

    for chunk in range(chunks):
        fetch(chunk).start()
    for chunk in range(chunks):
        fetch(chunk).wait()
        columns = pl.ds(chunk * block, block)
        share = jnp.dot(x_ref[...], held[chunk], preferred_element_type=jnp.float32)
        if arrived:
            share += arrived[0][:, columns].astype(jnp.float32)
        out_ref[:, columns] = share.astype(out_ref.dtype)


def output_share(spot, gated, w_out, owners, arrived=None):
    rows, channels = gated.shape
    wide = w_out.shape[1] // owners
    block = min(256, wide)
    operands = [(IN_VMEM, gated), (IN_HBM, w_out)]
    if arrived is not None:
        operands.append((IN_VMEM, arrived))
    return kernel_call(
        share_kernel,
        "output_share",
        spot,
        operands,
        [(IN_VMEM, jax.ShapeDtypeStruct((rows, wide), jnp.bfloat16))],
        {},
        [
            pltpu.VMEM((wide // block, channels, block), jnp.bfloat16),
            pltpu.SemaphoreType.DMA((wide // block,)),
        ],
        2 * rows * channels * wide,
        2 * channels * wide,
    )[0]


def split_sums(values, channels):
    parts = []
    rest = values
    for _ in range(3):
        part = lax.reduce_precision(rest, 8, 7)
        parts.append(part.astype(jnp.bfloat16))
        rest = rest - part
    flat = jnp.concatenate(parts)
    count = -(-flat.shape[0] // channels)
    return jnp.pad(flat, (0, count * channels - flat.shape[0])).reshape(count, channels)


def after(array, earlier):
    return lax.optimization_barrier((array, earlier))[0]


def per_device(token_ids, embed, norm_gain, w_in, filters, w_out, cache_rows, owner, lengths):
    steps, seqs = token_ids.shape
    vocab, channels = embed.shape
    rows = cache_rows.shape[0]
    taps = filters.shape[1]
    tokens = steps * seqs
    owners = lax.axis_size("tensor")
    halves = lax.axis_size("batch")
    mine = lax.axis_index("tensor")
    half = lax.axis_index("batch")
    outer, inner, outer_size = mine // INNER, mine % INNER, owners // INNER

    onehot = token_ids.reshape(-1)[:, None] == jnp.arange(vocab, dtype=jnp.int32)[None, :]
    stream = jnp.dot(onehot.astype(jnp.bfloat16), embed, preferred_element_type=jnp.float32)
    squares = split_sums(jnp.sum(stream * stream, axis=1), channels)
    square_rows = squares.shape[0]
    filler = jnp.zeros((-(taps + 1 + square_rows) % PACKED, channels), jnp.bfloat16)
    small = jnp.concatenate([filters.T, norm_gain[None, :], squares, filler], axis=0)
    smalls = spread(small)
    streams = spread(stream.astype(jnp.bfloat16))

    def spot_at(back):
        return jnp.stack([(outer + back) % outer_size, inner]).astype(jnp.int32)

    owner_grid = owner.reshape(owners, halves, rows)
    arrived = lax.dynamic_index_in_dim(owner_grid, half, 1, keepdims=False) - half * seqs
    seq_index = jnp.arange(seqs, dtype=jnp.int32)
    own = lax.dynamic_index_in_dim(arrived, mine, 0, keepdims=False)
    row_lengths = jnp.sum(jnp.where(own[:, None] == seq_index[None, :], lengths[None, :], 0), axis=1)
    row_lengths = jnp.broadcast_to(row_lengths[:, None], (rows, LANES))
    step_index = jnp.arange(steps, dtype=jnp.int32)
    place = (
        (step_index[:, None, None, None, None] == step_index[None, None, None, :, None])
        & (seq_index[None, :, None, None, None] == arrived[None, None, :, None, :])
    ).reshape(tokens, owners * steps * rows)
    place = place.astype(jnp.bfloat16)

    cache = cache_rows.transpose(1, 0, 2)
    terms = None
    for back, (near, far) in enumerate(smalls):
        if 0 < back < outer_size - 1:
            near = after(near, streams[back][0])
        terms = history_terms(cache, near, far, row_lengths, spot_at(-back), steps, terms)
    terms = lax.all_to_all(terms, "tensor", 0, 0, tiled=True)

    total = 0.0
    for near, far in smalls:
        for block in (near, far):
            flat = block[taps + 1 : taps + 1 + square_rows].reshape(-1)[: 3 * tokens]
            total = total + jnp.sum(flat.astype(jnp.float32).reshape(3, tokens), axis=0)
    inv_rms = lax.rsqrt(total / D + EPSILON)
    inv_rms = jnp.broadcast_to(inv_rms[:, None], (tokens, LANES))

    near_taps = filters[:, : 2 * steps].T.astype(jnp.float32)
    sums = None
    for back in range(outer_size):
        ends = None
        if back == outer_size - 1:
            ends = (steps, near_taps, place, terms.reshape(owners * steps * rows, channels))
        sums = projected(spot_at(-back), streams[back], smalls[back], taps, inv_rms, w_in, sums, ends)
    gated = sums

    def spot_to(ahead, flip):
        return ((outer + ahead) % outer_size * INNER + (inner + flip) % INNER)[None].astype(jnp.int32)

    order = sorted(range(outer_size), key=lambda ahead: (ahead == 0, -min(ahead, outer_size - ahead)))
    across = {
        ahead: moved(output_share(spot_to(ahead, 1), gated, w_out, owners), 0, 1) for ahead in order
    }
    out = stream
    for ahead in order:
        share = output_share(spot_to(ahead, 0), gated, w_out, owners, across[ahead])
        out = out + (moved(share, ahead, 0) if ahead else share).astype(jnp.float32)
    return out.astype(jnp.bfloat16).reshape(steps, seqs, channels)


def solution(mesh):
    in_specs = (
        P(None, ("groups", "batch")),
        P(None, "tensor"),
        P("tensor"),
        P(None, "tensor"),
        P("tensor", None),
        P("tensor", None),
        P(("groups", "tensor", "batch"), None, None),
        P("groups"),
        P(("groups", "batch")),
    )
    out_specs = P(None, ("groups", "batch"), "tensor")
    return jax.shard_map(
        per_device, mesh=mesh, in_specs=in_specs, out_specs=out_specs, check_vma=False
    )
```

```python
import functools

import jax
import jax.numpy as jnp
from jax import lax
from jax.experimental import pallas as pl
from jax.experimental.pallas import tpu as pltpu
from jax.sharding import PartitionSpec as P

D = 8192
EPSILON = 1e-05
LANES = 128
INNER = 2
DEPTH = 3
VMEM_LIMIT = 16 * 1024 * 1024
IN_SMEM = pl.BlockSpec(memory_space=pltpu.SMEM)
IN_VMEM = pl.BlockSpec(memory_space=pltpu.VMEM)
IN_HBM = pl.BlockSpec(memory_space=pltpu.HBM)
ANYWHERE = pl.BlockSpec(memory_space=pl.ANY)


def moved(array, outer_by, flip):
    owners = lax.axis_size("tensor")
    outer_size = owners // INNER
    pairs = []
    for source in range(owners):
        outer, inner = source // INNER, source % INNER
        pairs.append((source, (outer + outer_by) % outer_size * INNER + (inner ^ flip)))
    return lax.ppermute(array, "tensor", pairs)


def spread(block):
    outer_size = lax.axis_size("tensor") // INNER
    blocks = []
    held = block
    for step in range(outer_size):
        if step:
            held = moved(held, 1, 0)
        blocks.append((held, moved(held, 0, 1)))
    return blocks


def kernel_call(kernel, name, spot, operands, outputs, aliases, scratch, flops, moved_bytes):
    specs, args = zip(*operands)
    args = [
        pltpu.with_memory_space_constraint(arg, pltpu.HBM) if spec is IN_HBM else arg
        for spec, arg in operands
    ]
    out_specs, out_shape = zip(*outputs)
    return pl.pallas_call(
        kernel,
        in_specs=[IN_SMEM, *specs],
        out_specs=list(out_specs),
        out_shape=list(out_shape),
        input_output_aliases=aliases,
        scratch_shapes=scratch,
        compiler_params=pltpu.CompilerParams(vmem_limit_bytes=VMEM_LIMIT),
        cost_estimate=pl.CostEstimate(flops=flops, bytes_accessed=moved_bytes, transcendentals=0),
        name=name,
    )(spot, *args)


def history_kernel(steps, first, spot, lengths_ref, near_ref, far_ref, cache_hbm, *refs):
    terms_ref, held, taps_scr, sems = refs if first else refs[1:]
    if not first:
        terms_ref[...] = refs[0][...]
    _, lags, rows, width = held.shape
    channels = near_ref.shape[1]
    parts = channels // width
    lengths = jnp.concatenate([lengths_ref[...]] * (width // LANES), axis=1)

    def owner_of(flip):
        return spot[0] * INNER + (spot[1] + flip) % INNER

    def fetch(index):
        start = (owner_of(index // parts) * parts + index % parts) * width
        columns = pl.ds(pl.multiple_of(start, width), width)
        return pltpu.make_async_copy(cache_hbm.at[:, :, columns], held.at[index], sems.at[index])

    for index in range(2 * parts):
        fetch(index).start()

    def one_part(index, carry):
        fetch(index).wait()
        flip = index // parts
        at = pl.ds(pl.multiple_of(index % parts * width, width), width)

        @pl.when(flip == 0)
        def _():
            taps_scr[...] = near_ref[pl.ds(0, lags + 1), at].astype(jnp.float32)

        @pl.when(flip == 1)
        def _():
            taps_scr[...] = far_ref[pl.ds(0, lags + 1), at].astype(jnp.float32)

        def tap(lag):
            return jnp.broadcast_to(taps_scr[pl.ds(lag, 1), :], (rows, width))

        taps = [tap(1 + step) for step in range(steps)]
        sums = [jnp.zeros((rows, width), jnp.float32) for _ in range(steps)]
        for lag in range(lags):
            values = jnp.where(lengths > lag, held[index, lag].astype(jnp.float32), 0.0)
            for step in range(min(steps, lags - lag)):
                sums[step] += values * taps[step]
            taps = taps[1:]
            if lag + 1 + steps <= lags:
                taps.append(tap(lag + 1 + steps))
        for step in range(steps):
            terms_ref[owner_of(flip), step, :, at] = sums[step].astype(terms_ref.dtype)
        return carry

    lax.fori_loop(0, 2 * parts, one_part, 0)


def history_terms(cache, near, far, lengths, spot, steps, earlier):
    lags, rows, total = cache.shape
    channels = near.shape[1]
    width = min(4 * LANES, channels)
    count = 2 * channels // width
    operands = [(IN_VMEM, lengths), (IN_VMEM, near), (IN_VMEM, far), (IN_HBM, cache)]
    aliases = {}
    if earlier is not None:
        aliases = {len(operands) + 1: 0}
        operands.append((IN_VMEM, earlier))
    shape = (total // channels, steps, rows, channels)
    return kernel_call(
        functools.partial(history_kernel, steps, earlier is None),
        "history_terms",
        spot,
        operands,
        [(IN_VMEM, jax.ShapeDtypeStruct(shape, jnp.bfloat16))],
        aliases,
        [
            pltpu.VMEM((count, lags, rows, width), jnp.bfloat16),
            pltpu.VMEM((lags + 1, width), jnp.float32),
            pltpu.SemaphoreType.DMA((count,)),
        ],
        2400 * steps * rows * lags * channels // 2,
        4 * rows * lags * channels,
    )[0]


def project_kernel(steps, first, last, ahead, spot, near, far, gain_ref, inv_ref, w_hbm, *refs):
    refs = list(refs)
    earlier = None if first else refs.pop(0)
    taps_ref, place_ref, terms_any = (refs.pop(0) for _ in range(3)) if last else (None,) * 3
    next_hbm = refs.pop(0) if ahead else None
    total_ref = refs.pop(0)
    gated_ref = refs.pop(0) if last else None
    next_ref = refs.pop(0) if ahead else None
    blocks, normed, held, sems, block_sems, extra_sem, *terms_scr = refs
    _, rows, channels = blocks.shape
    slots, depth, block = held.shape
    chunks = 3 * channels // block
    in_rows = pl.ds(pl.multiple_of(spot[0] * depth, depth), depth)

    def fetch(chunk):
        columns = pl.ds(pl.multiple_of(chunk * block, block), block)
        slot = lax.rem(chunk, slots)
        return pltpu.make_async_copy(w_hbm.at[in_rows, columns], held.at[slot], sems.at[slot])

    copies = [
        pltpu.make_async_copy(x_any, blocks.at[flip], block_sems.at[flip])
        for flip, x_any in enumerate((near, far))
    ]
    for copy in copies:
        copy.start()
    for chunk in range(min(slots, chunks)):
        fetch(chunk).start()
    if last:
        extra = pltpu.make_async_copy(terms_any, terms_scr[0], extra_sem.at[0])
        extra.start()
    if ahead:
        extra = pltpu.make_async_copy(next_hbm, next_ref, extra_sem.at[0])
        extra.start()

    scale = inv_ref[:, :1]
    for flip, copy in enumerate(copies):
        copy.wait()
        inner = (spot[1] + flip) % INNER
        gain = gain_ref[pl.ds(spot[0] * INNER + inner, 1), :]
        normed[:, pl.ds(pl.multiple_of(inner * channels, channels), channels)] = (
            blocks[flip].astype(jnp.float32) * scale * gain
        ).astype(jnp.bfloat16)

    def one_chunk(chunk, carry):
        fetch(chunk).wait()
        columns = pl.ds(pl.multiple_of(chunk * block, block), block)
        term = jnp.dot(
            normed[...], held[lax.rem(chunk, slots)], preferred_element_type=jnp.float32
        )
        total_ref[:, columns] = term if first else earlier[:, columns] + term

        @pl.when(chunk + slots < chunks)
        def _():
            fetch(chunk + slots).start()

        return carry

    lax.fori_loop(0, chunks, one_chunk, 0)
    if last or ahead:
        extra.wait()
    if not last:
        return
    seqs = rows // steps
    wide = min(256, channels)

    def one_gate(chunk, carry):
        start = pl.multiple_of(chunk * wide, wide)
        at = pl.ds(start, wide)
        history = jnp.dot(place_ref[...], terms_scr[0][:, at], preferred_element_type=jnp.float32)
        keys = total_ref[:, pl.ds(pl.multiple_of(channels + start, wide), wide)]
        values = total_ref[:, pl.ds(pl.multiple_of(2 * channels + start, wide), wide)]
        recent = (keys * values).astype(jnp.bfloat16).astype(jnp.float32)
        for step in range(steps):
            rows_at = pl.ds(step * seqs, seqs)
            filtered = history[step * seqs : (step + 1) * seqs]
            for back in range(step + 1):
                older = recent[(step - back) * seqs : (step - back + 1) * seqs]
                filtered += taps_ref[pl.ds(back, 1), at] * older
            gated_ref[rows_at, at] = (total_ref[rows_at, at] * filtered).astype(jnp.bfloat16)
        return carry

    lax.fori_loop(0, channels // wide, one_gate, 0)


def projected(spot, pair, gains, inv_rms, w_in, earlier, ends=None, ahead=None):
    near, far = pair
    rows, channels = near.shape
    block = min(512, channels)
    first, last = earlier is None, ends is not None
    operands = [(ANYWHERE, near), (ANYWHERE, far), (IN_VMEM, gains), (IN_VMEM, inv_rms), (IN_HBM, w_in)]
    aliases = {}
    if not first:
        aliases = {len(operands) + 1: 0}
        operands.append((IN_VMEM, earlier))
    outputs = [(IN_VMEM, jax.ShapeDtypeStruct((rows, 3 * channels), jnp.float32))]
    scratch = [
        pltpu.VMEM((INNER, rows, channels), jnp.bfloat16),
        pltpu.VMEM((rows, INNER * channels), jnp.bfloat16),
        pltpu.VMEM((DEPTH, INNER * channels, block), jnp.bfloat16),
        pltpu.SemaphoreType.DMA((DEPTH,)),
        pltpu.SemaphoreType.DMA((INNER,)),
        pltpu.SemaphoreType.DMA((1,)),
    ]
    steps = 1
    if last:
        steps, taps, place, terms = ends
        operands += [(IN_VMEM, taps), (IN_VMEM, place), (ANYWHERE, terms)]
        outputs.append((IN_VMEM, jax.ShapeDtypeStruct((rows, channels), jnp.bfloat16)))
        scratch.append(pltpu.VMEM(terms.shape, jnp.bfloat16))
    if ahead is not None:
        operands.append((IN_HBM, ahead))
        outputs.append((IN_VMEM, jax.ShapeDtypeStruct(ahead.shape, ahead.dtype)))
    out = kernel_call(
        functools.partial(project_kernel, steps, first, last, ahead is not None),
        "gated_rows" if last else "projected_part",
        spot,
        operands,
        outputs,
        aliases,
        scratch,
        4 * rows * INNER * channels * 3 * channels,
        4 * INNER * channels * 3 * channels,
    )
    return (out[0], out[1]) if ahead is not None else out[-1]


def share_kernel(spot, x_ref, w_ref, *refs):
    *arrived, out_ref, held, sem = refs
    wide = out_ref.shape[1]
    block = min(512, wide)
    if arrived:
        copy = pltpu.make_async_copy(arrived[0], held, sem.at[0])
        copy.start()
    for start in range(0, wide, block):
        columns = pl.ds(start, block)
        in_columns = pl.ds(pl.multiple_of(spot[0] * wide + start, block), block)
        share = jnp.dot(x_ref[...], w_ref[:, in_columns], preferred_element_type=jnp.float32)
        if arrived:
            if start == 0:
                copy.wait()
            share += held[:, columns].astype(jnp.float32)
        out_ref[:, columns] = share.astype(out_ref.dtype)


def output_share(spot, gated, w_out, owners, arrived=None):
    rows, channels = gated.shape
    wide = w_out.shape[1] // owners
    operands = [(IN_VMEM, gated), (IN_VMEM, w_out)]
    if arrived is not None:
        operands.append((ANYWHERE, arrived))
    return kernel_call(
        share_kernel,
        "output_share",
        spot,
        operands,
        [(IN_VMEM, jax.ShapeDtypeStruct((rows, wide), jnp.bfloat16))],
        {},
        [pltpu.VMEM((rows, wide), jnp.bfloat16), pltpu.SemaphoreType.DMA((1,))],
        2 * rows * channels * wide,
        2 * channels * wide,
    )[0]


def after(array, earlier):
    return lax.optimization_barrier((array, earlier))[0]


def per_device(token_ids, embed, norm_gain, w_in, filters, w_out, cache_rows, owner, lengths):
    steps, seqs = token_ids.shape
    vocab, channels = embed.shape
    rows = cache_rows.shape[0]
    tokens = steps * seqs
    owners = lax.axis_size("tensor")
    halves = lax.axis_size("batch")
    mine = lax.axis_index("tensor")
    half = lax.axis_index("batch")
    outer, inner, outer_size = mine // INNER, mine % INNER, owners // INNER

    onehot = token_ids.reshape(-1)[:, None] == jnp.arange(vocab, dtype=jnp.int32)[None, :]
    stream = jnp.dot(onehot.astype(jnp.bfloat16), embed, preferred_element_type=jnp.float32)
    tiny = jnp.concatenate([norm_gain.astype(jnp.float32), jnp.sum(stream * stream, axis=1)])
    tiny = tiny.reshape(-1, LANES)
    tiny = lax.all_to_all(
        jnp.broadcast_to(tiny[None], (owners, *tiny.shape)), "tensor", 0, 0, tiled=True
    )
    gain_rows = channels // LANES
    gains = tiny[:, :gain_rows].reshape(owners, channels)
    inv_rms = lax.rsqrt(jnp.sum(tiny[:, gain_rows:], axis=0).reshape(tokens) / D + EPSILON)
    inv_rms = jnp.broadcast_to(inv_rms[:, None], (tokens, LANES))
    lag_taps = spread(filters.T)
    streams = spread(stream.astype(jnp.bfloat16))

    def spot_at(back):
        return jnp.stack([(outer + back) % outer_size, inner]).astype(jnp.int32)

    owner_grid = owner.reshape(owners, halves, rows)
    arrived = lax.dynamic_index_in_dim(owner_grid, half, 1, keepdims=False) - half * seqs
    seq_index = jnp.arange(seqs, dtype=jnp.int32)
    own = lax.dynamic_index_in_dim(arrived, mine, 0, keepdims=False)
    row_lengths = jnp.sum(jnp.where(own[:, None] == seq_index[None, :], lengths[None, :], 0), axis=1)
    row_lengths = jnp.broadcast_to(row_lengths[:, None], (rows, LANES))
    step_index = jnp.arange(steps, dtype=jnp.int32)
    place = (
        (step_index[:, None, None, None, None] == step_index[None, None, None, :, None])
        & (seq_index[None, :, None, None, None] == arrived[None, None, :, None, :])
    ).reshape(tokens, owners * steps * rows)
    place = place.astype(jnp.bfloat16)

    cache = cache_rows.transpose(1, 0, 2)
    near_taps = filters[:, : 2 * steps].T.astype(jnp.float32)
    terms = sums = None
    for back, (near, far) in enumerate(lag_taps):
        if 0 < back <= outer_size // 2:
            sums = projected(spot_at(1 - back), streams[back - 1], gains, inv_rms, w_in, sums)
            near = after(near, sums)
        terms = history_terms(cache, near, far, row_lengths, spot_at(-back), steps, terms)
    terms = lax.all_to_all(terms, "tensor", 0, 0, tiled=True)
    terms = terms.reshape(owners * steps * rows, channels)
    for back in range(outer_size // 2, outer_size - 1):
        ahead = w_out if back == outer_size - 2 else None
        sums = projected(spot_at(-back), streams[back], gains, inv_rms, w_in, sums, ahead=ahead)
    sums, w_out = sums
    ends = (steps, near_taps, place, terms)
    gated = projected(spot_at(1 - outer_size), streams[-1], gains, inv_rms, w_in, sums, ends)

    def spot_to(ahead, flip):
        return ((outer + ahead) % outer_size * INNER + (inner + flip) % INNER)[None].astype(jnp.int32)

    order = sorted(range(outer_size), key=lambda ahead: (ahead == 0, -min(ahead, outer_size - ahead)))
    across = {
        ahead: moved(output_share(spot_to(ahead, 1), gated, w_out, owners), 0, 1) for ahead in order
    }
    out = stream
    for ahead in order:
        share = output_share(spot_to(ahead, 0), gated, w_out, owners, across[ahead])
        out = out + (moved(share, ahead, 0) if ahead else share).astype(jnp.float32)
    return out.astype(jnp.bfloat16).reshape(steps, seqs, channels)


def solution(mesh):
    in_specs = (
        P(None, ("groups", "batch")),
        P(None, "tensor"),
        P("tensor"),
        P(None, "tensor"),
        P("tensor", None),
        P("tensor", None),
        P(("groups", "tensor", "batch"), None, None),
        P("groups"),
        P(("groups", "batch")),
    )
    out_specs = P(None, ("groups", "batch"), "tensor")
    return jax.shard_map(
        per_device, mesh=mesh, in_specs=in_specs, out_specs=out_specs, check_vma=False
    )
```

```python
import functools

import jax
import jax.numpy as jnp
from jax import lax
from jax.experimental import pallas as pl
from jax.experimental.pallas import tpu as pltpu
from jax.sharding import PartitionSpec as P

D = 8192
EPSILON = 1e-05
LANES = 128
INNER = 2
DEPTH = 3
VMEM_LIMIT = 16 * 1024 * 1024
IN_SMEM = pl.BlockSpec(memory_space=pltpu.SMEM)
IN_VMEM = pl.BlockSpec(memory_space=pltpu.VMEM)
IN_HBM = pl.BlockSpec(memory_space=pltpu.HBM)


def moved(array, outer_by, flip):
    owners = lax.axis_size("tensor")
    outer_size = owners // INNER
    pairs = []
    for source in range(owners):
        outer, inner = source // INNER, source % INNER
        pairs.append((source, (outer + outer_by) % outer_size * INNER + (inner ^ flip)))
    return lax.ppermute(array, "tensor", pairs)


def spread(block):
    outer_size = lax.axis_size("tensor") // INNER
    forward = backward = block
    blocks = [(0, block, moved(block, 0, 1))]
    for step in range(1, outer_size // 2 + 1):
        forward = moved(forward, 1, 0)
        blocks.append((step, forward, moved(forward, 0, 1)))
        if step < outer_size - step:
            backward = moved(backward, -1, 0)
            blocks.append((-step, backward, moved(backward, 0, 1)))
    return blocks


def kernel_call(kernel, name, spot, operands, outputs, aliases, scratch, flops, moved_bytes):
    specs, args = zip(*operands)
    args = [
        pltpu.with_memory_space_constraint(arg, pltpu.HBM) if spec is IN_HBM else arg
        for spec, arg in operands
    ]
    out_specs, out_shape = zip(*outputs)
    return pl.pallas_call(
        kernel,
        in_specs=[IN_SMEM, *specs],
        out_specs=list(out_specs),
        out_shape=list(out_shape),
        input_output_aliases=aliases,
        scratch_shapes=scratch,
        compiler_params=pltpu.CompilerParams(vmem_limit_bytes=VMEM_LIMIT),
        cost_estimate=pl.CostEstimate(flops=flops, bytes_accessed=moved_bytes, transcendentals=0),
        name=name,
    )(spot, *args)


def history_kernel(steps, first, spot, lengths_ref, near_ref, far_ref, cache_hbm, *refs):
    terms_ref, held, taps_scr, sems = refs if first else refs[1:]
    if not first:
        terms_ref[...] = refs[0][...]
    _, lags, rows, width = held.shape
    channels = near_ref.shape[1]
    parts = channels // width
    lengths = jnp.concatenate([lengths_ref[...]] * (width // LANES), axis=1)

    def owner_of(flip):
        return spot[0] * INNER + (spot[1] + flip) % INNER

    def fetch(index):
        start = (owner_of(index // parts) * parts + index % parts) * width
        columns = pl.ds(pl.multiple_of(start, width), width)
        return pltpu.make_async_copy(cache_hbm.at[:, :, columns], held.at[index], sems.at[index])

    for index in range(2 * parts):
        fetch(index).start()

    def one_part(index, carry):
        fetch(index).wait()
        flip = index // parts
        at = pl.ds(pl.multiple_of(index % parts * width, width), width)

        @pl.when(flip == 0)
        def _():
            taps_scr[...] = near_ref[pl.ds(0, lags + 1), at].astype(jnp.float32)

        @pl.when(flip == 1)
        def _():
            taps_scr[...] = far_ref[pl.ds(0, lags + 1), at].astype(jnp.float32)

        def tap(lag):
            return jnp.broadcast_to(taps_scr[pl.ds(lag, 1), :], (rows, width))

        taps = [tap(1 + step) for step in range(steps)]
        sums = [jnp.zeros((rows, width), jnp.float32) for _ in range(steps)]
        for lag in range(lags):
            values = jnp.where(lengths > lag, held[index, lag].astype(jnp.float32), 0.0)
            for step in range(min(steps, lags - lag)):
                sums[step] += values * taps[step]
            taps = taps[1:]
            if lag + 1 + steps <= lags:
                taps.append(tap(lag + 1 + steps))
        for step in range(steps):
            terms_ref[owner_of(flip), step, :, at] = sums[step].astype(terms_ref.dtype)
        return carry

    lax.fori_loop(0, 2 * parts, one_part, 0)


def history_terms(cache, near, far, lengths, spot, steps, earlier):
    lags, rows, total = cache.shape
    channels = near.shape[1]
    width = min(4 * LANES, channels)
    count = 2 * channels // width
    operands = [(IN_VMEM, lengths), (IN_VMEM, near), (IN_VMEM, far), (IN_HBM, cache)]
    aliases = {}
    if earlier is not None:
        aliases = {len(operands) + 1: 0}
        operands.append((IN_VMEM, earlier))
    shape = (total // channels, steps, rows, channels)
    return kernel_call(
        functools.partial(history_kernel, steps, earlier is None),
        "history_terms",
        spot,
        operands,
        [(IN_VMEM, jax.ShapeDtypeStruct(shape, jnp.bfloat16))],
        aliases,
        [
            pltpu.VMEM((count, lags, rows, width), jnp.bfloat16),
            pltpu.VMEM((lags + 1, width), jnp.float32),
            pltpu.SemaphoreType.DMA((count,)),
        ],
        2400 * steps * rows * lags * channels // 2,
        4 * rows * lags * channels,
    )[0]


def project_kernel(steps, first, last, spot, near, far, gain_ref, inv_ref, w_hbm, *refs):
    refs = list(refs)
    earlier = None if first else refs.pop(0)
    taps_ref, place_ref, terms_any = (refs.pop(0) for _ in range(3)) if last else (None,) * 3
    total_ref = refs.pop(0)
    gated_ref = refs.pop(0) if last else None
    blocks, normed, held, sems, block_sems, extra_sem, *terms_scr = refs
    _, rows, channels = blocks.shape
    slots, depth, block = held.shape
    chunks = 3 * channels // block
    in_rows = pl.ds(pl.multiple_of(spot[0] * depth, depth), depth)

    def fetch(chunk):
        columns = pl.ds(pl.multiple_of(chunk * block, block), block)
        slot = lax.rem(chunk, slots)
        return pltpu.make_async_copy(w_hbm.at[in_rows, columns], held.at[slot], sems.at[slot])

    copies = [
        pltpu.make_async_copy(x_any, blocks.at[flip], block_sems.at[flip])
        for flip, x_any in enumerate((near, far))
    ]
    for copy in copies:
        copy.start()
    for chunk in range(min(slots, chunks)):
        fetch(chunk).start()
    if last:
        extra = pltpu.make_async_copy(terms_any, terms_scr[0], extra_sem.at[0])
        extra.start()

    scale = inv_ref[:, :1]
    for flip, copy in enumerate(copies):
        copy.wait()
        inner = (spot[1] + flip) % INNER
        gain = gain_ref[pl.ds(spot[0] * INNER + inner, 1), :]
        normed[:, pl.ds(pl.multiple_of(inner * channels, channels), channels)] = (
            blocks[flip].astype(jnp.float32) * scale * gain
        ).astype(jnp.bfloat16)

    def one_chunk(chunk, carry):
        fetch(chunk).wait()
        columns = pl.ds(pl.multiple_of(chunk * block, block), block)
        term = jnp.dot(
            normed[...], held[lax.rem(chunk, slots)], preferred_element_type=jnp.float32
        )
        total_ref[:, columns] = term if first else earlier[:, columns] + term

        @pl.when(chunk + slots < chunks)
        def _():
            fetch(chunk + slots).start()

        return carry

    lax.fori_loop(0, chunks, one_chunk, 0)
    if not last:
        return
    extra.wait()
    seqs = rows // steps
    wide = min(256, channels)

    def one_gate(chunk, carry):
        start = pl.multiple_of(chunk * wide, wide)
        at = pl.ds(start, wide)
        history = jnp.dot(place_ref[...], terms_scr[0][:, at], preferred_element_type=jnp.float32)
        keys = total_ref[:, pl.ds(pl.multiple_of(channels + start, wide), wide)]
        values = total_ref[:, pl.ds(pl.multiple_of(2 * channels + start, wide), wide)]
        recent = (keys * values).astype(jnp.bfloat16).astype(jnp.float32)
        for step in range(steps):
            rows_at = pl.ds(step * seqs, seqs)
            filtered = history[step * seqs : (step + 1) * seqs]
            for back in range(step + 1):
                older = recent[(step - back) * seqs : (step - back + 1) * seqs]
                filtered += taps_ref[pl.ds(back, 1), at] * older
            gated_ref[rows_at, at] = (total_ref[rows_at, at] * filtered).astype(jnp.bfloat16)
        return carry

    lax.fori_loop(0, channels // wide, one_gate, 0)


def projected(spot, pair, gains, inv_rms, w_in, earlier, ends=None):
    near, far = pair
    rows, channels = near.shape
    block = min(512, channels)
    first, last = earlier is None, ends is not None
    operands = [(IN_HBM, near), (IN_HBM, far), (IN_VMEM, gains), (IN_VMEM, inv_rms), (IN_HBM, w_in)]
    aliases = {}
    if not first:
        aliases = {len(operands) + 1: 0}
        operands.append((IN_VMEM, earlier))
    outputs = [(IN_VMEM, jax.ShapeDtypeStruct((rows, 3 * channels), jnp.float32))]
    scratch = [
        pltpu.VMEM((INNER, rows, channels), jnp.bfloat16),
        pltpu.VMEM((rows, INNER * channels), jnp.bfloat16),
        pltpu.VMEM((DEPTH, INNER * channels, block), jnp.bfloat16),
        pltpu.SemaphoreType.DMA((DEPTH,)),
        pltpu.SemaphoreType.DMA((INNER,)),
        pltpu.SemaphoreType.DMA((1,)),
    ]
    steps = 1
    if last:
        steps, taps, place, terms = ends
        operands += [(IN_VMEM, taps), (IN_VMEM, place), (IN_HBM, terms)]
        outputs.append((IN_VMEM, jax.ShapeDtypeStruct((rows, channels), jnp.bfloat16)))
        scratch.append(pltpu.VMEM(terms.shape, jnp.bfloat16))
    return kernel_call(
        functools.partial(project_kernel, steps, first, last),
        "gated_rows" if last else "projected_part",
        spot,
        operands,
        outputs,
        aliases,
        scratch,
        4 * rows * INNER * channels * 3 * channels,
        4 * INNER * channels * 3 * channels,
    )[-1]


def share_kernel(spot, x_ref, w_hbm, *refs):
    *outs, held, sems = refs
    wide = outs[0].shape[1]
    slots, _, block = held.shape
    parts = wide // block
    chunks = len(outs) * parts

    def fetch(chunk):
        start = pl.multiple_of(spot[chunk // parts] * wide + chunk % parts * block, block)
        slot = chunk % slots
        return pltpu.make_async_copy(w_hbm.at[:, pl.ds(start, block)], held.at[slot], sems.at[slot])

    for chunk in range(min(slots, chunks)):
        fetch(chunk).start()
    for chunk in range(chunks):
        fetch(chunk).wait()
        out_ref = outs[chunk // parts]
        share = jnp.dot(x_ref[...], held[chunk % slots], preferred_element_type=jnp.float32)
        out_ref[:, pl.ds(chunk % parts * block, block)] = share.astype(out_ref.dtype)
        if chunk + slots < chunks:
            fetch(chunk + slots).start()


def output_shares(targets, gated, w_out, owners):
    rows, channels = gated.shape
    wide = w_out.shape[1] // owners
    block = min(512, wide)
    return kernel_call(
        share_kernel,
        "output_shares",
        jnp.stack([which for which, _ in targets]).astype(jnp.int32),
        [(IN_VMEM, gated), (IN_HBM, w_out)],
        [(IN_VMEM, jax.ShapeDtypeStruct((rows, wide), kind)) for _, kind in targets],
        {},
        [pltpu.VMEM((DEPTH, channels, block), jnp.bfloat16), pltpu.SemaphoreType.DMA((DEPTH,))],
        2 * rows * channels * wide * len(targets),
        2 * channels * wide * len(targets),
    )


def after(array, earlier):
    return lax.optimization_barrier((array, earlier))[0]


def per_device(token_ids, embed, norm_gain, w_in, filters, w_out, cache_rows, owner, lengths):
    steps, seqs = token_ids.shape
    vocab, channels = embed.shape
    rows = cache_rows.shape[0]
    tokens = steps * seqs
    owners = lax.axis_size("tensor")
    halves = lax.axis_size("batch")
    mine = lax.axis_index("tensor")
    half = lax.axis_index("batch")
    outer, inner, outer_size = mine // INNER, mine % INNER, owners // INNER

    onehot = token_ids.reshape(-1)[:, None] == jnp.arange(vocab, dtype=jnp.int32)[None, :]
    stream = jnp.dot(onehot.astype(jnp.bfloat16), embed, preferred_element_type=jnp.float32)
    tiny = jnp.concatenate([norm_gain.astype(jnp.float32), jnp.sum(stream * stream, axis=1)])
    tiny = tiny.reshape(-1, LANES)
    tiny = lax.all_to_all(
        jnp.broadcast_to(tiny[None], (owners, *tiny.shape)), "tensor", 0, 0, tiled=True
    )
    gain_rows = channels // LANES
    gains = tiny[:, :gain_rows].reshape(owners, channels)
    inv_rms = lax.rsqrt(jnp.sum(tiny[:, gain_rows:], axis=0).reshape(tokens) / D + EPSILON)
    inv_rms = jnp.broadcast_to(inv_rms[:, None], (tokens, LANES))
    own_taps = filters.T
    lag_taps = spread(own_taps)
    streams = spread(after(stream.astype(jnp.bfloat16), own_taps))

    def spot_at(back):
        return jnp.stack([(outer + back) % outer_size, inner]).astype(jnp.int32)

    owner_grid = owner.reshape(owners, halves, rows)
    arrived = lax.dynamic_index_in_dim(owner_grid, half, 1, keepdims=False) - half * seqs
    seq_index = jnp.arange(seqs, dtype=jnp.int32)
    own = lax.dynamic_index_in_dim(arrived, mine, 0, keepdims=False)
    row_lengths = jnp.sum(jnp.where(own[:, None] == seq_index[None, :], lengths[None, :], 0), axis=1)
    row_lengths = jnp.broadcast_to(row_lengths[:, None], (rows, LANES))
    step_index = jnp.arange(steps, dtype=jnp.int32)
    place = (
        (step_index[:, None, None, None, None] == step_index[None, None, None, :, None])
        & (seq_index[None, :, None, None, None] == arrived[None, None, :, None, :])
    ).reshape(tokens, owners * steps * rows)
    place = place.astype(jnp.bfloat16)

    cache = cache_rows.transpose(1, 0, 2)
    near_taps = filters[:, : 2 * steps].T.astype(jnp.float32)
    terms = sums = None
    parts = len(streams)
    for index, (back, near, far) in enumerate(lag_taps):
        if index:
            near = after(near, sums)
        terms = history_terms(cache, near, far, row_lengths, spot_at(-back), steps, terms)
        if 2 * index < parts:
            at, *pair = streams[index]
            pair[0] = after(pair[0], terms)
            sums = projected(spot_at(-at), pair, gains, inv_rms, w_in, sums)
    terms = lax.all_to_all(terms, "tensor", 0, 0, tiled=True)
    terms = terms.reshape(owners * steps * rows, channels)
    for index in range((parts + 1) // 2, parts):
        at, *pair = streams[index]
        ends = (steps, near_taps, place, terms) if index == parts - 1 else None
        sums = projected(spot_at(-at), pair, gains, inv_rms, w_in, sums, ends)
    gated = sums

    def owner_at(ahead, flip):
        return (outer + ahead) % outer_size * INNER + (inner + flip) % INNER

    order = sorted(range(outer_size), key=lambda ahead: (ahead == 0, -min(ahead, outer_size - ahead)))
    targets = [(owner_at(ahead, 1), jnp.bfloat16) for ahead in order]
    targets += [(owner_at(ahead, 0), jnp.float32) for ahead in order]
    shares = list(output_shares(targets[:2], gated, w_out, owners))
    across = [moved(share, 0, 1) for share in shares]
    for start in range(2, len(targets), 6):
        shares += output_shares(targets[start : start + 6], gated, w_out, owners)
    across += [moved(share, 0, 1) for share in shares[2:outer_size]]
    out = stream
    for ahead, own_share, arrived_share in zip(order, shares[outer_size:], across):
        share = own_share + arrived_share.astype(jnp.float32)
        out = out + (moved(share.astype(jnp.bfloat16), ahead, 0) if ahead else share)
    return out.astype(jnp.bfloat16).reshape(steps, seqs, channels)


def solution(mesh):
    in_specs = (
        P(None, ("groups", "batch")),
        P(None, "tensor"),
        P("tensor"),
        P(None, "tensor"),
        P("tensor", None),
        P("tensor", None),
        P(("groups", "tensor", "batch"), None, None),
        P("groups"),
        P(("groups", "batch")),
    )
    out_specs = P(None, ("groups", "batch"), "tensor")
    return jax.shard_map(
        per_device, mesh=mesh, in_specs=in_specs, out_specs=out_specs, check_vma=False
    )
```

```python
import functools

import jax
import jax.numpy as jnp
from jax import lax
from jax.experimental import pallas as pl
from jax.experimental.pallas import tpu as pltpu
from jax.sharding import PartitionSpec as P

D = 8192
EPSILON = 1e-05
LANES = 128
INNER = 2
DEPTH = 3
VMEM_LIMIT = 16 * 1024 * 1024
LARGE_LIMIT = 30 * 1024 * 1024
IN_SMEM = pl.BlockSpec(memory_space=pltpu.SMEM)
IN_VMEM = pl.BlockSpec(memory_space=pltpu.VMEM)
IN_HBM = pl.BlockSpec(memory_space=pltpu.HBM)


def moved(array, outer_by, flip):
    owners = lax.axis_size("tensor")
    outer_size = owners // INNER
    pairs = []
    for source in range(owners):
        outer, inner = source // INNER, source % INNER
        pairs.append((source, (outer + outer_by) % outer_size * INNER + (inner ^ flip)))
    return lax.ppermute(array, "tensor", pairs)


def spread(block):
    outer_size = lax.axis_size("tensor") // INNER
    forward = backward = block
    blocks = [(0, block, moved(block, 0, 1))]
    for step in range(1, outer_size // 2 + 1):
        forward = moved(forward, 1, 0)
        blocks.append((step, forward, moved(forward, 0, 1)))
        if step < outer_size - step:
            backward = moved(backward, -1, 0)
            blocks.append((-step, backward, moved(backward, 0, 1)))
    return blocks


def kernel_call(kernel, name, spot, operands, outputs, aliases, scratch, flops, moved_bytes, limit=VMEM_LIMIT):
    specs, args = zip(*operands)
    args = [
        pltpu.with_memory_space_constraint(arg, pltpu.HBM) if spec is IN_HBM else arg
        for spec, arg in operands
    ]
    out_specs, out_shape = zip(*outputs)
    return pl.pallas_call(
        kernel,
        in_specs=[IN_SMEM, *specs],
        out_specs=list(out_specs),
        out_shape=list(out_shape),
        input_output_aliases=aliases,
        scratch_shapes=scratch,
        compiler_params=pltpu.CompilerParams(vmem_limit_bytes=limit),
        cost_estimate=pl.CostEstimate(flops=flops, bytes_accessed=moved_bytes, transcendentals=0),
        name=name,
    )(spot, *args)


def history_kernel(steps, first, spot, lengths_ref, near_ref, far_ref, cache_hbm, *refs):
    terms_ref, held, taps_scr, sems = refs if first else refs[1:]
    if not first:
        terms_ref[...] = refs[0][...]
    _, lags, rows, width = held.shape
    channels = near_ref.shape[1]
    parts = channels // width
    lengths = jnp.concatenate([lengths_ref[...]] * (width // LANES), axis=1)

    def owner_of(flip):
        return spot[0] * INNER + (spot[1] + flip) % INNER

    def fetch(index):
        start = (owner_of(index // parts) * parts + index % parts) * width
        columns = pl.ds(pl.multiple_of(start, width), width)
        return pltpu.make_async_copy(cache_hbm.at[:, :, columns], held.at[index], sems.at[index])

    for index in range(2 * parts):
        fetch(index).start()

    def one_part(index, carry):
        fetch(index).wait()
        flip = index // parts
        at = pl.ds(pl.multiple_of(index % parts * width, width), width)

        @pl.when(flip == 0)
        def _():
            taps_scr[...] = near_ref[pl.ds(0, lags + 1), at].astype(jnp.float32)

        @pl.when(flip == 1)
        def _():
            taps_scr[...] = far_ref[pl.ds(0, lags + 1), at].astype(jnp.float32)

        def tap(lag):
            return jnp.broadcast_to(taps_scr[pl.ds(lag, 1), :], (rows, width))

        taps = [tap(1 + step) for step in range(steps)]
        sums = [jnp.zeros((rows, width), jnp.float32) for _ in range(steps)]
        for lag in range(lags):
            values = jnp.where(lengths > lag, held[index, lag].astype(jnp.float32), 0.0)
            for step in range(min(steps, lags - lag)):
                sums[step] += values * taps[step]
            taps = taps[1:]
            if lag + 1 + steps <= lags:
                taps.append(tap(lag + 1 + steps))
        for step in range(steps):
            terms_ref[owner_of(flip), step, :, at] = sums[step].astype(terms_ref.dtype)
        return carry

    lax.fori_loop(0, 2 * parts, one_part, 0)


def history_terms(cache, near, far, lengths, spot, steps, earlier):
    lags, rows, total = cache.shape
    channels = near.shape[1]
    width = min(4 * LANES, channels)
    count = 2 * channels // width
    operands = [(IN_VMEM, lengths), (IN_VMEM, near), (IN_VMEM, far), (IN_HBM, cache)]
    aliases = {}
    if earlier is not None:
        aliases = {len(operands) + 1: 0}
        operands.append((IN_VMEM, earlier))
    shape = (total // channels, steps, rows, channels)
    return kernel_call(
        functools.partial(history_kernel, steps, earlier is None),
        "history_terms",
        spot,
        operands,
        [(IN_VMEM, jax.ShapeDtypeStruct(shape, jnp.bfloat16))],
        aliases,
        [
            pltpu.VMEM((count, lags, rows, width), jnp.bfloat16),
            pltpu.VMEM((lags + 1, width), jnp.float32),
            pltpu.SemaphoreType.DMA((count,)),
        ],
        2400 * steps * rows * lags * channels // 2,
        4 * rows * lags * channels,
    )[0]


def project_kernel(steps, first, last, spot, near, far, gain_ref, inv_ref, w_hbm, *refs):
    refs = list(refs)
    earlier = None if first else refs.pop(0)
    taps_ref, place_ref, terms_hbm, out_hbm = (refs.pop(0) for _ in range(4)) if last else (None,) * 4
    total_ref = refs.pop(0)
    gated_ref = refs.pop(0) if last else None
    shares = []
    while last and len(refs) > 9:
        shares.append(refs.pop(0))
    blocks, normed, held, sems, block_sems, *last_scr = refs
    if last:
        terms_ref, out_held, terms_sem, out_sems = last_scr
    _, rows, channels = blocks.shape
    slots, depth, block = held.shape
    chunks = 3 * channels // block
    in_rows = pl.ds(pl.multiple_of(spot[0] * depth, depth), depth)

    def fetch(chunk):
        columns = pl.ds(pl.multiple_of(chunk * block, block), block)
        slot = lax.rem(chunk, slots)
        return pltpu.make_async_copy(w_hbm.at[in_rows, columns], held.at[slot], sems.at[slot])

    copies = [
        pltpu.make_async_copy(x_any, blocks.at[flip], block_sems.at[flip])
        for flip, x_any in enumerate((near, far))
    ]
    for copy in copies:
        copy.start()
    for chunk in range(min(slots, chunks)):
        fetch(chunk).start()
    if last:
        terms_copy = pltpu.make_async_copy(terms_hbm, terms_ref, terms_sem.at[0])
        terms_copy.start()

    def fetch_out(index):
        start = pl.multiple_of(spot[2 + index] * shares[0].shape[1], shares[0].shape[1])
        columns = pl.ds(start, shares[0].shape[1])
        return pltpu.make_async_copy(out_hbm.at[:, columns], out_held.at[index], out_sems.at[index])


    scale = inv_ref[:, :1]
    for flip, copy in enumerate(copies):
        copy.wait()
        inner = (spot[1] + flip) % INNER
        gain = gain_ref[pl.ds(spot[0] * INNER + inner, 1), :]
        normed[:, pl.ds(pl.multiple_of(inner * channels, channels), channels)] = (
            blocks[flip].astype(jnp.float32) * scale * gain
        ).astype(jnp.bfloat16)

    def one_chunk(chunk, carry):
        fetch(chunk).wait()
        columns = pl.ds(pl.multiple_of(chunk * block, block), block)
        term = jnp.dot(
            normed[...], held[lax.rem(chunk, slots)], preferred_element_type=jnp.float32
        )
        total_ref[:, columns] = term if first else earlier[:, columns] + term

        @pl.when(chunk + slots < chunks)
        def _():
            fetch(chunk + slots).start()

        for index in range(len(shares)):

            @pl.when(chunk == index % chunks)
            def _():
                fetch_out(index).start()

        return carry

    lax.fori_loop(0, chunks, one_chunk, 0)
    if not last:
        return
    terms_copy.wait()
    seqs = rows // steps
    wide = min(256, channels)

    def one_gate(chunk, carry):
        start = pl.multiple_of(chunk * wide, wide)
        at = pl.ds(start, wide)
        history = jnp.dot(place_ref[...], terms_ref[:, at], preferred_element_type=jnp.float32)
        keys = total_ref[:, pl.ds(pl.multiple_of(channels + start, wide), wide)]
        values = total_ref[:, pl.ds(pl.multiple_of(2 * channels + start, wide), wide)]
        recent = (keys * values).astype(jnp.bfloat16).astype(jnp.float32)
        for step in range(steps):
            rows_at = pl.ds(step * seqs, seqs)
            filtered = history[step * seqs : (step + 1) * seqs]
            for back in range(step + 1):
                older = recent[(step - back) * seqs : (step - back + 1) * seqs]
                filtered += taps_ref[pl.ds(back, 1), at] * older
            gated_ref[rows_at, at] = (total_ref[rows_at, at] * filtered).astype(jnp.bfloat16)
        return carry

    lax.fori_loop(0, channels // wide, one_gate, 0)
    for index, share_ref in enumerate(shares):
        fetch_out(index).wait()
        width = share_ref.shape[1]
        for start in range(0, width, block):
            columns = pl.ds(start, min(block, width))
            share = jnp.dot(
                gated_ref[...], out_held[index, :, columns], preferred_element_type=jnp.float32
            )
            share_ref[:, columns] = share.astype(share_ref.dtype)


def projected(spot, pair, gains, inv_rms, w_in, earlier, ends=None):
    near, far = pair
    rows, channels = near.shape
    block = min(512, channels)
    first, last = earlier is None, ends is not None
    operands = [(IN_HBM, near), (IN_HBM, far), (IN_VMEM, gains), (IN_VMEM, inv_rms), (IN_HBM, w_in)]
    aliases = {}
    if not first:
        aliases = {len(operands) + 1: 0}
        operands.append((IN_VMEM, earlier))
    outputs = [(IN_VMEM, jax.ShapeDtypeStruct((rows, 3 * channels), jnp.float32))]
    scratch = [
        pltpu.VMEM((INNER, rows, channels), jnp.bfloat16),
        pltpu.VMEM((rows, INNER * channels), jnp.bfloat16),
        pltpu.VMEM((DEPTH, INNER * channels, block), jnp.bfloat16),
        pltpu.SemaphoreType.DMA((DEPTH,)),
        pltpu.SemaphoreType.DMA((INNER,)),
    ]
    steps = 1
    if last:
        steps, taps, place, terms, w_out, targets = ends
        operands += [(IN_VMEM, taps), (IN_VMEM, place), (IN_HBM, terms), (IN_HBM, w_out)]
        outputs.append((IN_VMEM, jax.ShapeDtypeStruct((rows, channels), jnp.bfloat16)))
        wide = w_out.shape[1] * channels // w_in.shape[0]
        outputs += [(IN_VMEM, jax.ShapeDtypeStruct((rows, wide), jnp.bfloat16)) for _ in targets]
        spot = jnp.concatenate([spot, jnp.stack(targets).astype(jnp.int32)])
        scratch += [
            pltpu.VMEM(terms.shape, jnp.bfloat16),
            pltpu.VMEM((len(targets), channels, wide), jnp.bfloat16),
            pltpu.SemaphoreType.DMA((1,)),
            pltpu.SemaphoreType.DMA((len(targets),)),
        ]
    out = kernel_call(
        functools.partial(project_kernel, steps, first, last),
        "gated_rows" if last else "projected_part",
        spot,
        operands,
        outputs,
        aliases,
        scratch,
        4 * rows * INNER * channels * 3 * channels,
        4 * INNER * channels * 3 * channels,
        LARGE_LIMIT if last else VMEM_LIMIT,
    )
    return out[1:] if last else out[0]


def share_kernel(spot, x_ref, w_hbm, *refs):
    *outs, held, sems = refs
    wide = outs[0].shape[1]
    slots, _, block = held.shape
    parts = wide // block
    chunks = len(outs) * parts

    def fetch(chunk):
        start = pl.multiple_of(spot[chunk // parts] * wide + chunk % parts * block, block)
        slot = chunk % slots
        return pltpu.make_async_copy(w_hbm.at[:, pl.ds(start, block)], held.at[slot], sems.at[slot])

    for chunk in range(min(slots, chunks)):
        fetch(chunk).start()
    for chunk in range(chunks):
        fetch(chunk).wait()
        out_ref = outs[chunk // parts]
        share = jnp.dot(x_ref[...], held[chunk % slots], preferred_element_type=jnp.float32)
        out_ref[:, pl.ds(chunk % parts * block, block)] = share.astype(out_ref.dtype)
        if chunk + slots < chunks:
            fetch(chunk + slots).start()


def output_shares(targets, gated, w_out, owners):
    rows, channels = gated.shape
    wide = w_out.shape[1] // owners
    block = min(512, wide)
    return kernel_call(
        share_kernel,
        "output_shares",
        jnp.stack(targets).astype(jnp.int32),
        [(IN_VMEM, gated), (IN_HBM, w_out)],
        [(IN_VMEM, jax.ShapeDtypeStruct((rows, wide), jnp.float32)) for _ in targets],
        {},
        [pltpu.VMEM((DEPTH, channels, block), jnp.bfloat16), pltpu.SemaphoreType.DMA((DEPTH,))],
        2 * rows * channels * wide * len(targets),
        2 * channels * wide * len(targets),
    )


def after(array, earlier):
    return lax.optimization_barrier((array, earlier))[0]


def per_device(token_ids, embed, norm_gain, w_in, filters, w_out, cache_rows, owner, lengths):
    steps, seqs = token_ids.shape
    vocab, channels = embed.shape
    rows = cache_rows.shape[0]
    tokens = steps * seqs
    owners = lax.axis_size("tensor")
    halves = lax.axis_size("batch")
    mine = lax.axis_index("tensor")
    half = lax.axis_index("batch")
    outer, inner, outer_size = mine // INNER, mine % INNER, owners // INNER

    onehot = token_ids.reshape(-1)[:, None] == jnp.arange(vocab, dtype=jnp.int32)[None, :]
    stream = jnp.dot(onehot.astype(jnp.bfloat16), embed, preferred_element_type=jnp.float32)
    tiny = jnp.concatenate([norm_gain.astype(jnp.float32), jnp.sum(stream * stream, axis=1)])
    tiny = tiny.reshape(-1, LANES)
    tiny = lax.all_to_all(
        jnp.broadcast_to(tiny[None], (owners, *tiny.shape)), "tensor", 0, 0, tiled=True
    )
    own_taps = filters.T
    lag_taps = spread(own_taps)
    streams = spread(after(stream.astype(jnp.bfloat16), own_taps))

    def spot_at(back):
        return jnp.stack([(outer + back) % outer_size, inner]).astype(jnp.int32)

    owner_grid = owner.reshape(owners, halves, rows)
    arrived = lax.dynamic_index_in_dim(owner_grid, half, 1, keepdims=False) - half * seqs
    seq_index = jnp.arange(seqs, dtype=jnp.int32)
    own = lax.dynamic_index_in_dim(arrived, mine, 0, keepdims=False)
    row_lengths = jnp.sum(jnp.where(own[:, None] == seq_index[None, :], lengths[None, :], 0), axis=1)
    row_lengths = jnp.broadcast_to(row_lengths[:, None], (rows, LANES))
    step_index = jnp.arange(steps, dtype=jnp.int32)
    place = (
        (step_index[:, None, None, None, None] == step_index[None, None, None, :, None])
        & (seq_index[None, :, None, None, None] == arrived[None, None, :, None, :])
    ).reshape(tokens, owners * steps * rows)
    place = place.astype(jnp.bfloat16)

    cache = cache_rows.transpose(1, 0, 2)
    near_taps = filters[:, : 2 * steps].T.astype(jnp.float32)
    def owner_at(ahead, flip):
        return (outer + ahead) % outer_size * INNER + (inner + flip) % INNER

    order = sorted(range(outer_size), key=lambda ahead: (ahead == 0, -min(ahead, outer_size - ahead)))
    first_terms = history_terms(cache, *lag_taps[0][1:], row_lengths, spot_at(0), steps, None)
    tiny = after(tiny, first_terms)
    gain_rows = channels // LANES
    gains = tiny[:, :gain_rows].reshape(owners, channels)
    inv_rms = lax.rsqrt(jnp.sum(tiny[:, gain_rows:], axis=0).reshape(tokens) / D + EPSILON)
    inv_rms = jnp.broadcast_to(inv_rms[:, None], (tokens, LANES))

    terms, sums = first_terms, None
    parts = len(streams)
    for index, (back, near, far) in enumerate(lag_taps):
        if index:
            near = after(near, sums)
            terms = history_terms(cache, near, far, row_lengths, spot_at(-back), steps, terms)
        if 2 * index < parts:
            at, *pair = streams[index]
            pair[0] = after(pair[0], terms)
            sums = projected(spot_at(-at), pair, gains, inv_rms, w_in, sums)
    terms = lax.all_to_all(terms, "tensor", 0, 0, tiled=True)
    terms = terms.reshape(owners * steps * rows, channels)
    for index in range((parts + 1) // 2, parts):
        at, *pair = streams[index]
        ends = None
        if index == parts - 1:
            targets = [owner_at(ahead, 1) for ahead in order]
            ends = (steps, near_taps, place, terms, w_out, targets)
        sums = projected(spot_at(-at), pair, gains, inv_rms, w_in, sums, ends)
    gated, *across = sums

    across = [moved(share, 0, 1) for share in across]
    own_shares = output_shares([owner_at(ahead, 0) for ahead in order], gated, w_out, owners)
    out = stream
    for ahead, own_share, arrived_share in zip(order, own_shares, across):
        share = own_share + arrived_share.astype(jnp.float32)
        out = out + (moved(share.astype(jnp.bfloat16), ahead, 0) if ahead else share)
    return out.astype(jnp.bfloat16).reshape(steps, seqs, channels)


def solution(mesh):
    in_specs = (
        P(None, ("groups", "batch")),
        P(None, "tensor"),
        P("tensor"),
        P(None, "tensor"),
        P("tensor", None),
        P("tensor", None),
        P(("groups", "tensor", "batch"), None, None),
        P("groups"),
        P(("groups", "batch")),
    )
    out_specs = P(None, ("groups", "batch"), "tensor")
    return jax.shard_map(
        per_device, mesh=mesh, in_specs=in_specs, out_specs=out_specs, check_vma=False
    )
```

```python
import functools

import jax
import jax.numpy as jnp
from jax import lax
from jax.experimental import pallas as pl
from jax.experimental.pallas import tpu as pltpu
from jax.sharding import PartitionSpec as P

D = 8192
EPSILON = 1e-05
LANES = 128
INNER = 2
DEPTH = 3
VMEM_LIMIT = 16 * 1024 * 1024
SHARE_LIMIT = 28 * 1024 * 1024
IN_SMEM = pl.BlockSpec(memory_space=pltpu.SMEM)
IN_VMEM = pl.BlockSpec(memory_space=pltpu.VMEM)
IN_HBM = pl.BlockSpec(memory_space=pltpu.HBM)


def moved(array, outer_by, flip):
    owners = lax.axis_size("tensor")
    outer_size = owners // INNER
    pairs = []
    for source in range(owners):
        outer, inner = source // INNER, source % INNER
        pairs.append((source, (outer + outer_by) % outer_size * INNER + (inner ^ flip)))
    return lax.ppermute(array, "tensor", pairs)


def spread(block):
    outer_size = lax.axis_size("tensor") // INNER
    forward = backward = block
    blocks = [(0, block, moved(block, 0, 1))]
    for step in range(1, outer_size // 2 + 1):
        forward = moved(forward, 1, 0)
        blocks.append((step, forward, moved(forward, 0, 1)))
        if step < outer_size - step:
            backward = moved(backward, -1, 0)
            blocks.append((-step, backward, moved(backward, 0, 1)))
    return blocks


def kernel_call(kernel, name, spot, operands, outputs, aliases, scratch, flops, moved_bytes):
    specs, args = zip(*operands)
    args = [
        pltpu.with_memory_space_constraint(arg, pltpu.HBM) if spec is IN_HBM else arg
        for spec, arg in operands
    ]
    out_specs, out_shape = zip(*outputs)
    return pl.pallas_call(
        kernel,
        in_specs=[IN_SMEM, *specs],
        out_specs=list(out_specs),
        out_shape=list(out_shape),
        input_output_aliases=aliases,
        scratch_shapes=scratch,
        compiler_params=pltpu.CompilerParams(vmem_limit_bytes=VMEM_LIMIT),
        cost_estimate=pl.CostEstimate(flops=flops, bytes_accessed=moved_bytes, transcendentals=0),
        name=name,
    )(spot, *args)


def history_kernel(steps, first, spot, lengths_ref, near_ref, far_ref, cache_hbm, *refs):
    terms_ref, held, taps_scr, sems = refs if first else refs[1:]
    if not first:
        terms_ref[...] = refs[0][...]
    _, lags, rows, width = held.shape
    channels = near_ref.shape[1]
    parts = channels // width
    lengths = jnp.concatenate([lengths_ref[...]] * (width // LANES), axis=1)

    def owner_of(flip):
        return spot[0] * INNER + (spot[1] + flip) % INNER

    def fetch(index):
        start = (owner_of(index // parts) * parts + index % parts) * width
        columns = pl.ds(pl.multiple_of(start, width), width)
        return pltpu.make_async_copy(cache_hbm.at[:, :, columns], held.at[index], sems.at[index])

    for index in range(2 * parts):
        fetch(index).start()

    def one_part(index, carry):
        fetch(index).wait()
        flip = index // parts
        at = pl.ds(pl.multiple_of(index % parts * width, width), width)

        @pl.when(flip == 0)
        def _():
            taps_scr[...] = near_ref[pl.ds(0, lags + 1), at].astype(jnp.float32)

        @pl.when(flip == 1)
        def _():
            taps_scr[...] = far_ref[pl.ds(0, lags + 1), at].astype(jnp.float32)

        def tap(lag):
            return jnp.broadcast_to(taps_scr[pl.ds(lag, 1), :], (rows, width))

        taps = [tap(1 + step) for step in range(steps)]
        sums = [jnp.zeros((rows, width), jnp.float32) for _ in range(steps)]
        for lag in range(lags):
            values = jnp.where(lengths > lag, held[index, lag].astype(jnp.float32), 0.0)
            for step in range(min(steps, lags - lag)):
                sums[step] += values * taps[step]
            taps = taps[1:]
            if lag + 1 + steps <= lags:
                taps.append(tap(lag + 1 + steps))
        for step in range(steps):
            terms_ref[owner_of(flip), step, :, at] = sums[step].astype(terms_ref.dtype)
        return carry

    lax.fori_loop(0, 2 * parts, one_part, 0)


def history_terms(cache, near, far, lengths, spot, steps, earlier):
    lags, rows, total = cache.shape
    channels = near.shape[1]
    width = min(4 * LANES, channels)
    count = 2 * channels // width
    operands = [(IN_VMEM, lengths), (IN_VMEM, near), (IN_VMEM, far), (IN_HBM, cache)]
    aliases = {}
    if earlier is not None:
        aliases = {len(operands) + 1: 0}
        operands.append((IN_VMEM, earlier))
    shape = (total // channels, steps, rows, channels)
    return kernel_call(
        functools.partial(history_kernel, steps, earlier is None),
        "history_terms",
        spot,
        operands,
        [(IN_VMEM, jax.ShapeDtypeStruct(shape, jnp.bfloat16))],
        aliases,
        [
            pltpu.VMEM((count, lags, rows, width), jnp.bfloat16),
            pltpu.VMEM((lags + 1, width), jnp.float32),
            pltpu.SemaphoreType.DMA((count,)),
        ],
        2400 * steps * rows * lags * channels // 2,
        4 * rows * lags * channels,
    )[0]


def project_kernel(steps, first, last, spot, near, far, gain_ref, inv_ref, w_hbm, *refs):
    refs = list(refs)
    earlier = None if first else refs.pop(0)
    taps_ref, place_ref, terms_any = (refs.pop(0) for _ in range(3)) if last else (None,) * 3
    total_ref = refs.pop(0)
    gated_ref = refs.pop(0) if last else None
    blocks, normed, held, sems, block_sems, extra_sem, *terms_scr = refs
    _, rows, channels = blocks.shape
    slots, depth, block = held.shape
    chunks = 3 * channels // block
    in_rows = pl.ds(pl.multiple_of(spot[0] * depth, depth), depth)

    def fetch(chunk):
        columns = pl.ds(pl.multiple_of(chunk * block, block), block)
        slot = lax.rem(chunk, slots)
        return pltpu.make_async_copy(w_hbm.at[in_rows, columns], held.at[slot], sems.at[slot])

    copies = [
        pltpu.make_async_copy(x_any, blocks.at[flip], block_sems.at[flip])
        for flip, x_any in enumerate((near, far))
    ]
    for copy in copies:
        copy.start()
    for chunk in range(min(slots, chunks)):
        fetch(chunk).start()
    if last:
        extra = pltpu.make_async_copy(terms_any, terms_scr[0], extra_sem.at[0])
        extra.start()

    scale = inv_ref[:, :1]
    for flip, copy in enumerate(copies):
        copy.wait()
        inner = (spot[1] + flip) % INNER
        gain = gain_ref[pl.ds(spot[0] * INNER + inner, 1), :]
        normed[:, pl.ds(pl.multiple_of(inner * channels, channels), channels)] = (
            blocks[flip].astype(jnp.float32) * scale * gain
        ).astype(jnp.bfloat16)

    def one_chunk(chunk, carry):
        fetch(chunk).wait()
        columns = pl.ds(pl.multiple_of(chunk * block, block), block)
        term = jnp.dot(
            normed[...], held[lax.rem(chunk, slots)], preferred_element_type=jnp.float32
        )
        total_ref[:, columns] = term if first else earlier[:, columns] + term

        @pl.when(chunk + slots < chunks)
        def _():
            fetch(chunk + slots).start()

        return carry

    lax.fori_loop(0, chunks, one_chunk, 0)
    if not last:
        return
    extra.wait()
    seqs = rows // steps
    wide = min(256, channels)

    def one_gate(chunk, carry):
        start = pl.multiple_of(chunk * wide, wide)
        at = pl.ds(start, wide)
        history = jnp.dot(place_ref[...], terms_scr[0][:, at], preferred_element_type=jnp.float32)
        keys = total_ref[:, pl.ds(pl.multiple_of(channels + start, wide), wide)]
        values = total_ref[:, pl.ds(pl.multiple_of(2 * channels + start, wide), wide)]
        recent = (keys * values).astype(jnp.bfloat16).astype(jnp.float32)
        for step in range(steps):
            rows_at = pl.ds(step * seqs, seqs)
            filtered = history[step * seqs : (step + 1) * seqs]
            for back in range(step + 1):
                older = recent[(step - back) * seqs : (step - back + 1) * seqs]
                filtered += taps_ref[pl.ds(back, 1), at] * older
            gated_ref[rows_at, at] = (total_ref[rows_at, at] * filtered).astype(jnp.bfloat16)
        return carry

    lax.fori_loop(0, channels // wide, one_gate, 0)


def projected(spot, pair, gains, inv_rms, w_in, earlier, ends=None):
    near, far = pair
    rows, channels = near.shape
    block = min(512, channels)
    first, last = earlier is None, ends is not None
    operands = [(IN_HBM, near), (IN_HBM, far), (IN_VMEM, gains), (IN_VMEM, inv_rms), (IN_HBM, w_in)]
    aliases = {}
    if not first:
        aliases = {len(operands) + 1: 0}
        operands.append((IN_VMEM, earlier))
    outputs = [(IN_VMEM, jax.ShapeDtypeStruct((rows, 3 * channels), jnp.float32))]
    scratch = [
        pltpu.VMEM((INNER, rows, channels), jnp.bfloat16),
        pltpu.VMEM((rows, INNER * channels), jnp.bfloat16),
        pltpu.VMEM((DEPTH, INNER * channels, block), jnp.bfloat16),
        pltpu.SemaphoreType.DMA((DEPTH,)),
        pltpu.SemaphoreType.DMA((INNER,)),
        pltpu.SemaphoreType.DMA((1,)),
    ]
    steps = 1
    if last:
        steps, taps, place, terms = ends
        operands += [(IN_VMEM, taps), (IN_VMEM, place), (IN_HBM, terms)]
        outputs.append((IN_VMEM, jax.ShapeDtypeStruct((rows, channels), jnp.bfloat16)))
        scratch.append(pltpu.VMEM(terms.shape, jnp.bfloat16))
    return kernel_call(
        functools.partial(project_kernel, steps, first, last),
        "gated_rows" if last else "projected_part",
        spot,
        operands,
        outputs,
        aliases,
        scratch,
        4 * rows * INNER * channels * 3 * channels,
        4 * INNER * channels * 3 * channels,
    )[-1]


def share_kernel(spot, x_ref, w_ref, *refs):
    share = jnp.dot(x_ref[...], w_ref[...], preferred_element_type=jnp.float32)
    if len(refs) > 1:
        share += refs[0][...].astype(jnp.float32)
    refs[-1][...] = share.astype(refs[-1].dtype)


def output_share(spot, gated, w_out, owners, arrived=None):
    rows, channels = gated.shape
    wide = w_out.shape[1] // owners
    block = min(512, wide)
    blocks = wide // block
    specs = [
        pl.BlockSpec((rows, channels), lambda c, _: (0, 0)),
        pl.BlockSpec((channels, block), lambda c, spot: (0, spot[0] * blocks + c)),
    ]
    args = [gated, w_out]
    if arrived is not None:
        specs.append(pl.BlockSpec((rows, block), lambda c, _: (0, c)))
        args.append(arrived)
    return pl.pallas_call(
        share_kernel,
        grid_spec=pltpu.PrefetchScalarGridSpec(
            num_scalar_prefetch=1,
            grid=(blocks,),
            in_specs=specs,
            out_specs=pl.BlockSpec((rows, block), lambda c, _: (0, c)),
        ),
        out_shape=jax.ShapeDtypeStruct((rows, wide), jnp.bfloat16),
        compiler_params=pltpu.CompilerParams(vmem_limit_bytes=SHARE_LIMIT),
        cost_estimate=pl.CostEstimate(
            flops=2 * rows * channels * wide,
            bytes_accessed=2 * channels * wide,
            transcendentals=0,
        ),
        name="output_share",
    )(spot, *args)


def after(array, earlier):
    return lax.optimization_barrier((array, earlier))[0]


def per_device(token_ids, embed, norm_gain, w_in, filters, w_out, cache_rows, owner, lengths):
    steps, seqs = token_ids.shape
    vocab, channels = embed.shape
    rows = cache_rows.shape[0]
    tokens = steps * seqs
    owners = lax.axis_size("tensor")
    halves = lax.axis_size("batch")
    mine = lax.axis_index("tensor")
    half = lax.axis_index("batch")
    outer, inner, outer_size = mine // INNER, mine % INNER, owners // INNER

    onehot = token_ids.reshape(-1)[:, None] == jnp.arange(vocab, dtype=jnp.int32)[None, :]
    stream = jnp.dot(onehot.astype(jnp.bfloat16), embed, preferred_element_type=jnp.float32)
    tiny = jnp.concatenate([norm_gain.astype(jnp.float32), jnp.sum(stream * stream, axis=1)])
    tiny = tiny.reshape(-1, LANES)
    tiny = lax.all_to_all(
        jnp.broadcast_to(tiny[None], (owners, *tiny.shape)), "tensor", 0, 0, tiled=True
    )
    own_taps = filters.T
    lag_taps = spread(own_taps)
    streams = spread(after(stream.astype(jnp.bfloat16), own_taps))

    def spot_at(back):
        return jnp.stack([(outer + back) % outer_size, inner]).astype(jnp.int32)

    owner_grid = owner.reshape(owners, halves, rows)
    arrived = lax.dynamic_index_in_dim(owner_grid, half, 1, keepdims=False) - half * seqs
    seq_index = jnp.arange(seqs, dtype=jnp.int32)
    own = lax.dynamic_index_in_dim(arrived, mine, 0, keepdims=False)
    row_lengths = jnp.sum(jnp.where(own[:, None] == seq_index[None, :], lengths[None, :], 0), axis=1)
    row_lengths = jnp.broadcast_to(row_lengths[:, None], (rows, LANES))
    step_index = jnp.arange(steps, dtype=jnp.int32)
    place = (
        (step_index[:, None, None, None, None] == step_index[None, None, None, :, None])
        & (seq_index[None, :, None, None, None] == arrived[None, None, :, None, :])
    ).reshape(tokens, owners * steps * rows)
    place = place.astype(jnp.bfloat16)

    cache = cache_rows.transpose(1, 0, 2)
    near_taps = filters[:, : 2 * steps].T.astype(jnp.float32)
    first_terms = history_terms(cache, *lag_taps[0][1:], row_lengths, spot_at(0), steps, None)
    tiny = after(tiny, first_terms)
    gain_rows = channels // LANES
    gains = tiny[:, :gain_rows].reshape(owners, channels)
    inv_rms = lax.rsqrt(jnp.sum(tiny[:, gain_rows:], axis=0).reshape(tokens) / D + EPSILON)
    inv_rms = jnp.broadcast_to(inv_rms[:, None], (tokens, LANES))

    terms, sums = first_terms, None
    parts = len(streams)
    for index, (back, near, far) in enumerate(lag_taps):
        if index:
            near = after(near, sums)
            terms = history_terms(cache, near, far, row_lengths, spot_at(-back), steps, terms)
        if 2 * index < parts:
            at, *pair = streams[index]
            pair[0] = after(pair[0], terms)
            sums = projected(spot_at(-at), pair, gains, inv_rms, w_in, sums)
    terms = lax.all_to_all(terms, "tensor", 0, 0, tiled=True)
    terms = terms.reshape(owners * steps * rows, channels)
    for index in range((parts + 1) // 2, parts):
        at, *pair = streams[index]
        ends = (steps, near_taps, place, terms) if index == parts - 1 else None
        sums = projected(spot_at(-at), pair, gains, inv_rms, w_in, sums, ends)
    gated = sums

    def spot_to(ahead, flip):
        return ((outer + ahead) % outer_size * INNER + (inner + flip) % INNER)[None].astype(jnp.int32)

    order = sorted(range(outer_size), key=lambda ahead: (ahead == 0, -min(ahead, outer_size - ahead)))
    across = {
        ahead: moved(output_share(spot_to(ahead, 1), gated, w_out, owners), 0, 1) for ahead in order
    }
    out = stream
    for ahead in order:
        share = output_share(spot_to(ahead, 0), gated, w_out, owners, across[ahead])
        out = out + (moved(share, ahead, 0) if ahead else share).astype(jnp.float32)
    return out.astype(jnp.bfloat16).reshape(steps, seqs, channels)


def solution(mesh):
    in_specs = (
        P(None, ("groups", "batch")),
        P(None, "tensor"),
        P("tensor"),
        P(None, "tensor"),
        P("tensor", None),
        P("tensor", None),
        P(("groups", "tensor", "batch"), None, None),
        P("groups"),
        P(("groups", "batch")),
    )
    out_specs = P(None, ("groups", "batch"), "tensor")
    return jax.shard_map(
        per_device, mesh=mesh, in_specs=in_specs, out_specs=out_specs, check_vma=False
    )
```

```python
import functools

import jax
import jax.numpy as jnp
from jax import lax
from jax.experimental import pallas as pl
from jax.experimental.pallas import tpu as pltpu
from jax.sharding import PartitionSpec as P

D = 8192
EPSILON = 1e-05
LANES = 128
INNER = 2
DEPTH = 3
VMEM_LIMIT = 16 * 1024 * 1024
IN_SMEM = pl.BlockSpec(memory_space=pltpu.SMEM)
IN_VMEM = pl.BlockSpec(memory_space=pltpu.VMEM)
IN_HBM = pl.BlockSpec(memory_space=pltpu.HBM)


def moved(array, outer_by, flip):
    owners = lax.axis_size("tensor")
    outer_size = owners // INNER
    pairs = []
    for source in range(owners):
        outer, inner = source // INNER, source % INNER
        pairs.append((source, (outer + outer_by) % outer_size * INNER + (inner ^ flip)))
    return lax.ppermute(array, "tensor", pairs)


def spread(block):
    outer_size = lax.axis_size("tensor") // INNER
    forward = backward = block
    blocks = [(0, block, moved(block, 0, 1))]
    for step in range(1, outer_size // 2 + 1):
        forward = moved(forward, 1, 0)
        blocks.append((step, forward, moved(forward, 0, 1)))
        if step < outer_size - step:
            backward = moved(backward, -1, 0)
            blocks.append((-step, backward, moved(backward, 0, 1)))
    return blocks


def kernel_call(kernel, name, spot, operands, outputs, aliases, scratch, flops, moved_bytes):
    specs, args = zip(*operands)
    args = [
        pltpu.with_memory_space_constraint(arg, pltpu.HBM) if spec is IN_HBM else arg
        for spec, arg in operands
    ]
    out_specs, out_shape = zip(*outputs)
    return pl.pallas_call(
        kernel,
        in_specs=[IN_SMEM, *specs],
        out_specs=list(out_specs),
        out_shape=list(out_shape),
        input_output_aliases=aliases,
        scratch_shapes=scratch,
        compiler_params=pltpu.CompilerParams(vmem_limit_bytes=VMEM_LIMIT),
        cost_estimate=pl.CostEstimate(flops=flops, bytes_accessed=moved_bytes, transcendentals=0),
        name=name,
    )(spot, *args)


def history_kernel(steps, first, spot, lengths_ref, near_ref, far_ref, cache_hbm, *refs):
    terms_ref, held, taps_scr, sems = refs if first else refs[1:]
    if not first:
        terms_ref[...] = refs[0][...]
    _, lags, rows, width = held.shape
    channels = near_ref.shape[1]
    parts = channels // width
    lengths = jnp.concatenate([lengths_ref[...]] * (width // LANES), axis=1)

    def owner_of(flip):
        return spot[0] * INNER + (spot[1] + flip) % INNER

    def fetch(index):
        start = (owner_of(index // parts) * parts + index % parts) * width
        columns = pl.ds(pl.multiple_of(start, width), width)
        return pltpu.make_async_copy(cache_hbm.at[:, :, columns], held.at[index], sems.at[index])

    for index in range(2 * parts):
        fetch(index).start()

    def one_part(index, carry):
        fetch(index).wait()
        flip = index // parts
        at = pl.ds(pl.multiple_of(index % parts * width, width), width)

        @pl.when(flip == 0)
        def _():
            taps_scr[...] = near_ref[pl.ds(0, lags + 1), at].astype(jnp.float32)

        @pl.when(flip == 1)
        def _():
            taps_scr[...] = far_ref[pl.ds(0, lags + 1), at].astype(jnp.float32)

        def tap(lag):
            return jnp.broadcast_to(taps_scr[pl.ds(lag, 1), :], (rows, width))

        taps = [tap(1 + step) for step in range(steps)]
        sums = [jnp.zeros((rows, width), jnp.float32) for _ in range(steps)]
        for lag in range(lags):
            values = jnp.where(lengths > lag, held[index, lag].astype(jnp.float32), 0.0)
            for step in range(min(steps, lags - lag)):
                sums[step] += values * taps[step]
            taps = taps[1:]
            if lag + 1 + steps <= lags:
                taps.append(tap(lag + 1 + steps))
        for step in range(steps):
            terms_ref[owner_of(flip), step, :, at] = sums[step].astype(terms_ref.dtype)
        return carry

    lax.fori_loop(0, 2 * parts, one_part, 0)


def history_terms(cache, near, far, lengths, spot, steps, earlier):
    lags, rows, total = cache.shape
    channels = near.shape[1]
    width = min(4 * LANES, channels)
    count = 2 * channels // width
    operands = [(IN_VMEM, lengths), (IN_VMEM, near), (IN_VMEM, far), (IN_HBM, cache)]
    aliases = {}
    if earlier is not None:
        aliases = {len(operands) + 1: 0}
        operands.append((IN_VMEM, earlier))
    shape = (total // channels, steps, rows, channels)
    return kernel_call(
        functools.partial(history_kernel, steps, earlier is None),
        "history_terms",
        spot,
        operands,
        [(IN_VMEM, jax.ShapeDtypeStruct(shape, jnp.bfloat16))],
        aliases,
        [
            pltpu.VMEM((count, lags, rows, width), jnp.bfloat16),
            pltpu.VMEM((lags + 1, width), jnp.float32),
            pltpu.SemaphoreType.DMA((count,)),
        ],
        2400 * steps * rows * lags * channels // 2,
        4 * rows * lags * channels,
    )[0]


def project_kernel(steps, first, last, spot, near, far, gain_ref, inv_ref, w_hbm, *refs):
    refs = list(refs)
    earlier = None if first else refs.pop(0)
    taps_ref, place_ref, terms_any = (refs.pop(0) for _ in range(3)) if last else (None,) * 3
    total_ref = refs.pop(0)
    gated_ref = refs.pop(0) if last else None
    blocks, normed, held, sems, block_sems, extra_sem, *terms_scr = refs
    _, rows, channels = blocks.shape
    slots, depth, block = held.shape
    chunks = 3 * channels // block
    in_rows = pl.ds(pl.multiple_of(spot[0] * depth, depth), depth)

    def fetch(chunk):
        columns = pl.ds(pl.multiple_of(chunk * block, block), block)
        slot = lax.rem(chunk, slots)
        return pltpu.make_async_copy(w_hbm.at[in_rows, columns], held.at[slot], sems.at[slot])

    copies = [
        pltpu.make_async_copy(x_any, blocks.at[flip], block_sems.at[flip])
        for flip, x_any in enumerate((near, far))
    ]
    for copy in copies:
        copy.start()
    for chunk in range(min(slots, chunks)):
        fetch(chunk).start()
    if last:
        extra = pltpu.make_async_copy(terms_any, terms_scr[0], extra_sem.at[0])
        extra.start()

    scale = inv_ref[:, :1]
    for flip, copy in enumerate(copies):
        copy.wait()
        inner = (spot[1] + flip) % INNER
        gain = gain_ref[pl.ds(spot[0] * INNER + inner, 1), :]
        normed[:, pl.ds(pl.multiple_of(inner * channels, channels), channels)] = (
            blocks[flip].astype(jnp.float32) * scale * gain
        ).astype(jnp.bfloat16)

    def one_chunk(chunk, carry):
        fetch(chunk).wait()
        columns = pl.ds(pl.multiple_of(chunk * block, block), block)
        term = jnp.dot(
            normed[...], held[lax.rem(chunk, slots)], preferred_element_type=jnp.float32
        )
        total_ref[:, columns] = term if first else earlier[:, columns] + term

        @pl.when(chunk + slots < chunks)
        def _():
            fetch(chunk + slots).start()

        return carry

    lax.fori_loop(0, chunks, one_chunk, 0)
    if not last:
        return
    extra.wait()
    seqs = rows // steps
    wide = min(256, channels)

    def one_gate(chunk, carry):
        start = pl.multiple_of(chunk * wide, wide)
        at = pl.ds(start, wide)
        history = jnp.dot(place_ref[...], terms_scr[0][:, at], preferred_element_type=jnp.float32)
        keys = total_ref[:, pl.ds(pl.multiple_of(channels + start, wide), wide)]
        values = total_ref[:, pl.ds(pl.multiple_of(2 * channels + start, wide), wide)]
        recent = (keys * values).astype(jnp.bfloat16).astype(jnp.float32)
        for step in range(steps):
            rows_at = pl.ds(step * seqs, seqs)
            filtered = history[step * seqs : (step + 1) * seqs]
            for back in range(step + 1):
                older = recent[(step - back) * seqs : (step - back + 1) * seqs]
                filtered += taps_ref[pl.ds(back, 1), at] * older
            gated_ref[rows_at, at] = (total_ref[rows_at, at] * filtered).astype(jnp.bfloat16)
        return carry

    lax.fori_loop(0, channels // wide, one_gate, 0)


def projected(spot, pair, gains, inv_rms, w_in, earlier, ends=None):
    near, far = pair
    rows, channels = near.shape
    block = min(512, channels)
    first, last = earlier is None, ends is not None
    operands = [(IN_HBM, near), (IN_HBM, far), (IN_VMEM, gains), (IN_VMEM, inv_rms), (IN_HBM, w_in)]
    aliases = {}
    if not first:
        aliases = {len(operands) + 1: 0}
        operands.append((IN_VMEM, earlier))
    outputs = [(IN_VMEM, jax.ShapeDtypeStruct((rows, 3 * channels), jnp.float32))]
    scratch = [
        pltpu.VMEM((INNER, rows, channels), jnp.bfloat16),
        pltpu.VMEM((rows, INNER * channels), jnp.bfloat16),
        pltpu.VMEM((DEPTH, INNER * channels, block), jnp.bfloat16),
        pltpu.SemaphoreType.DMA((DEPTH,)),
        pltpu.SemaphoreType.DMA((INNER,)),
        pltpu.SemaphoreType.DMA((1,)),
    ]
    steps = 1
    if last:
        steps, taps, place, terms = ends
        operands += [(IN_VMEM, taps), (IN_VMEM, place), (IN_HBM, terms)]
        outputs.append((IN_VMEM, jax.ShapeDtypeStruct((rows, channels), jnp.bfloat16)))
        scratch.append(pltpu.VMEM(terms.shape, jnp.bfloat16))
    return kernel_call(
        functools.partial(project_kernel, steps, first, last),
        "gated_rows" if last else "projected_part",
        spot,
        operands,
        outputs,
        aliases,
        scratch,
        4 * rows * INNER * channels * 3 * channels,
        4 * INNER * channels * 3 * channels,
    )[-1]


def share_kernel(spot, x_ref, w_ref, *outs):
    wide = outs[0].shape[1]
    block = min(512, wide)
    for index, out_ref in enumerate(outs):
        for start in range(0, wide, block):
            columns = pl.ds(pl.multiple_of(spot[index] * wide + start, block), block)
            share = jnp.dot(x_ref[...], w_ref[:, columns], preferred_element_type=jnp.float32)
            out_ref[:, pl.ds(start, block)] = share.astype(out_ref.dtype)


def output_shares(targets, gated, w_out, owners):
    rows, channels = gated.shape
    wide = w_out.shape[1] // owners
    return kernel_call(
        share_kernel,
        "output_shares",
        jnp.stack([which for which, _ in targets]).astype(jnp.int32),
        [(IN_VMEM, gated), (IN_VMEM, w_out)],
        [(IN_VMEM, jax.ShapeDtypeStruct((rows, wide), kind)) for _, kind in targets],
        {},
        [],
        2 * rows * channels * wide * len(targets),
        2 * channels * wide * len(targets),
    )


def after(array, earlier):
    return lax.optimization_barrier((array, earlier))[0]


def per_device(token_ids, embed, norm_gain, w_in, filters, w_out, cache_rows, owner, lengths):
    steps, seqs = token_ids.shape
    vocab, channels = embed.shape
    rows = cache_rows.shape[0]
    tokens = steps * seqs
    owners = lax.axis_size("tensor")
    halves = lax.axis_size("batch")
    mine = lax.axis_index("tensor")
    half = lax.axis_index("batch")
    outer, inner, outer_size = mine // INNER, mine % INNER, owners // INNER

    onehot = token_ids.reshape(-1)[:, None] == jnp.arange(vocab, dtype=jnp.int32)[None, :]
    stream = jnp.dot(onehot.astype(jnp.bfloat16), embed, preferred_element_type=jnp.float32)
    tiny = jnp.concatenate([norm_gain.astype(jnp.float32), jnp.sum(stream * stream, axis=1)])
    tiny = tiny.reshape(-1, LANES)
    tiny = lax.all_to_all(
        jnp.broadcast_to(tiny[None], (owners, *tiny.shape)), "tensor", 0, 0, tiled=True
    )
    own_taps = filters.T
    lag_taps = spread(own_taps)
    streams = spread(after(stream.astype(jnp.bfloat16), own_taps))

    def spot_at(back):
        return jnp.stack([(outer + back) % outer_size, inner]).astype(jnp.int32)

    owner_grid = owner.reshape(owners, halves, rows)
    arrived = lax.dynamic_index_in_dim(owner_grid, half, 1, keepdims=False) - half * seqs
    seq_index = jnp.arange(seqs, dtype=jnp.int32)
    own = lax.dynamic_index_in_dim(arrived, mine, 0, keepdims=False)
    row_lengths = jnp.sum(jnp.where(own[:, None] == seq_index[None, :], lengths[None, :], 0), axis=1)
    row_lengths = jnp.broadcast_to(row_lengths[:, None], (rows, LANES))
    step_index = jnp.arange(steps, dtype=jnp.int32)
    place = (
        (step_index[:, None, None, None, None] == step_index[None, None, None, :, None])
        & (seq_index[None, :, None, None, None] == arrived[None, None, :, None, :])
    ).reshape(tokens, owners * steps * rows)
    place = place.astype(jnp.bfloat16)

    cache = cache_rows.transpose(1, 0, 2)
    first_terms = history_terms(cache, *lag_taps[0][1:], row_lengths, spot_at(0), steps, None)
    near_taps = filters[:, : 2 * steps].T.astype(jnp.float32)
    tiny = after(tiny, (first_terms, place, near_taps))
    gain_rows = channels // LANES
    gains = tiny[:, :gain_rows].reshape(owners, channels)
    inv_rms = lax.rsqrt(jnp.sum(tiny[:, gain_rows:], axis=0).reshape(tokens) / D + EPSILON)
    inv_rms = jnp.broadcast_to(inv_rms[:, None], (tokens, LANES))

    terms, sums = first_terms, None
    parts = len(streams)
    for index, (back, near, far) in enumerate(lag_taps):
        if index:
            near = after(near, sums)
            terms = history_terms(cache, near, far, row_lengths, spot_at(-back), steps, terms)
        if 2 * index < parts:
            at, *pair = streams[index]
            pair[0] = after(pair[0], terms)
            sums = projected(spot_at(-at), pair, gains, inv_rms, w_in, sums)
    terms = lax.all_to_all(terms, "tensor", 0, 0, tiled=True)
    terms = terms.reshape(owners * steps * rows, channels)
    for index in range((parts + 1) // 2, parts):
        at, *pair = streams[index]
        ends = (steps, near_taps, place, terms) if index == parts - 1 else None
        sums = projected(spot_at(-at), pair, gains, inv_rms, w_in, sums, ends)
    gated = sums

    def owner_at(ahead, flip):
        return (outer + ahead) % outer_size * INNER + (inner + flip) % INNER

    order = sorted(range(outer_size), key=lambda ahead: (ahead == 0, -min(ahead, outer_size - ahead)))
    targets = [(owner_at(ahead, 1), jnp.bfloat16) for ahead in order]
    targets += [(owner_at(ahead, 0), jnp.float32) for ahead in order]
    shares = output_shares(targets, gated, w_out, owners)
    across = [moved(share, 0, 1) for share in shares[:outer_size]]
    out = stream
    for ahead, own_share, arrived_share in zip(order, shares[outer_size:], across):
        share = own_share + arrived_share.astype(jnp.float32)
        if ahead:
            share = share.astype(jnp.bfloat16)
        out = out + (moved(share, ahead, 0) if ahead else share).astype(jnp.float32)
    return out.astype(jnp.bfloat16).reshape(steps, seqs, channels)


def solution(mesh):
    in_specs = (
        P(None, ("groups", "batch")),
        P(None, "tensor"),
        P("tensor"),
        P(None, "tensor"),
        P("tensor", None),
        P("tensor", None),
        P(("groups", "tensor", "batch"), None, None),
        P("groups"),
        P(("groups", "batch")),
    )
    out_specs = P(None, ("groups", "batch"), "tensor")
    return jax.shard_map(
        per_device, mesh=mesh, in_specs=in_specs, out_specs=out_specs, check_vma=False
    )
```

```python
import functools

import jax
import jax.numpy as jnp
from jax import lax
from jax.experimental import pallas as pl
from jax.experimental.pallas import tpu as pltpu
from jax.sharding import PartitionSpec as P

D = 8192
EPSILON = 1e-05
LANES = 128
INNER = 2
DEPTH = 3
VMEM_LIMIT = 16 * 1024 * 1024
IN_SMEM = pl.BlockSpec(memory_space=pltpu.SMEM)
IN_VMEM = pl.BlockSpec(memory_space=pltpu.VMEM)
IN_HBM = pl.BlockSpec(memory_space=pltpu.HBM)
ANYWHERE = pl.BlockSpec(memory_space=pl.ANY)


def moved(array, outer_by, flip):
    owners = lax.axis_size("tensor")
    outer_size = owners // INNER
    pairs = []
    for source in range(owners):
        outer, inner = source // INNER, source % INNER
        pairs.append((source, (outer + outer_by) % outer_size * INNER + (inner ^ flip)))
    return lax.ppermute(array, "tensor", pairs)


def spread(block):
    outer_size = lax.axis_size("tensor") // INNER
    forward = backward = block
    blocks = [(0, block, moved(block, 0, 1))]
    for step in range(1, outer_size // 2 + 1):
        forward = moved(forward, 1, 0)
        blocks.append((step, forward, moved(forward, 0, 1)))
        if step < outer_size - step:
            backward = moved(backward, -1, 0)
            blocks.append((-step, backward, moved(backward, 0, 1)))
    return blocks


def kernel_call(kernel, name, spot, operands, outputs, aliases, scratch, flops, moved_bytes):
    specs, args = zip(*operands)
    args = [
        pltpu.with_memory_space_constraint(arg, pltpu.HBM) if spec is IN_HBM else arg
        for spec, arg in operands
    ]
    out_specs, out_shape = zip(*outputs)
    return pl.pallas_call(
        kernel,
        in_specs=[IN_SMEM, *specs],
        out_specs=list(out_specs),
        out_shape=list(out_shape),
        input_output_aliases=aliases,
        scratch_shapes=scratch,
        compiler_params=pltpu.CompilerParams(vmem_limit_bytes=VMEM_LIMIT),
        cost_estimate=pl.CostEstimate(flops=flops, bytes_accessed=moved_bytes, transcendentals=0),
        name=name,
    )(spot, *args)


def history_kernel(steps, count, first, spot, lengths_ref, *refs):
    tap_refs, cache_hbm = refs[:count], refs[count]
    terms_ref, held, taps_scr, sems = refs[-4:]
    if not first:
        terms_ref[...] = refs[count + 1][...]
    slots, lags, rows, width = held.shape
    owners, _, channels = tap_refs[0].shape
    per_owner = terms_ref.shape[3] // width
    at = pl.ds(pl.multiple_of(spot[0] * width, width), width)
    lengths = jnp.concatenate([lengths_ref[...]] * (width // LANES), axis=1)

    def fetch(owner):
        columns = pl.ds(pl.multiple_of((owner * per_owner + spot[0]) * width, width), width)
        slot = lax.rem(owner, slots)
        return pltpu.make_async_copy(cache_hbm.at[:, :, columns], held.at[slot], sems.at[slot])

    for owner in range(min(slots, owners)):
        fetch(owner).start()

    def one_owner(owner, carry):
        for index, tap_ref in enumerate(tap_refs):
            start = pl.multiple_of((spot[1] + index) % count * channels, channels)
            taps_scr[:, pl.ds(start, channels)] = tap_ref[owner].astype(jnp.float32)
        fetch(owner).wait()
        slot = lax.rem(owner, slots)

        def tap(lag):
            return jnp.broadcast_to(taps_scr[pl.ds(lag, 1), :], (rows, width))

        taps = [tap(1 + step) for step in range(steps)]
        sums = [jnp.zeros((rows, width), jnp.float32) for _ in range(steps)]
        for lag in range(lags):
            values = jnp.where(lengths > lag, held[slot, lag].astype(jnp.float32), 0.0)
            for step in range(min(steps, lags - lag)):
                sums[step] += values * taps[step]
            taps = taps[1:]
            if lag + 1 + steps <= lags:
                taps.append(tap(lag + 1 + steps))
        for step in range(steps):
            terms_ref[owner, step, :, at] = sums[step].astype(terms_ref.dtype)

        @pl.when(owner + slots < owners)
        def _():
            fetch(owner + slots).start()

        return carry

    lax.fori_loop(0, owners, one_owner, 0)


def history_terms(cache, tap_parts, lengths, spot, steps, earlier):
    lags, rows, total = cache.shape
    owners, tap_rows, channels = tap_parts[0].shape
    count = len(tap_parts)
    width = count * channels
    operands = [(IN_VMEM, lengths), *[(IN_VMEM, taps) for taps in tap_parts], (IN_HBM, cache)]
    aliases = {}
    if earlier is not None:
        aliases = {len(operands) + 1: 0}
        operands.append((IN_VMEM, earlier))
    shape = (owners, steps, rows, total // owners)
    slots = min(DEPTH, owners)
    return kernel_call(
        functools.partial(history_kernel, steps, count, earlier is None),
        "history_terms",
        spot,
        operands,
        [(IN_VMEM, jax.ShapeDtypeStruct(shape, jnp.bfloat16))],
        aliases,
        [
            pltpu.VMEM((slots, lags, rows, width), jnp.bfloat16),
            pltpu.VMEM((tap_rows, width), jnp.float32),
            pltpu.SemaphoreType.DMA((slots,)),
        ],
        1200 * steps * rows * lags * owners * width // 2,
        2 * rows * lags * owners * width,
    )[0]


def project_kernel(steps, first, last, spot, near, far, gain_ref, inv_ref, w_hbm, *refs):
    refs = list(refs)
    earlier = None if first else refs.pop(0)
    taps_ref, place_ref, terms_any = (refs.pop(0) for _ in range(3)) if last else (None,) * 3
    total_ref = refs.pop(0)
    gated_ref = refs.pop(0) if last else None
    blocks, normed, held, sems, block_sems, extra_sem, *terms_scr = refs
    _, rows, channels = blocks.shape
    slots, depth, block = held.shape
    chunks = 3 * channels // block
    in_rows = pl.ds(pl.multiple_of(spot[0] * depth, depth), depth)

    def fetch(chunk):
        columns = pl.ds(pl.multiple_of(chunk * block, block), block)
        slot = lax.rem(chunk, slots)
        return pltpu.make_async_copy(w_hbm.at[in_rows, columns], held.at[slot], sems.at[slot])

    copies = [
        pltpu.make_async_copy(x_any, blocks.at[flip], block_sems.at[flip])
        for flip, x_any in enumerate((near, far))
    ]
    for copy in copies:
        copy.start()
    for chunk in range(min(slots, chunks)):
        fetch(chunk).start()
    if last:
        extra = pltpu.make_async_copy(terms_any, terms_scr[0], extra_sem.at[0])
        extra.start()

    scale = inv_ref[:, :1]
    for flip, copy in enumerate(copies):
        copy.wait()
        inner = (spot[1] + flip) % INNER
        gain = gain_ref[pl.ds(spot[0] * INNER + inner, 1), :]
        normed[:, pl.ds(pl.multiple_of(inner * channels, channels), channels)] = (
            blocks[flip].astype(jnp.float32) * scale * gain
        ).astype(jnp.bfloat16)

    def one_chunk(chunk, carry):
        fetch(chunk).wait()
        columns = pl.ds(pl.multiple_of(chunk * block, block), block)
        term = jnp.dot(
            normed[...], held[lax.rem(chunk, slots)], preferred_element_type=jnp.float32
        )
        total_ref[:, columns] = term if first else earlier[:, columns] + term

        @pl.when(chunk + slots < chunks)
        def _():
            fetch(chunk + slots).start()

        return carry

    lax.fori_loop(0, chunks, one_chunk, 0)
    if not last:
        return
    extra.wait()
    seqs = rows // steps
    wide = min(256, channels)

    def one_gate(chunk, carry):
        start = pl.multiple_of(chunk * wide, wide)
        at = pl.ds(start, wide)
        history = jnp.dot(place_ref[...], terms_scr[0][:, at], preferred_element_type=jnp.float32)
        keys = total_ref[:, pl.ds(pl.multiple_of(channels + start, wide), wide)]
        values = total_ref[:, pl.ds(pl.multiple_of(2 * channels + start, wide), wide)]
        recent = (keys * values).astype(jnp.bfloat16).astype(jnp.float32)
        for step in range(steps):
            rows_at = pl.ds(step * seqs, seqs)
            filtered = history[step * seqs : (step + 1) * seqs]
            for back in range(step + 1):
                older = recent[(step - back) * seqs : (step - back + 1) * seqs]
                filtered += taps_ref[pl.ds(back, 1), at] * older
            gated_ref[rows_at, at] = (total_ref[rows_at, at] * filtered).astype(jnp.bfloat16)
        return carry

    lax.fori_loop(0, channels // wide, one_gate, 0)


def projected(spot, pair, gains, inv_rms, w_in, earlier, ends=None):
    near, far = pair
    rows, channels = near.shape
    block = min(512, channels)
    first, last = earlier is None, ends is not None
    operands = [(IN_HBM, near), (IN_HBM, far), (IN_VMEM, gains), (IN_VMEM, inv_rms), (IN_HBM, w_in)]
    aliases = {}
    if not first:
        aliases = {len(operands) + 1: 0}
        operands.append((IN_VMEM, earlier))
    outputs = [(IN_VMEM, jax.ShapeDtypeStruct((rows, 3 * channels), jnp.float32))]
    scratch = [
        pltpu.VMEM((INNER, rows, channels), jnp.bfloat16),
        pltpu.VMEM((rows, INNER * channels), jnp.bfloat16),
        pltpu.VMEM((DEPTH, INNER * channels, block), jnp.bfloat16),
        pltpu.SemaphoreType.DMA((DEPTH,)),
        pltpu.SemaphoreType.DMA((INNER,)),
        pltpu.SemaphoreType.DMA((1,)),
    ]
    steps = 1
    if last:
        steps, taps, place, terms = ends
        operands += [(IN_VMEM, taps), (IN_VMEM, place), (IN_HBM, terms)]
        outputs.append((IN_VMEM, jax.ShapeDtypeStruct((rows, channels), jnp.bfloat16)))
        scratch.append(pltpu.VMEM(terms.shape, jnp.bfloat16))
    return kernel_call(
        functools.partial(project_kernel, steps, first, last),
        "gated_rows" if last else "projected_part",
        spot,
        operands,
        outputs,
        aliases,
        scratch,
        4 * rows * INNER * channels * 3 * channels,
        4 * INNER * channels * 3 * channels,
    )[-1]


def share_kernel(spot, x_ref, w_any, *refs):
    *outs, held, sems = refs
    wide = outs[0].shape[1]
    slots, _, block = held.shape
    parts = wide // block
    chunks = len(outs) * parts

    def fetch(chunk):
        start = pl.multiple_of(spot[chunk // parts] * wide + chunk % parts * block, block)
        slot = chunk % slots
        return pltpu.make_async_copy(w_any.at[:, pl.ds(start, block)], held.at[slot], sems.at[slot])

    for chunk in range(min(slots, chunks)):
        fetch(chunk).start()
    for chunk in range(chunks):
        fetch(chunk).wait()
        out_ref = outs[chunk // parts]
        share = jnp.dot(x_ref[...], held[chunk % slots], preferred_element_type=jnp.float32)
        out_ref[:, pl.ds(chunk % parts * block, block)] = share.astype(out_ref.dtype)
        if chunk + slots < chunks:
            fetch(chunk + slots).start()


def output_shares(targets, gated, w_out, owners):
    rows, channels = gated.shape
    wide = w_out.shape[1] // owners
    block = min(512, wide)
    return kernel_call(
        share_kernel,
        "output_shares",
        jnp.stack([which for which, _ in targets]).astype(jnp.int32),
        [(IN_VMEM, gated), (ANYWHERE, w_out)],
        [(IN_VMEM, jax.ShapeDtypeStruct((rows, wide), kind)) for _, kind in targets],
        {},
        [pltpu.VMEM((4, channels, block), jnp.bfloat16), pltpu.SemaphoreType.DMA((4,))],
        2 * rows * channels * wide * len(targets),
        2 * channels * wide * len(targets),
    )


def gathered_taps(filters):
    owners = lax.axis_size("tensor")
    channels = filters.shape[0]
    if lax.axis_size("groups") != 2 or lax.axis_size("batch") != 2 or channels % (4 * LANES):
        return [(0, 0, [lax.all_gather(filters.T, "tensor")])]
    group, half = lax.axis_index("groups"), lax.axis_index("batch")
    quarter = channels // 4
    own = lax.dynamic_slice_in_dim(filters, (group * 2 + half) * quarter, quarter, 0).T
    own = jnp.broadcast_to(own[None], (owners, *own.shape))
    own = lax.all_to_all(own, "tensor", 0, 0, tiled=True)
    swap = [(0, 1), (1, 0)]
    across = lax.ppermute(own, "groups", swap)
    return [
        (group, half, [own, lax.ppermute(own, "batch", swap)]),
        (1 - group, half, [across, lax.ppermute(across, "batch", swap)]),
    ]


def after(array, earlier):
    return lax.optimization_barrier((array, earlier))[0]


def per_device(token_ids, embed, norm_gain, w_in, filters, w_out, cache_rows, owner, lengths):
    steps, seqs = token_ids.shape
    vocab, channels = embed.shape
    rows = cache_rows.shape[0]
    tokens = steps * seqs
    owners = lax.axis_size("tensor")
    halves = lax.axis_size("batch")
    mine = lax.axis_index("tensor")
    half = lax.axis_index("batch")
    outer, inner, outer_size = mine // INNER, mine % INNER, owners // INNER

    onehot = token_ids.reshape(-1)[:, None] == jnp.arange(vocab, dtype=jnp.int32)[None, :]
    stream = jnp.dot(onehot.astype(jnp.bfloat16), embed, preferred_element_type=jnp.float32)
    tiny = jnp.concatenate([norm_gain.astype(jnp.float32), jnp.sum(stream * stream, axis=1)])
    tiny = tiny.reshape(-1, LANES)
    tiny = lax.all_to_all(
        jnp.broadcast_to(tiny[None], (owners, *tiny.shape)), "tensor", 0, 0, tiled=True
    )
    lag_taps = gathered_taps(filters)
    streams = spread(stream.astype(jnp.bfloat16))

    def spot_at(back):
        return jnp.stack([(outer + back) % outer_size, inner]).astype(jnp.int32)

    owner_grid = owner.reshape(owners, halves, rows)
    arrived = lax.dynamic_index_in_dim(owner_grid, half, 1, keepdims=False) - half * seqs
    seq_index = jnp.arange(seqs, dtype=jnp.int32)
    own = lax.dynamic_index_in_dim(arrived, mine, 0, keepdims=False)
    row_lengths = jnp.sum(jnp.where(own[:, None] == seq_index[None, :], lengths[None, :], 0), axis=1)
    row_lengths = jnp.broadcast_to(row_lengths[:, None], (rows, LANES))
    step_index = jnp.arange(steps, dtype=jnp.int32)
    place = (
        (step_index[:, None, None, None, None] == step_index[None, None, None, :, None])
        & (seq_index[None, :, None, None, None] == arrived[None, None, :, None, :])
    ).reshape(tokens, owners * steps * rows)
    place = place.astype(jnp.bfloat16)

    cache = cache_rows.transpose(1, 0, 2)
    def history_part(part, after_these, earlier):
        place_at, first, parts = part
        if after_these is not None:
            parts = [after(parts[0], after_these), *parts[1:]]
        spot = jnp.stack([jnp.int32(place_at), jnp.int32(first)])
        return history_terms(cache, parts, row_lengths, spot, steps, earlier)

    first_terms = history_part(lag_taps[0], None, None)
    near_taps = filters[:, : 2 * steps].T.astype(jnp.float32)
    tiny = after(tiny, (first_terms, place, near_taps))
    gain_rows = channels // LANES
    gains = tiny[:, :gain_rows].reshape(owners, channels)
    inv_rms = lax.rsqrt(jnp.sum(tiny[:, gain_rows:], axis=0).reshape(tokens) / D + EPSILON)
    inv_rms = jnp.broadcast_to(inv_rms[:, None], (tokens, LANES))

    at, *pair = streams[0]
    pair[0] = after(pair[0], first_terms)
    sums = projected(spot_at(-at), pair, gains, inv_rms, w_in, None)
    terms = first_terms
    for part in lag_taps[1:]:
        terms = history_part(part, (sums, streams[1][1]), terms)
    sent = lax.all_to_all(terms, "tensor", 0, 0, tiled=True)
    sent = sent.reshape(owners * steps * rows, channels)
    for index in range(1, len(streams)):
        at, *pair = streams[index]
        if index == 1:
            pair[0] = after(pair[0], (terms, streams[-1][1]))
        ends = (steps, near_taps, place, sent) if index == len(streams) - 1 else None
        sums = projected(spot_at(-at), pair, gains, inv_rms, w_in, sums, ends)
    gated = sums

    def owner_at(ahead, flip):
        return (outer + ahead) % outer_size * INNER + (inner + flip) % INNER

    order = sorted(range(outer_size), key=lambda ahead: (ahead == 0, -min(ahead, outer_size - ahead)))
    targets = [(owner_at(ahead, 1), jnp.bfloat16) for ahead in order]
    targets += [(owner_at(ahead, 0), jnp.float32) for ahead in order]
    shares = output_shares(targets, gated, w_out, owners)
    across = [moved(share, 0, 1) for share in shares[:outer_size]]
    out = stream
    for ahead, own_share, arrived_share in zip(order, shares[outer_size:], across):
        share = own_share + arrived_share.astype(jnp.float32)
        if ahead:
            share = share.astype(jnp.bfloat16)
        out = out + (moved(share, ahead, 0) if ahead else share).astype(jnp.float32)
    return out.astype(jnp.bfloat16).reshape(steps, seqs, channels)


def solution(mesh):
    in_specs = (
        P(None, ("groups", "batch")),
        P(None, "tensor"),
        P("tensor"),
        P(None, "tensor"),
        P("tensor", None),
        P("tensor", None),
        P(("groups", "tensor", "batch"), None, None),
        P("groups"),
        P(("groups", "batch")),
    )
    out_specs = P(None, ("groups", "batch"), "tensor")
    return jax.shard_map(
        per_device, mesh=mesh, in_specs=in_specs, out_specs=out_specs, check_vma=False
    )
```

```python
import functools

import jax
import jax.numpy as jnp
from jax import lax
from jax.experimental import pallas as pl
from jax.experimental.pallas import tpu as pltpu
from jax.sharding import PartitionSpec as P

D = 8192
EPSILON = 1e-05
LANES = 128
INNER = 2
DEPTH = 3
VMEM_LIMIT = 16 * 1024 * 1024
IN_SMEM = pl.BlockSpec(memory_space=pltpu.SMEM)
IN_VMEM = pl.BlockSpec(memory_space=pltpu.VMEM)
IN_HBM = pl.BlockSpec(memory_space=pltpu.HBM)


def moved(array, outer_by, flip):
    owners = lax.axis_size("tensor")
    outer_size = owners // INNER
    pairs = []
    for source in range(owners):
        outer, inner = source // INNER, source % INNER
        pairs.append((source, (outer + outer_by) % outer_size * INNER + (inner ^ flip)))
    return lax.ppermute(array, "tensor", pairs)


def spread(block):
    outer_size = lax.axis_size("tensor") // INNER
    forward = backward = block
    blocks = [(0, block, moved(block, 0, 1))]
    for step in range(1, outer_size // 2 + 1):
        forward = moved(forward, 1, 0)
        blocks.append((step, forward, moved(forward, 0, 1)))
        if step < outer_size - step:
            backward = moved(backward, -1, 0)
            blocks.append((-step, backward, moved(backward, 0, 1)))
    return blocks


def kernel_call(kernel, name, spot, operands, outputs, aliases, scratch, flops, moved_bytes):
    specs, args = zip(*operands)
    args = [
        pltpu.with_memory_space_constraint(arg, pltpu.HBM) if spec is IN_HBM else arg
        for spec, arg in operands
    ]
    out_specs, out_shape = zip(*outputs)
    return pl.pallas_call(
        kernel,
        in_specs=[IN_SMEM, *specs],
        out_specs=list(out_specs),
        out_shape=list(out_shape),
        input_output_aliases=aliases,
        scratch_shapes=scratch,
        compiler_params=pltpu.CompilerParams(vmem_limit_bytes=VMEM_LIMIT),
        cost_estimate=pl.CostEstimate(flops=flops, bytes_accessed=moved_bytes, transcendentals=0),
        name=name,
    )(spot, *args)


def history_kernel(steps, count, first, spot, lengths_ref, *refs):
    tap_refs, cache_hbm = refs[:count], refs[count]
    terms_ref, held, taps_scr, sems = refs[-4:]
    if not first:
        terms_ref[...] = refs[count + 1][...]
    slots, lags, rows, width = held.shape
    owners, _, channels = tap_refs[0].shape
    per_owner = terms_ref.shape[3] // width
    at = pl.ds(pl.multiple_of(spot[0] * width, width), width)
    lengths = jnp.concatenate([lengths_ref[...]] * (width // LANES), axis=1)

    def fetch(owner):
        columns = pl.ds(pl.multiple_of((owner * per_owner + spot[0]) * width, width), width)
        slot = lax.rem(owner, slots)
        return pltpu.make_async_copy(cache_hbm.at[:, :, columns], held.at[slot], sems.at[slot])

    for owner in range(min(slots, owners)):
        fetch(owner).start()

    def one_owner(owner, carry):
        for index, tap_ref in enumerate(tap_refs):
            start = pl.multiple_of((spot[1] + index) % count * channels, channels)
            taps_scr[:, pl.ds(start, channels)] = tap_ref[owner].astype(jnp.float32)
        fetch(owner).wait()
        slot = lax.rem(owner, slots)

        def tap(lag):
            return jnp.broadcast_to(taps_scr[pl.ds(lag, 1), :], (rows, width))

        taps = [tap(1 + step) for step in range(steps)]
        sums = [jnp.zeros((rows, width), jnp.float32) for _ in range(steps)]
        for lag in range(lags):
            values = jnp.where(lengths > lag, held[slot, lag].astype(jnp.float32), 0.0)
            for step in range(min(steps, lags - lag)):
                sums[step] += values * taps[step]
            taps = taps[1:]
            if lag + 1 + steps <= lags:
                taps.append(tap(lag + 1 + steps))
        for step in range(steps):
            terms_ref[owner, step, :, at] = sums[step].astype(terms_ref.dtype)

        @pl.when(owner + slots < owners)
        def _():
            fetch(owner + slots).start()

        return carry

    lax.fori_loop(0, owners, one_owner, 0)


def history_terms(cache, tap_parts, lengths, spot, steps, earlier):
    lags, rows, total = cache.shape
    owners, tap_rows, channels = tap_parts[0].shape
    count = len(tap_parts)
    width = count * channels
    operands = [(IN_VMEM, lengths), *[(IN_VMEM, taps) for taps in tap_parts], (IN_HBM, cache)]
    aliases = {}
    if earlier is not None:
        aliases = {len(operands) + 1: 0}
        operands.append((IN_VMEM, earlier))
    shape = (owners, steps, rows, total // owners)
    slots = min(DEPTH, owners)
    return kernel_call(
        functools.partial(history_kernel, steps, count, earlier is None),
        "history_terms",
        spot,
        operands,
        [(IN_VMEM, jax.ShapeDtypeStruct(shape, jnp.bfloat16))],
        aliases,
        [
            pltpu.VMEM((slots, lags, rows, width), jnp.bfloat16),
            pltpu.VMEM((tap_rows, width), jnp.float32),
            pltpu.SemaphoreType.DMA((slots,)),
        ],
        1200 * steps * rows * lags * owners * width // 2,
        2 * rows * lags * owners * width,
    )[0]


def project_kernel(steps, first, last, spot, near, far, gain_ref, inv_ref, w_hbm, *refs):
    refs = list(refs)
    earlier = None if first else refs.pop(0)
    taps_ref, place_ref, terms_any = (refs.pop(0) for _ in range(3)) if last else (None,) * 3
    total_ref = refs.pop(0)
    gated_ref = refs.pop(0) if last else None
    blocks, normed, held, sems, block_sems, extra_sem, *terms_scr = refs
    _, rows, channels = blocks.shape
    slots, depth, block = held.shape
    chunks = 3 * channels // block
    in_rows = pl.ds(pl.multiple_of(spot[0] * depth, depth), depth)

    def fetch(chunk):
        columns = pl.ds(pl.multiple_of(chunk * block, block), block)
        slot = lax.rem(chunk, slots)
        return pltpu.make_async_copy(w_hbm.at[in_rows, columns], held.at[slot], sems.at[slot])

    copies = [
        pltpu.make_async_copy(x_any, blocks.at[flip], block_sems.at[flip])
        for flip, x_any in enumerate((near, far))
    ]
    for copy in copies:
        copy.start()
    for chunk in range(min(slots, chunks)):
        fetch(chunk).start()
    if last:
        extra = pltpu.make_async_copy(terms_any, terms_scr[0], extra_sem.at[0])
        extra.start()

    scale = inv_ref[:, :1]
    for flip, copy in enumerate(copies):
        copy.wait()
        inner = (spot[1] + flip) % INNER
        gain = gain_ref[pl.ds(spot[0] * INNER + inner, 1), :]
        normed[:, pl.ds(pl.multiple_of(inner * channels, channels), channels)] = (
            blocks[flip].astype(jnp.float32) * scale * gain
        ).astype(jnp.bfloat16)

    def one_chunk(chunk, carry):
        fetch(chunk).wait()
        columns = pl.ds(pl.multiple_of(chunk * block, block), block)
        term = jnp.dot(
            normed[...], held[lax.rem(chunk, slots)], preferred_element_type=jnp.float32
        )
        total_ref[:, columns] = term if first else earlier[:, columns] + term

        @pl.when(chunk + slots < chunks)
        def _():
            fetch(chunk + slots).start()

        return carry

    lax.fori_loop(0, chunks, one_chunk, 0)
    if not last:
        return
    extra.wait()
    seqs = rows // steps
    wide = min(256, channels)

    def one_gate(chunk, carry):
        start = pl.multiple_of(chunk * wide, wide)
        at = pl.ds(start, wide)
        history = jnp.dot(place_ref[...], terms_scr[0][:, at], preferred_element_type=jnp.float32)
        keys = total_ref[:, pl.ds(pl.multiple_of(channels + start, wide), wide)]
        values = total_ref[:, pl.ds(pl.multiple_of(2 * channels + start, wide), wide)]
        recent = (keys * values).astype(jnp.bfloat16).astype(jnp.float32)
        for step in range(steps):
            rows_at = pl.ds(step * seqs, seqs)
            filtered = history[step * seqs : (step + 1) * seqs]
            for back in range(step + 1):
                older = recent[(step - back) * seqs : (step - back + 1) * seqs]
                filtered += taps_ref[pl.ds(back, 1), at] * older
            gated_ref[rows_at, at] = (total_ref[rows_at, at] * filtered).astype(jnp.bfloat16)
        return carry

    lax.fori_loop(0, channels // wide, one_gate, 0)


def projected(spot, pair, gains, inv_rms, w_in, earlier, ends=None):
    near, far = pair
    rows, channels = near.shape
    block = min(512, channels)
    first, last = earlier is None, ends is not None
    operands = [(IN_HBM, near), (IN_HBM, far), (IN_VMEM, gains), (IN_VMEM, inv_rms), (IN_HBM, w_in)]
    aliases = {}
    if not first:
        aliases = {len(operands) + 1: 0}
        operands.append((IN_VMEM, earlier))
    outputs = [(IN_VMEM, jax.ShapeDtypeStruct((rows, 3 * channels), jnp.float32))]
    scratch = [
        pltpu.VMEM((INNER, rows, channels), jnp.bfloat16),
        pltpu.VMEM((rows, INNER * channels), jnp.bfloat16),
        pltpu.VMEM((DEPTH, INNER * channels, block), jnp.bfloat16),
        pltpu.SemaphoreType.DMA((DEPTH,)),
        pltpu.SemaphoreType.DMA((INNER,)),
        pltpu.SemaphoreType.DMA((1,)),
    ]
    steps = 1
    if last:
        steps, taps, place, terms = ends
        operands += [(IN_VMEM, taps), (IN_VMEM, place), (IN_HBM, terms)]
        outputs.append((IN_VMEM, jax.ShapeDtypeStruct((rows, channels), jnp.bfloat16)))
        scratch.append(pltpu.VMEM(terms.shape, jnp.bfloat16))
    return kernel_call(
        functools.partial(project_kernel, steps, first, last),
        "gated_rows" if last else "projected_part",
        spot,
        operands,
        outputs,
        aliases,
        scratch,
        4 * rows * INNER * channels * 3 * channels,
        4 * INNER * channels * 3 * channels,
    )[-1]


def share_kernel(spot, x_ref, w_ref, *outs):
    wide = outs[0].shape[1]
    block = min(512, wide)
    for index, out_ref in enumerate(outs):
        for start in range(0, wide, block):
            columns = pl.ds(pl.multiple_of(spot[index] * wide + start, block), block)
            share = jnp.dot(x_ref[...], w_ref[:, columns], preferred_element_type=jnp.float32)
            out_ref[:, pl.ds(start, block)] = share.astype(out_ref.dtype)


def output_shares(targets, gated, w_out, owners):
    rows, channels = gated.shape
    wide = w_out.shape[1] // owners
    return kernel_call(
        share_kernel,
        "output_shares",
        jnp.stack([which for which, _ in targets]).astype(jnp.int32),
        [(IN_VMEM, gated), (IN_VMEM, w_out)],
        [(IN_VMEM, jax.ShapeDtypeStruct((rows, wide), kind)) for _, kind in targets],
        {},
        [],
        2 * rows * channels * wide * len(targets),
        2 * channels * wide * len(targets),
    )


def gathered_taps(filters):
    owners = lax.axis_size("tensor")
    channels = filters.shape[0]
    if lax.axis_size("groups") != 2 or lax.axis_size("batch") != 2 or channels % (4 * LANES):
        return [(0, 0, [lax.all_gather(filters.T, "tensor")])]
    group, half = lax.axis_index("groups"), lax.axis_index("batch")
    quarter = channels // 4
    own = lax.dynamic_slice_in_dim(filters, (group * 2 + half) * quarter, quarter, 0).T
    own = jnp.broadcast_to(own[None], (owners, *own.shape))
    own = lax.all_to_all(own, "tensor", 0, 0, tiled=True)
    swap = [(0, 1), (1, 0)]
    across = lax.ppermute(own, "groups", swap)
    return [
        (group, half, [own, lax.ppermute(own, "batch", swap)]),
        (1 - group, half, [across, lax.ppermute(across, "batch", swap)]),
    ]


def after(array, earlier):
    return lax.optimization_barrier((array, earlier))[0]


def per_device(token_ids, embed, norm_gain, w_in, filters, w_out, cache_rows, owner, lengths):
    steps, seqs = token_ids.shape
    vocab, channels = embed.shape
    rows = cache_rows.shape[0]
    tokens = steps * seqs
    owners = lax.axis_size("tensor")
    halves = lax.axis_size("batch")
    mine = lax.axis_index("tensor")
    half = lax.axis_index("batch")
    outer, inner, outer_size = mine // INNER, mine % INNER, owners // INNER

    onehot = token_ids.reshape(-1)[:, None] == jnp.arange(vocab, dtype=jnp.int32)[None, :]
    stream = jnp.dot(onehot.astype(jnp.bfloat16), embed, preferred_element_type=jnp.float32)
    tiny = jnp.concatenate([norm_gain.astype(jnp.float32), jnp.sum(stream * stream, axis=1)])
    tiny = tiny.reshape(-1, LANES)
    tiny = lax.all_to_all(
        jnp.broadcast_to(tiny[None], (owners, *tiny.shape)), "tensor", 0, 0, tiled=True
    )
    lag_taps = gathered_taps(filters)
    streams = spread(after(stream.astype(jnp.bfloat16), (lag_taps[0][2][0], tiny)))

    def spot_at(back):
        return jnp.stack([(outer + back) % outer_size, inner]).astype(jnp.int32)

    owner_grid = owner.reshape(owners, halves, rows)
    arrived = lax.dynamic_index_in_dim(owner_grid, half, 1, keepdims=False) - half * seqs
    seq_index = jnp.arange(seqs, dtype=jnp.int32)
    own = lax.dynamic_index_in_dim(arrived, mine, 0, keepdims=False)
    row_lengths = jnp.sum(jnp.where(own[:, None] == seq_index[None, :], lengths[None, :], 0), axis=1)
    row_lengths = jnp.broadcast_to(row_lengths[:, None], (rows, LANES))
    step_index = jnp.arange(steps, dtype=jnp.int32)
    place = (
        (step_index[:, None, None, None, None] == step_index[None, None, None, :, None])
        & (seq_index[None, :, None, None, None] == arrived[None, None, :, None, :])
    ).reshape(tokens, owners * steps * rows)
    place = place.astype(jnp.bfloat16)

    cache = cache_rows.transpose(1, 0, 2)
    def history_part(part, after_these, earlier):
        place_at, first, parts = part
        if after_these is not None:
            parts = [after(parts[0], after_these), *parts[1:]]
        spot = jnp.stack([jnp.int32(place_at), jnp.int32(first)])
        return history_terms(cache, parts, row_lengths, spot, steps, earlier)

    first_terms = history_part(lag_taps[0], None, None)
    near_taps = filters[:, : 2 * steps].T.astype(jnp.float32)
    tiny = after(tiny, (first_terms, place, near_taps))
    gain_rows = channels // LANES
    gains = tiny[:, :gain_rows].reshape(owners, channels)
    inv_rms = lax.rsqrt(jnp.sum(tiny[:, gain_rows:], axis=0).reshape(tokens) / D + EPSILON)
    inv_rms = jnp.broadcast_to(inv_rms[:, None], (tokens, LANES))

    at, *pair = streams[0]
    pair[0] = after(pair[0], first_terms)
    sums = projected(spot_at(-at), pair, gains, inv_rms, w_in, None)
    terms = first_terms
    for part in lag_taps[1:]:
        terms = history_part(part, (sums, streams[1][1]), terms)
    sent = lax.all_to_all(terms, "tensor", 0, 0, tiled=True)
    sent = sent.reshape(owners * steps * rows, channels)
    for index in range(1, len(streams)):
        at, *pair = streams[index]
        if index == 1:
            pair[0] = after(pair[0], (terms, streams[-1][1]))
        ends = (steps, near_taps, place, sent) if index == len(streams) - 1 else None
        sums = projected(spot_at(-at), pair, gains, inv_rms, w_in, sums, ends)
    gated = sums

    def owner_at(ahead, flip):
        return (outer + ahead) % outer_size * INNER + (inner + flip) % INNER

    order = sorted(range(outer_size), key=lambda ahead: (ahead == 0, -min(ahead, outer_size - ahead)))
    targets = [(owner_at(ahead, 1), jnp.bfloat16) for ahead in order]
    targets += [(owner_at(ahead, 0), jnp.float32) for ahead in order]
    shares = output_shares(targets, gated, w_out, owners)
    across = [moved(share, 0, 1) for share in shares[:outer_size]]
    out = stream
    for ahead, own_share, arrived_share in zip(order, shares[outer_size:], across):
        share = own_share + arrived_share.astype(jnp.float32)
        if ahead:
            share = share.astype(jnp.bfloat16)
        out = out + (moved(share, ahead, 0) if ahead else share).astype(jnp.float32)
    return out.astype(jnp.bfloat16).reshape(steps, seqs, channels)


def solution(mesh):
    in_specs = (
        P(None, ("groups", "batch")),
        P(None, "tensor"),
        P("tensor"),
        P(None, "tensor"),
        P("tensor", None),
        P("tensor", None),
        P(("groups", "tensor", "batch"), None, None),
        P("groups"),
        P(("groups", "batch")),
    )
    out_specs = P(None, ("groups", "batch"), "tensor")
    return jax.shard_map(
        per_device, mesh=mesh, in_specs=in_specs, out_specs=out_specs, check_vma=False
    )
```

```python
import functools

import jax
import jax.numpy as jnp
from jax import lax
from jax.experimental import pallas as pl
from jax.experimental.pallas import tpu as pltpu
from jax.sharding import PartitionSpec as P

D = 8192
EPSILON = 1e-05
LANES = 128
INNER = 2
DEPTH = 3
VMEM_LIMIT = 16 * 1024 * 1024
IN_SMEM = pl.BlockSpec(memory_space=pltpu.SMEM)
IN_VMEM = pl.BlockSpec(memory_space=pltpu.VMEM)
IN_HBM = pl.BlockSpec(memory_space=pltpu.HBM)


def moved(array, outer_by, flip):
    owners = lax.axis_size("tensor")
    outer_size = owners // INNER
    pairs = []
    for source in range(owners):
        outer, inner = source // INNER, source % INNER
        pairs.append((source, (outer + outer_by) % outer_size * INNER + (inner ^ flip)))
    return lax.ppermute(array, "tensor", pairs)


def spread(block):
    outer_size = lax.axis_size("tensor") // INNER
    forward = backward = block
    blocks = [(0, block, moved(block, 0, 1))]
    for step in range(1, outer_size // 2 + 1):
        forward = moved(forward, 1, 0)
        blocks.append((step, forward, moved(forward, 0, 1)))
        if step < outer_size - step:
            backward = moved(backward, -1, 0)
            blocks.append((-step, backward, moved(backward, 0, 1)))
    return blocks


def kernel_call(kernel, name, spot, operands, outputs, aliases, scratch, flops, moved_bytes):
    specs, args = zip(*operands)
    args = [
        pltpu.with_memory_space_constraint(arg, pltpu.HBM) if spec is IN_HBM else arg
        for spec, arg in operands
    ]
    out_specs, out_shape = zip(*outputs)
    return pl.pallas_call(
        kernel,
        in_specs=[IN_SMEM, *specs],
        out_specs=list(out_specs),
        out_shape=list(out_shape),
        input_output_aliases=aliases,
        scratch_shapes=scratch,
        compiler_params=pltpu.CompilerParams(vmem_limit_bytes=VMEM_LIMIT),
        cost_estimate=pl.CostEstimate(flops=flops, bytes_accessed=moved_bytes, transcendentals=0),
        name=name,
    )(spot, *args)


def history_kernel(steps, first, spot, lengths_ref, near_ref, far_ref, cache_hbm, *refs):
    terms_ref, held, taps_scr, sems = refs if first else refs[1:]
    if not first:
        terms_ref[...] = refs[0][...]
    _, lags, rows, width = held.shape
    channels = near_ref.shape[1]
    parts = channels // width
    lengths = jnp.concatenate([lengths_ref[...]] * (width // LANES), axis=1)

    def owner_of(flip):
        return spot[0] * INNER + (spot[1] + flip) % INNER

    def fetch(index):
        start = (owner_of(index // parts) * parts + index % parts) * width
        columns = pl.ds(pl.multiple_of(start, width), width)
        return pltpu.make_async_copy(cache_hbm.at[:, :, columns], held.at[index], sems.at[index])

    for index in range(2 * parts):
        fetch(index).start()

    def one_part(index, carry):
        fetch(index).wait()
        flip = index // parts
        at = pl.ds(pl.multiple_of(index % parts * width, width), width)

        @pl.when(flip == 0)
        def _():
            taps_scr[...] = near_ref[pl.ds(0, lags + 1), at].astype(jnp.float32)

        @pl.when(flip == 1)
        def _():
            taps_scr[...] = far_ref[pl.ds(0, lags + 1), at].astype(jnp.float32)

        def tap(lag):
            return jnp.broadcast_to(taps_scr[pl.ds(lag, 1), :], (rows, width))

        taps = [tap(1 + step) for step in range(steps)]
        sums = [jnp.zeros((rows, width), jnp.float32) for _ in range(steps)]
        for lag in range(lags):
            values = jnp.where(lengths > lag, held[index, lag].astype(jnp.float32), 0.0)
            for step in range(min(steps, lags - lag)):
                sums[step] += values * taps[step]
            taps = taps[1:]
            if lag + 1 + steps <= lags:
                taps.append(tap(lag + 1 + steps))
        for step in range(steps):
            terms_ref[owner_of(flip), step, :, at] = sums[step].astype(terms_ref.dtype)
        return carry

    lax.fori_loop(0, 2 * parts, one_part, 0)


def history_terms(cache, near, far, lengths, spot, steps, earlier):
    lags, rows, total = cache.shape
    channels = near.shape[1]
    width = min(4 * LANES, channels)
    count = 2 * channels // width
    operands = [(IN_VMEM, lengths), (IN_VMEM, near), (IN_VMEM, far), (IN_HBM, cache)]
    aliases = {}
    if earlier is not None:
        aliases = {len(operands) + 1: 0}
        operands.append((IN_VMEM, earlier))
    shape = (total // channels, steps, rows, channels)
    return kernel_call(
        functools.partial(history_kernel, steps, earlier is None),
        "history_terms",
        spot,
        operands,
        [(IN_VMEM, jax.ShapeDtypeStruct(shape, jnp.bfloat16))],
        aliases,
        [
            pltpu.VMEM((count, lags, rows, width), jnp.bfloat16),
            pltpu.VMEM((lags + 1, width), jnp.float32),
            pltpu.SemaphoreType.DMA((count,)),
        ],
        2400 * steps * rows * lags * channels // 2,
        4 * rows * lags * channels,
    )[0]


def project_kernel(steps, first, last, spot, near, far, gain_ref, inv_ref, w_hbm, *refs):
    refs = list(refs)
    earlier = None if first else refs.pop(0)
    taps_ref, place_ref, terms_any = (refs.pop(0) for _ in range(3)) if last else (None,) * 3
    total_ref = refs.pop(0)
    gated_ref = refs.pop(0) if last else None
    blocks, normed, held, sems, block_sems, extra_sem, *terms_scr = refs
    _, rows, channels = blocks.shape
    slots, depth, block = held.shape
    chunks = 3 * channels // block
    in_rows = pl.ds(pl.multiple_of(spot[0] * depth, depth), depth)

    def fetch(chunk):
        columns = pl.ds(pl.multiple_of(chunk * block, block), block)
        slot = lax.rem(chunk, slots)
        return pltpu.make_async_copy(w_hbm.at[in_rows, columns], held.at[slot], sems.at[slot])

    copies = [
        pltpu.make_async_copy(x_any, blocks.at[flip], block_sems.at[flip])
        for flip, x_any in enumerate((near, far))
    ]
    for copy in copies:
        copy.start()
    for chunk in range(min(slots, chunks)):
        fetch(chunk).start()
    if last:
        extra = pltpu.make_async_copy(terms_any, terms_scr[0], extra_sem.at[0])
        extra.start()

    scale = inv_ref[:, :1]
    for flip, copy in enumerate(copies):
        copy.wait()
        inner = (spot[1] + flip) % INNER
        gain = gain_ref[pl.ds(spot[0] * INNER + inner, 1), :]
        normed[:, pl.ds(pl.multiple_of(inner * channels, channels), channels)] = (
            blocks[flip].astype(jnp.float32) * scale * gain
        ).astype(jnp.bfloat16)

    def one_chunk(chunk, carry):
        fetch(chunk).wait()
        columns = pl.ds(pl.multiple_of(chunk * block, block), block)
        term = jnp.dot(
            normed[...], held[lax.rem(chunk, slots)], preferred_element_type=jnp.float32
        )
        total_ref[:, columns] = term if first else earlier[:, columns] + term

        @pl.when(chunk + slots < chunks)
        def _():
            fetch(chunk + slots).start()

        return carry

    lax.fori_loop(0, chunks, one_chunk, 0)
    if not last:
        return
    extra.wait()
    seqs = rows // steps
    wide = min(256, channels)

    def one_gate(chunk, carry):
        start = pl.multiple_of(chunk * wide, wide)
        at = pl.ds(start, wide)
        history = jnp.dot(place_ref[...], terms_scr[0][:, at], preferred_element_type=jnp.float32)
        keys = total_ref[:, pl.ds(pl.multiple_of(channels + start, wide), wide)]
        values = total_ref[:, pl.ds(pl.multiple_of(2 * channels + start, wide), wide)]
        recent = (keys * values).astype(jnp.bfloat16).astype(jnp.float32)
        for step in range(steps):
            rows_at = pl.ds(step * seqs, seqs)
            filtered = history[step * seqs : (step + 1) * seqs]
            for back in range(step + 1):
                older = recent[(step - back) * seqs : (step - back + 1) * seqs]
                filtered += taps_ref[pl.ds(back, 1), at] * older
            gated_ref[rows_at, at] = (total_ref[rows_at, at] * filtered).astype(jnp.bfloat16)
        return carry

    lax.fori_loop(0, channels // wide, one_gate, 0)


def projected(spot, pair, gains, inv_rms, w_in, earlier, ends=None):
    near, far = pair
    rows, channels = near.shape
    block = min(512, channels)
    first, last = earlier is None, ends is not None
    operands = [(IN_HBM, near), (IN_HBM, far), (IN_VMEM, gains), (IN_VMEM, inv_rms), (IN_HBM, w_in)]
    aliases = {}
    if not first:
        aliases = {len(operands) + 1: 0}
        operands.append((IN_VMEM, earlier))
    outputs = [(IN_VMEM, jax.ShapeDtypeStruct((rows, 3 * channels), jnp.float32))]
    scratch = [
        pltpu.VMEM((INNER, rows, channels), jnp.bfloat16),
        pltpu.VMEM((rows, INNER * channels), jnp.bfloat16),
        pltpu.VMEM((DEPTH, INNER * channels, block), jnp.bfloat16),
        pltpu.SemaphoreType.DMA((DEPTH,)),
        pltpu.SemaphoreType.DMA((INNER,)),
        pltpu.SemaphoreType.DMA((1,)),
    ]
    steps = 1
    if last:
        steps, taps, place, terms = ends
        operands += [(IN_VMEM, taps), (IN_VMEM, place), (IN_HBM, terms)]
        outputs.append((IN_VMEM, jax.ShapeDtypeStruct((rows, channels), jnp.bfloat16)))
        scratch.append(pltpu.VMEM(terms.shape, jnp.bfloat16))
    return kernel_call(
        functools.partial(project_kernel, steps, first, last),
        "gated_rows" if last else "projected_part",
        spot,
        operands,
        outputs,
        aliases,
        scratch,
        4 * rows * INNER * channels * 3 * channels,
        4 * INNER * channels * 3 * channels,
    )[-1]


def share_kernel(spot, x_ref, w_hbm, *refs):
    *outs, held, sems = refs
    wide = outs[0].shape[1]
    slots, _, block = held.shape
    parts = wide // block
    chunks = len(outs) * parts

    def fetch(chunk):
        start = pl.multiple_of(spot[chunk // parts] * wide + chunk % parts * block, block)
        slot = chunk % slots
        return pltpu.make_async_copy(w_hbm.at[:, pl.ds(start, block)], held.at[slot], sems.at[slot])

    for chunk in range(min(slots, chunks)):
        fetch(chunk).start()
    for chunk in range(chunks):
        fetch(chunk).wait()
        out_ref = outs[chunk // parts]
        share = jnp.dot(x_ref[...], held[chunk % slots], preferred_element_type=jnp.float32)
        out_ref[:, pl.ds(chunk % parts * block, block)] = share.astype(out_ref.dtype)
        if chunk + slots < chunks:
            fetch(chunk + slots).start()


def output_shares(targets, gated, w_out, owners):
    rows, channels = gated.shape
    wide = w_out.shape[1] // owners
    block = min(512, wide)
    return kernel_call(
        share_kernel,
        "output_shares",
        jnp.stack([which for which, _ in targets]).astype(jnp.int32),
        [(IN_VMEM, gated), (IN_HBM, w_out)],
        [(IN_VMEM, jax.ShapeDtypeStruct((rows, wide), kind)) for _, kind in targets],
        {},
        [pltpu.VMEM((DEPTH, channels, block), jnp.bfloat16), pltpu.SemaphoreType.DMA((DEPTH,))],
        2 * rows * channels * wide * len(targets),
        2 * channels * wide * len(targets),
    )


def after(array, earlier):
    return lax.optimization_barrier((array, earlier))[0]


def per_device(token_ids, embed, norm_gain, w_in, filters, w_out, cache_rows, owner, lengths):
    steps, seqs = token_ids.shape
    vocab, channels = embed.shape
    rows = cache_rows.shape[0]
    tokens = steps * seqs
    owners = lax.axis_size("tensor")
    halves = lax.axis_size("batch")
    mine = lax.axis_index("tensor")
    half = lax.axis_index("batch")
    outer, inner, outer_size = mine // INNER, mine % INNER, owners // INNER

    onehot = token_ids.reshape(-1)[:, None] == jnp.arange(vocab, dtype=jnp.int32)[None, :]
    stream = jnp.dot(onehot.astype(jnp.bfloat16), embed, preferred_element_type=jnp.float32)
    tiny = jnp.concatenate([norm_gain.astype(jnp.float32), jnp.sum(stream * stream, axis=1)])
    tiny = tiny.reshape(-1, LANES)
    tiny = lax.all_to_all(
        jnp.broadcast_to(tiny[None], (owners, *tiny.shape)), "tensor", 0, 0, tiled=True
    )
    own_taps = filters.T
    lag_taps = spread(own_taps)
    streams = spread(after(stream.astype(jnp.bfloat16), own_taps))

    def spot_at(back):
        return jnp.stack([(outer + back) % outer_size, inner]).astype(jnp.int32)

    owner_grid = owner.reshape(owners, halves, rows)
    arrived = lax.dynamic_index_in_dim(owner_grid, half, 1, keepdims=False) - half * seqs
    seq_index = jnp.arange(seqs, dtype=jnp.int32)
    own = lax.dynamic_index_in_dim(arrived, mine, 0, keepdims=False)
    row_lengths = jnp.sum(jnp.where(own[:, None] == seq_index[None, :], lengths[None, :], 0), axis=1)
    row_lengths = jnp.broadcast_to(row_lengths[:, None], (rows, LANES))
    step_index = jnp.arange(steps, dtype=jnp.int32)
    place = (
        (step_index[:, None, None, None, None] == step_index[None, None, None, :, None])
        & (seq_index[None, :, None, None, None] == arrived[None, None, :, None, :])
    ).reshape(tokens, owners * steps * rows)
    place = place.astype(jnp.bfloat16)

    cache = cache_rows.transpose(1, 0, 2)
    first_terms = history_terms(cache, *lag_taps[0][1:], row_lengths, spot_at(0), steps, None)
    near_taps = filters[:, : 2 * steps].T.astype(jnp.float32)
    tiny = after(tiny, (first_terms, place, near_taps))
    gain_rows = channels // LANES
    gains = tiny[:, :gain_rows].reshape(owners, channels)
    inv_rms = lax.rsqrt(jnp.sum(tiny[:, gain_rows:], axis=0).reshape(tokens) / D + EPSILON)
    inv_rms = jnp.broadcast_to(inv_rms[:, None], (tokens, LANES))

    terms, sums = first_terms, None
    parts = len(streams)
    for index, (back, near, far) in enumerate(lag_taps):
        if index:
            near = after(near, sums)
            terms = history_terms(cache, near, far, row_lengths, spot_at(-back), steps, terms)
        if 2 * index < parts:
            at, *pair = streams[index]
            pair[0] = after(pair[0], terms)
            sums = projected(spot_at(-at), pair, gains, inv_rms, w_in, sums)
    terms = lax.all_to_all(terms, "tensor", 0, 0, tiled=True)
    terms = terms.reshape(owners * steps * rows, channels)
    for index in range((parts + 1) // 2, parts):
        at, *pair = streams[index]
        ends = (steps, near_taps, place, terms) if index == parts - 1 else None
        sums = projected(spot_at(-at), pair, gains, inv_rms, w_in, sums, ends)
    gated = sums

    def owner_at(ahead, flip):
        return (outer + ahead) % outer_size * INNER + (inner + flip) % INNER

    order = sorted(range(outer_size), key=lambda ahead: (ahead == 0, -min(ahead, outer_size - ahead)))
    targets = [(owner_at(ahead, 1), jnp.bfloat16) for ahead in order]
    targets += [(owner_at(ahead, 0), jnp.float32) for ahead in order]
    shares = []
    for start in range(0, outer_size, 2):
        shares += output_shares(targets[start : start + 2], gated, w_out, owners)
    across = [moved(share, 0, 1) for share in shares]
    shares += output_shares(targets[outer_size:], gated, w_out, owners)
    out = stream
    for ahead, own_share, arrived_share in zip(order, shares[outer_size:], across):
        share = own_share + arrived_share.astype(jnp.float32)
        if ahead:
            share = share.astype(jnp.bfloat16)
        out = out + (moved(share, ahead, 0) if ahead else share).astype(jnp.float32)
    return out.astype(jnp.bfloat16).reshape(steps, seqs, channels)


def solution(mesh):
    in_specs = (
        P(None, ("groups", "batch")),
        P(None, "tensor"),
        P("tensor"),
        P(None, "tensor"),
        P("tensor", None),
        P("tensor", None),
        P(("groups", "tensor", "batch"), None, None),
        P("groups"),
        P(("groups", "batch")),
    )
    out_specs = P(None, ("groups", "batch"), "tensor")
    return jax.shard_map(
        per_device, mesh=mesh, in_specs=in_specs, out_specs=out_specs, check_vma=False
    )
```

```python
import functools

import jax
import jax.numpy as jnp
from jax import lax
from jax.experimental import pallas as pl
from jax.experimental.pallas import tpu as pltpu
from jax.sharding import PartitionSpec as P

D = 8192
EPSILON = 1e-05
LANES = 128
INNER = 2
DEPTH = 3
VMEM_LIMIT = 16 * 1024 * 1024
IN_SMEM = pl.BlockSpec(memory_space=pltpu.SMEM)
IN_VMEM = pl.BlockSpec(memory_space=pltpu.VMEM)
IN_HBM = pl.BlockSpec(memory_space=pltpu.HBM)


def moved(array, outer_by, flip):
    owners = lax.axis_size("tensor")
    outer_size = owners // INNER
    pairs = []
    for source in range(owners):
        outer, inner = source // INNER, source % INNER
        pairs.append((source, (outer + outer_by) % outer_size * INNER + (inner ^ flip)))
    return lax.ppermute(array, "tensor", pairs)


def spread(block):
    outer_size = lax.axis_size("tensor") // INNER
    forward = backward = block
    blocks = [(0, block, moved(block, 0, 1))]
    for step in range(1, outer_size // 2 + 1):
        forward = moved(forward, 1, 0)
        blocks.append((step, forward, moved(forward, 0, 1)))
        if step < outer_size - step:
            backward = moved(backward, -1, 0)
            blocks.append((-step, backward, moved(backward, 0, 1)))
    return blocks


def kernel_call(kernel, name, spot, operands, outputs, aliases, scratch, flops, moved_bytes):
    specs, args = zip(*operands)
    args = [
        pltpu.with_memory_space_constraint(arg, pltpu.HBM) if spec is IN_HBM else arg
        for spec, arg in operands
    ]
    out_specs, out_shape = zip(*outputs)
    return pl.pallas_call(
        kernel,
        in_specs=[IN_SMEM, *specs],
        out_specs=list(out_specs),
        out_shape=list(out_shape),
        input_output_aliases=aliases,
        scratch_shapes=scratch,
        compiler_params=pltpu.CompilerParams(vmem_limit_bytes=VMEM_LIMIT),
        cost_estimate=pl.CostEstimate(flops=flops, bytes_accessed=moved_bytes, transcendentals=0),
        name=name,
    )(spot, *args)


def history_kernel(steps, first, spot, lengths_ref, near_ref, far_ref, cache_hbm, *refs):
    terms_ref, held, taps_scr, sems = refs if first else refs[1:]
    if not first:
        terms_ref[...] = refs[0][...]
    _, lags, rows, width = held.shape
    channels = near_ref.shape[1]
    parts = channels // width
    lengths = jnp.concatenate([lengths_ref[...]] * (width // LANES), axis=1)

    def owner_of(flip):
        return spot[0] * INNER + (spot[1] + flip) % INNER

    def fetch(index):
        start = (owner_of(index // parts) * parts + index % parts) * width
        columns = pl.ds(pl.multiple_of(start, width), width)
        return pltpu.make_async_copy(cache_hbm.at[:, :, columns], held.at[index], sems.at[index])

    for index in range(2 * parts):
        fetch(index).start()

    def one_part(index, carry):
        fetch(index).wait()
        flip = index // parts
        at = pl.ds(pl.multiple_of(index % parts * width, width), width)

        @pl.when(flip == 0)
        def _():
            taps_scr[...] = near_ref[pl.ds(0, lags + 1), at].astype(jnp.float32)

        @pl.when(flip == 1)
        def _():
            taps_scr[...] = far_ref[pl.ds(0, lags + 1), at].astype(jnp.float32)

        def tap(lag):
            return jnp.broadcast_to(taps_scr[pl.ds(lag, 1), :], (rows, width))

        taps = [tap(1 + step) for step in range(steps)]
        sums = [jnp.zeros((rows, width), jnp.float32) for _ in range(steps)]
        for lag in range(lags):
            values = jnp.where(lengths > lag, held[index, lag].astype(jnp.float32), 0.0)
            for step in range(min(steps, lags - lag)):
                sums[step] += values * taps[step]
            taps = taps[1:]
            if lag + 1 + steps <= lags:
                taps.append(tap(lag + 1 + steps))
        for step in range(steps):
            terms_ref[owner_of(flip), step, :, at] = sums[step].astype(terms_ref.dtype)
        return carry

    lax.fori_loop(0, 2 * parts, one_part, 0)


def history_terms(cache, near, far, lengths, spot, steps, earlier):
    lags, rows, total = cache.shape
    channels = near.shape[1]
    width = min(4 * LANES, channels)
    count = 2 * channels // width
    operands = [(IN_VMEM, lengths), (IN_VMEM, near), (IN_VMEM, far), (IN_HBM, cache)]
    aliases = {}
    if earlier is not None:
        aliases = {len(operands) + 1: 0}
        operands.append((IN_VMEM, earlier))
    shape = (total // channels, steps, rows, channels)
    return kernel_call(
        functools.partial(history_kernel, steps, earlier is None),
        "history_terms",
        spot,
        operands,
        [(IN_VMEM, jax.ShapeDtypeStruct(shape, jnp.bfloat16))],
        aliases,
        [
            pltpu.VMEM((count, lags, rows, width), jnp.bfloat16),
            pltpu.VMEM((lags + 1, width), jnp.float32),
            pltpu.SemaphoreType.DMA((count,)),
        ],
        2400 * steps * rows * lags * channels // 2,
        4 * rows * lags * channels,
    )[0]


def project_kernel(steps, first, last, spot, near, far, gain_ref, inv_ref, w_hbm, *refs):
    refs = list(refs)
    earlier = None if first else refs.pop(0)
    taps_ref, place_ref, terms_hbm, out_hbm = (refs.pop(0) for _ in range(4)) if last else (None,) * 4
    total_ref = refs.pop(0)
    gated_ref = refs.pop(0) if last else None
    shares = []
    while last and len(refs) > 9:
        shares.append(refs.pop(0))
    blocks, normed, held, sems, block_sems, *last_scr = refs
    if last:
        terms_ref, out_held, terms_sem, out_sems = last_scr
    _, rows, channels = blocks.shape
    slots, depth, block = held.shape
    chunks = 3 * channels // block
    in_rows = pl.ds(pl.multiple_of(spot[0] * depth, depth), depth)

    def fetch(chunk):
        columns = pl.ds(pl.multiple_of(chunk * block, block), block)
        slot = lax.rem(chunk, slots)
        return pltpu.make_async_copy(w_hbm.at[in_rows, columns], held.at[slot], sems.at[slot])

    copies = [
        pltpu.make_async_copy(x_any, blocks.at[flip], block_sems.at[flip])
        for flip, x_any in enumerate((near, far))
    ]
    for copy in copies:
        copy.start()
    for chunk in range(min(slots, chunks)):
        fetch(chunk).start()
    if last:
        terms_copy = pltpu.make_async_copy(terms_hbm, terms_ref, terms_sem.at[0])
        terms_copy.start()

    def fetch_out(index):
        start = pl.multiple_of(spot[2 + index] * shares[0].shape[1], shares[0].shape[1])
        columns = pl.ds(start, shares[0].shape[1])
        return pltpu.make_async_copy(out_hbm.at[:, columns], out_held.at[index], out_sems.at[index])


    scale = inv_ref[:, :1]
    for flip, copy in enumerate(copies):
        copy.wait()
        inner = (spot[1] + flip) % INNER
        gain = gain_ref[pl.ds(spot[0] * INNER + inner, 1), :]
        normed[:, pl.ds(pl.multiple_of(inner * channels, channels), channels)] = (
            blocks[flip].astype(jnp.float32) * scale * gain
        ).astype(jnp.bfloat16)

    def one_chunk(chunk, carry):
        fetch(chunk).wait()
        columns = pl.ds(pl.multiple_of(chunk * block, block), block)
        term = jnp.dot(
            normed[...], held[lax.rem(chunk, slots)], preferred_element_type=jnp.float32
        )
        total_ref[:, columns] = term if first else earlier[:, columns] + term

        @pl.when(chunk + slots < chunks)
        def _():
            fetch(chunk + slots).start()

        for index in range(len(shares)):

            @pl.when(chunk == index % chunks)
            def _():
                fetch_out(index).start()

        return carry

    lax.fori_loop(0, chunks, one_chunk, 0)
    if not last:
        return
    terms_copy.wait()
    seqs = rows // steps
    wide = min(256, channels)

    def one_gate(chunk, carry):
        start = pl.multiple_of(chunk * wide, wide)
        at = pl.ds(start, wide)
        history = jnp.dot(place_ref[...], terms_ref[:, at], preferred_element_type=jnp.float32)
        keys = total_ref[:, pl.ds(pl.multiple_of(channels + start, wide), wide)]
        values = total_ref[:, pl.ds(pl.multiple_of(2 * channels + start, wide), wide)]
        recent = (keys * values).astype(jnp.bfloat16).astype(jnp.float32)
        for step in range(steps):
            rows_at = pl.ds(step * seqs, seqs)
            filtered = history[step * seqs : (step + 1) * seqs]
            for back in range(step + 1):
                older = recent[(step - back) * seqs : (step - back + 1) * seqs]
                filtered += taps_ref[pl.ds(back, 1), at] * older
            gated_ref[rows_at, at] = (total_ref[rows_at, at] * filtered).astype(jnp.bfloat16)
        return carry

    lax.fori_loop(0, channels // wide, one_gate, 0)
    for index, share_ref in enumerate(shares):
        fetch_out(index).wait()
        width = share_ref.shape[1]
        for start in range(0, width, block):
            columns = pl.ds(start, min(block, width))
            share = jnp.dot(
                gated_ref[...], out_held[index, :, columns], preferred_element_type=jnp.float32
            )
            share_ref[:, columns] = share.astype(share_ref.dtype)


def projected(spot, pair, gains, inv_rms, w_in, earlier, ends=None):
    near, far = pair
    rows, channels = near.shape
    block = min(512, channels)
    first, last = earlier is None, ends is not None
    operands = [(IN_HBM, near), (IN_HBM, far), (IN_VMEM, gains), (IN_VMEM, inv_rms), (IN_HBM, w_in)]
    aliases = {}
    if not first:
        aliases = {len(operands) + 1: 0}
        operands.append((IN_VMEM, earlier))
    outputs = [(IN_VMEM, jax.ShapeDtypeStruct((rows, 3 * channels), jnp.float32))]
    scratch = [
        pltpu.VMEM((INNER, rows, channels), jnp.bfloat16),
        pltpu.VMEM((rows, INNER * channels), jnp.bfloat16),
        pltpu.VMEM((DEPTH, INNER * channels, block), jnp.bfloat16),
        pltpu.SemaphoreType.DMA((DEPTH,)),
        pltpu.SemaphoreType.DMA((INNER,)),
    ]
    steps = 1
    if last:
        steps, taps, place, terms, w_out, targets = ends
        operands += [(IN_VMEM, taps), (IN_VMEM, place), (IN_HBM, terms), (IN_HBM, w_out)]
        outputs.append((IN_VMEM, jax.ShapeDtypeStruct((rows, channels), jnp.bfloat16)))
        wide = w_out.shape[1] * channels // w_in.shape[0]
        outputs += [(IN_VMEM, jax.ShapeDtypeStruct((rows, wide), jnp.bfloat16)) for _ in targets]
        spot = jnp.concatenate([spot, jnp.stack(targets).astype(jnp.int32)])
        scratch += [
            pltpu.VMEM(terms.shape, jnp.bfloat16),
            pltpu.VMEM((len(targets), channels, wide), jnp.bfloat16),
            pltpu.SemaphoreType.DMA((1,)),
            pltpu.SemaphoreType.DMA((len(targets),)),
        ]
    out = kernel_call(
        functools.partial(project_kernel, steps, first, last),
        "gated_rows" if last else "projected_part",
        spot,
        operands,
        outputs,
        aliases,
        scratch,
        4 * rows * INNER * channels * 3 * channels,
        4 * INNER * channels * 3 * channels,
    )
    return out[1:] if last else out[0]


def share_kernel(spot, x_ref, w_hbm, *refs):
    *outs, held, sems = refs
    wide = outs[0].shape[1]
    slots, _, block = held.shape
    parts = wide // block
    chunks = len(outs) * parts

    def fetch(chunk):
        start = pl.multiple_of(spot[chunk // parts] * wide + chunk % parts * block, block)
        slot = chunk % slots
        return pltpu.make_async_copy(w_hbm.at[:, pl.ds(start, block)], held.at[slot], sems.at[slot])

    for chunk in range(min(slots, chunks)):
        fetch(chunk).start()
    for chunk in range(chunks):
        fetch(chunk).wait()
        out_ref = outs[chunk // parts]
        share = jnp.dot(x_ref[...], held[chunk % slots], preferred_element_type=jnp.float32)
        out_ref[:, pl.ds(chunk % parts * block, block)] = share.astype(out_ref.dtype)
        if chunk + slots < chunks:
            fetch(chunk + slots).start()


def output_shares(targets, gated, w_out, owners):
    rows, channels = gated.shape
    wide = w_out.shape[1] // owners
    block = min(512, wide)
    return kernel_call(
        share_kernel,
        "output_shares",
        jnp.stack([which for which, _ in targets]).astype(jnp.int32),
        [(IN_VMEM, gated), (IN_HBM, w_out)],
        [(IN_VMEM, jax.ShapeDtypeStruct((rows, wide), kind)) for _, kind in targets],
        {},
        [pltpu.VMEM((DEPTH, channels, block), jnp.bfloat16), pltpu.SemaphoreType.DMA((DEPTH,))],
        2 * rows * channels * wide * len(targets),
        2 * channels * wide * len(targets),
    )


def after(array, earlier):
    return lax.optimization_barrier((array, earlier))[0]


def per_device(token_ids, embed, norm_gain, w_in, filters, w_out, cache_rows, owner, lengths):
    steps, seqs = token_ids.shape
    vocab, channels = embed.shape
    rows = cache_rows.shape[0]
    tokens = steps * seqs
    owners = lax.axis_size("tensor")
    halves = lax.axis_size("batch")
    mine = lax.axis_index("tensor")
    half = lax.axis_index("batch")
    outer, inner, outer_size = mine // INNER, mine % INNER, owners // INNER

    onehot = token_ids.reshape(-1)[:, None] == jnp.arange(vocab, dtype=jnp.int32)[None, :]
    stream = jnp.dot(onehot.astype(jnp.bfloat16), embed, preferred_element_type=jnp.float32)
    tiny = jnp.concatenate([norm_gain.astype(jnp.float32), jnp.sum(stream * stream, axis=1)])
    tiny = tiny.reshape(-1, LANES)
    tiny = lax.all_to_all(
        jnp.broadcast_to(tiny[None], (owners, *tiny.shape)), "tensor", 0, 0, tiled=True
    )
    own_taps = filters.T
    lag_taps = spread(own_taps)
    streams = spread(after(stream.astype(jnp.bfloat16), own_taps))

    def spot_at(back):
        return jnp.stack([(outer + back) % outer_size, inner]).astype(jnp.int32)

    owner_grid = owner.reshape(owners, halves, rows)
    arrived = lax.dynamic_index_in_dim(owner_grid, half, 1, keepdims=False) - half * seqs
    seq_index = jnp.arange(seqs, dtype=jnp.int32)
    own = lax.dynamic_index_in_dim(arrived, mine, 0, keepdims=False)
    row_lengths = jnp.sum(jnp.where(own[:, None] == seq_index[None, :], lengths[None, :], 0), axis=1)
    row_lengths = jnp.broadcast_to(row_lengths[:, None], (rows, LANES))
    step_index = jnp.arange(steps, dtype=jnp.int32)
    place = (
        (step_index[:, None, None, None, None] == step_index[None, None, None, :, None])
        & (seq_index[None, :, None, None, None] == arrived[None, None, :, None, :])
    ).reshape(tokens, owners * steps * rows)
    place = place.astype(jnp.bfloat16)

    cache = cache_rows.transpose(1, 0, 2)
    first_terms = history_terms(cache, *lag_taps[0][1:], row_lengths, spot_at(0), steps, None)
    near_taps = filters[:, : 2 * steps].T.astype(jnp.float32)
    tiny = after(tiny, (first_terms, place, near_taps))
    gain_rows = channels // LANES
    gains = tiny[:, :gain_rows].reshape(owners, channels)
    inv_rms = lax.rsqrt(jnp.sum(tiny[:, gain_rows:], axis=0).reshape(tokens) / D + EPSILON)
    inv_rms = jnp.broadcast_to(inv_rms[:, None], (tokens, LANES))

    def owner_at(ahead, flip):
        return (outer + ahead) % outer_size * INNER + (inner + flip) % INNER

    order = sorted(range(outer_size), key=lambda ahead: (ahead == 0, -min(ahead, outer_size - ahead)))
    targets = [(owner_at(ahead, 1), jnp.bfloat16) for ahead in order]
    targets += [(owner_at(ahead, 0), jnp.float32) for ahead in order]
    terms, sums = first_terms, None
    parts = len(streams)
    for index, (back, near, far) in enumerate(lag_taps):
        if index:
            near = after(near, sums)
            terms = history_terms(cache, near, far, row_lengths, spot_at(-back), steps, terms)
        if 2 * index < parts:
            at, *pair = streams[index]
            pair[0] = after(pair[0], terms)
            sums = projected(spot_at(-at), pair, gains, inv_rms, w_in, sums)
    terms = lax.all_to_all(terms, "tensor", 0, 0, tiled=True)
    terms = terms.reshape(owners * steps * rows, channels)
    for index in range((parts + 1) // 2, parts):
        at, *pair = streams[index]
        ends = None
        if index == parts - 1:
            ends = (steps, near_taps, place, terms, w_out, [which for which, _ in targets[:2]])
        sums = projected(spot_at(-at), pair, gains, inv_rms, w_in, sums, ends)
    gated, *shares = sums

    for start in range(2, outer_size, 2):
        shares += output_shares(targets[start : start + 2], gated, w_out, owners)
    across = [moved(share, 0, 1) for share in shares]
    shares += output_shares(targets[outer_size:], gated, w_out, owners)
    out = stream
    for ahead, own_share, arrived_share in zip(order, shares[outer_size:], across):
        share = own_share + arrived_share.astype(jnp.float32)
        if ahead:
            share = share.astype(jnp.bfloat16)
        out = out + (moved(share, ahead, 0) if ahead else share).astype(jnp.float32)
    return out.astype(jnp.bfloat16).reshape(steps, seqs, channels)


def solution(mesh):
    in_specs = (
        P(None, ("groups", "batch")),
        P(None, "tensor"),
        P("tensor"),
        P(None, "tensor"),
        P("tensor", None),
        P("tensor", None),
        P(("groups", "tensor", "batch"), None, None),
        P("groups"),
        P(("groups", "batch")),
    )
    out_specs = P(None, ("groups", "batch"), "tensor")
    return jax.shard_map(
        per_device, mesh=mesh, in_specs=in_specs, out_specs=out_specs, check_vma=False
    )
```

```python
import functools

import jax
import jax.numpy as jnp
from jax import lax
from jax.experimental import pallas as pl
from jax.experimental.pallas import tpu as pltpu
from jax.sharding import PartitionSpec as P

D = 8192
EPSILON = 1e-05
LANES = 128
INNER = 2
DEPTH = 3
VMEM_LIMIT = 16 * 1024 * 1024
IN_SMEM = pl.BlockSpec(memory_space=pltpu.SMEM)
IN_VMEM = pl.BlockSpec(memory_space=pltpu.VMEM)
IN_HBM = pl.BlockSpec(memory_space=pltpu.HBM)


def moved(array, outer_by, flip):
    owners = lax.axis_size("tensor")
    outer_size = owners // INNER
    pairs = []
    for source in range(owners):
        outer, inner = source // INNER, source % INNER
        pairs.append((source, (outer + outer_by) % outer_size * INNER + (inner ^ flip)))
    return lax.ppermute(array, "tensor", pairs)


def spread(block):
    outer_size = lax.axis_size("tensor") // INNER
    forward = backward = block
    blocks = [(0, block, moved(block, 0, 1))]
    for step in range(1, outer_size // 2 + 1):
        forward = moved(forward, 1, 0)
        blocks.append((step, forward, moved(forward, 0, 1)))
        if step < outer_size - step:
            backward = moved(backward, -1, 0)
            blocks.append((-step, backward, moved(backward, 0, 1)))
    return blocks


def kernel_call(kernel, name, spot, operands, outputs, aliases, scratch, flops, moved_bytes):
    specs, args = zip(*operands)
    args = [
        pltpu.with_memory_space_constraint(arg, pltpu.HBM) if spec is IN_HBM else arg
        for spec, arg in operands
    ]
    out_specs, out_shape = zip(*outputs)
    return pl.pallas_call(
        kernel,
        in_specs=[IN_SMEM, *specs],
        out_specs=list(out_specs),
        out_shape=list(out_shape),
        input_output_aliases=aliases,
        scratch_shapes=scratch,
        compiler_params=pltpu.CompilerParams(vmem_limit_bytes=VMEM_LIMIT),
        cost_estimate=pl.CostEstimate(flops=flops, bytes_accessed=moved_bytes, transcendentals=0),
        name=name,
    )(spot, *args)


def history_kernel(steps, first, spot, lengths_ref, near_ref, far_ref, cache_hbm, *refs):
    terms_ref, held, taps_scr, sems = refs if first else refs[1:]
    if not first:
        terms_ref[...] = refs[0][...]
    _, lags, rows, width = held.shape
    channels = near_ref.shape[1]
    parts = channels // width
    lengths = jnp.concatenate([lengths_ref[...]] * (width // LANES), axis=1)

    def owner_of(flip):
        return spot[0] * INNER + (spot[1] + flip) % INNER

    def fetch(index):
        start = (owner_of(index // parts) * parts + index % parts) * width
        columns = pl.ds(pl.multiple_of(start, width), width)
        return pltpu.make_async_copy(cache_hbm.at[:, :, columns], held.at[index], sems.at[index])

    for index in range(2 * parts):
        fetch(index).start()

    def one_part(index, carry):
        fetch(index).wait()
        flip = index // parts
        at = pl.ds(pl.multiple_of(index % parts * width, width), width)

        @pl.when(flip == 0)
        def _():
            taps_scr[...] = near_ref[pl.ds(0, lags + 1), at].astype(jnp.float32)

        @pl.when(flip == 1)
        def _():
            taps_scr[...] = far_ref[pl.ds(0, lags + 1), at].astype(jnp.float32)

        def tap(lag):
            return jnp.broadcast_to(taps_scr[pl.ds(lag, 1), :], (rows, width))

        taps = [tap(1 + step) for step in range(steps)]
        sums = [jnp.zeros((rows, width), jnp.float32) for _ in range(steps)]
        for lag in range(lags):
            values = jnp.where(lengths > lag, held[index, lag].astype(jnp.float32), 0.0)
            for step in range(min(steps, lags - lag)):
                sums[step] += values * taps[step]
            taps = taps[1:]
            if lag + 1 + steps <= lags:
                taps.append(tap(lag + 1 + steps))
        for step in range(steps):
            terms_ref[owner_of(flip), step, :, at] = sums[step].astype(terms_ref.dtype)
        return carry

    lax.fori_loop(0, 2 * parts, one_part, 0)


def history_terms(cache, near, far, lengths, spot, steps, earlier):
    lags, rows, total = cache.shape
    channels = near.shape[1]
    width = min(4 * LANES, channels)
    count = 2 * channels // width
    operands = [(IN_VMEM, lengths), (IN_VMEM, near), (IN_VMEM, far), (IN_HBM, cache)]
    aliases = {}
    if earlier is not None:
        aliases = {len(operands) + 1: 0}
        operands.append((IN_VMEM, earlier))
    shape = (total // channels, steps, rows, channels)
    return kernel_call(
        functools.partial(history_kernel, steps, earlier is None),
        "history_terms",
        spot,
        operands,
        [(IN_VMEM, jax.ShapeDtypeStruct(shape, jnp.bfloat16))],
        aliases,
        [
            pltpu.VMEM((count, lags, rows, width), jnp.bfloat16),
            pltpu.VMEM((lags + 1, width), jnp.float32),
            pltpu.SemaphoreType.DMA((count,)),
        ],
        2400 * steps * rows * lags * channels // 2,
        4 * rows * lags * channels,
    )[0]


def project_kernel(steps, first, last, spot, near, far, gain_ref, inv_ref, w_hbm, *refs):
    refs = list(refs)
    earlier = None if first else refs.pop(0)
    taps_ref, place_ref, terms_hbm, out_hbm = (refs.pop(0) for _ in range(4)) if last else (None,) * 4
    total_ref = refs.pop(0)
    gated_ref = refs.pop(0) if last else None
    shares = []
    while last and len(refs) > 9:
        shares.append(refs.pop(0))
    blocks, normed, held, sems, block_sems, *last_scr = refs
    if last:
        terms_ref, out_held, terms_sem, out_sems = last_scr
    _, rows, channels = blocks.shape
    slots, depth, block = held.shape
    chunks = 3 * channels // block
    in_rows = pl.ds(pl.multiple_of(spot[0] * depth, depth), depth)

    def fetch(chunk):
        columns = pl.ds(pl.multiple_of(chunk * block, block), block)
        slot = lax.rem(chunk, slots)
        return pltpu.make_async_copy(w_hbm.at[in_rows, columns], held.at[slot], sems.at[slot])

    copies = [
        pltpu.make_async_copy(x_any, blocks.at[flip], block_sems.at[flip])
        for flip, x_any in enumerate((near, far))
    ]
    for copy in copies:
        copy.start()
    for chunk in range(min(slots, chunks)):
        fetch(chunk).start()
    if last:
        terms_copy = pltpu.make_async_copy(terms_hbm, terms_ref, terms_sem.at[0])
        terms_copy.start()

    def fetch_out(index):
        start = pl.multiple_of(spot[2 + index] * shares[0].shape[1], shares[0].shape[1])
        columns = pl.ds(start, shares[0].shape[1])
        return pltpu.make_async_copy(out_hbm.at[:, columns], out_held.at[index], out_sems.at[index])


    scale = inv_ref[:, :1]
    for flip, copy in enumerate(copies):
        copy.wait()
        inner = (spot[1] + flip) % INNER
        gain = gain_ref[pl.ds(spot[0] * INNER + inner, 1), :]
        normed[:, pl.ds(pl.multiple_of(inner * channels, channels), channels)] = (
            blocks[flip].astype(jnp.float32) * scale * gain
        ).astype(jnp.bfloat16)

    def one_chunk(chunk, carry):
        fetch(chunk).wait()
        columns = pl.ds(pl.multiple_of(chunk * block, block), block)
        term = jnp.dot(
            normed[...], held[lax.rem(chunk, slots)], preferred_element_type=jnp.float32
        )
        total_ref[:, columns] = term if first else earlier[:, columns] + term

        @pl.when(chunk + slots < chunks)
        def _():
            fetch(chunk + slots).start()

        for index in range(len(shares)):

            @pl.when(chunk == index % chunks)
            def _():
                fetch_out(index).start()

        return carry

    lax.fori_loop(0, chunks, one_chunk, 0)
    if not last:
        return
    terms_copy.wait()
    seqs = rows // steps
    wide = min(256, channels)

    def one_gate(chunk, carry):
        start = pl.multiple_of(chunk * wide, wide)
        at = pl.ds(start, wide)
        history = jnp.dot(place_ref[...], terms_ref[:, at], preferred_element_type=jnp.float32)
        keys = total_ref[:, pl.ds(pl.multiple_of(channels + start, wide), wide)]
        values = total_ref[:, pl.ds(pl.multiple_of(2 * channels + start, wide), wide)]
        recent = (keys * values).astype(jnp.bfloat16).astype(jnp.float32)
        for step in range(steps):
            rows_at = pl.ds(step * seqs, seqs)
            filtered = history[step * seqs : (step + 1) * seqs]
            for back in range(step + 1):
                older = recent[(step - back) * seqs : (step - back + 1) * seqs]
                filtered += taps_ref[pl.ds(back, 1), at] * older
            gated_ref[rows_at, at] = (total_ref[rows_at, at] * filtered).astype(jnp.bfloat16)
        return carry

    lax.fori_loop(0, channels // wide, one_gate, 0)
    for index, share_ref in enumerate(shares):
        fetch_out(index).wait()
        width = share_ref.shape[1]
        for start in range(0, width, block):
            columns = pl.ds(start, min(block, width))
            share = jnp.dot(
                gated_ref[...], out_held[index, :, columns], preferred_element_type=jnp.float32
            )
            share_ref[:, columns] = share.astype(share_ref.dtype)


def projected(spot, pair, gains, inv_rms, w_in, earlier, ends=None):
    near, far = pair
    rows, channels = near.shape
    block = min(512, channels)
    first, last = earlier is None, ends is not None
    operands = [(IN_HBM, near), (IN_HBM, far), (IN_VMEM, gains), (IN_VMEM, inv_rms), (IN_HBM, w_in)]
    aliases = {}
    if not first:
        aliases = {len(operands) + 1: 0}
        operands.append((IN_VMEM, earlier))
    outputs = [(IN_VMEM, jax.ShapeDtypeStruct((rows, 3 * channels), jnp.float32))]
    scratch = [
        pltpu.VMEM((INNER, rows, channels), jnp.bfloat16),
        pltpu.VMEM((rows, INNER * channels), jnp.bfloat16),
        pltpu.VMEM((DEPTH, INNER * channels, block), jnp.bfloat16),
        pltpu.SemaphoreType.DMA((DEPTH,)),
        pltpu.SemaphoreType.DMA((INNER,)),
    ]
    steps = 1
    if last:
        steps, taps, place, terms, w_out, targets = ends
        operands += [(IN_VMEM, taps), (IN_VMEM, place), (IN_HBM, terms), (IN_HBM, w_out)]
        outputs.append((IN_VMEM, jax.ShapeDtypeStruct((rows, channels), jnp.bfloat16)))
        wide = w_out.shape[1] * channels // w_in.shape[0]
        outputs += [(IN_VMEM, jax.ShapeDtypeStruct((rows, wide), jnp.bfloat16)) for _ in targets]
        spot = jnp.concatenate([spot, jnp.stack(targets).astype(jnp.int32)])
        scratch += [
            pltpu.VMEM(terms.shape, jnp.bfloat16),
            pltpu.VMEM((len(targets), channels, wide), jnp.bfloat16),
            pltpu.SemaphoreType.DMA((1,)),
            pltpu.SemaphoreType.DMA((len(targets),)),
        ]
    out = kernel_call(
        functools.partial(project_kernel, steps, first, last),
        "gated_rows" if last else "projected_part",
        spot,
        operands,
        outputs,
        aliases,
        scratch,
        4 * rows * INNER * channels * 3 * channels,
        4 * INNER * channels * 3 * channels,
    )
    return out[1:] if last else out[0]


def share_kernel(spot, x_ref, w_hbm, *refs):
    *outs, held, sems = refs
    wide = outs[0].shape[1]
    slots, _, block = held.shape
    parts = wide // block
    chunks = len(outs) * parts

    def fetch(chunk):
        start = pl.multiple_of(spot[chunk // parts] * wide + chunk % parts * block, block)
        slot = chunk % slots
        return pltpu.make_async_copy(w_hbm.at[:, pl.ds(start, block)], held.at[slot], sems.at[slot])

    for chunk in range(min(slots, chunks)):
        fetch(chunk).start()
    for chunk in range(chunks):
        fetch(chunk).wait()
        out_ref = outs[chunk // parts]
        share = jnp.dot(x_ref[...], held[chunk % slots], preferred_element_type=jnp.float32)
        out_ref[:, pl.ds(chunk % parts * block, block)] = share.astype(out_ref.dtype)
        if chunk + slots < chunks:
            fetch(chunk + slots).start()


def output_shares(targets, gated, w_out, owners):
    rows, channels = gated.shape
    wide = w_out.shape[1] // owners
    block = min(512, wide)
    return kernel_call(
        share_kernel,
        "output_shares",
        jnp.stack([which for which, _ in targets]).astype(jnp.int32),
        [(IN_VMEM, gated), (IN_HBM, w_out)],
        [(IN_VMEM, jax.ShapeDtypeStruct((rows, wide), kind)) for _, kind in targets],
        {},
        [pltpu.VMEM((DEPTH, channels, block), jnp.bfloat16), pltpu.SemaphoreType.DMA((DEPTH,))],
        2 * rows * channels * wide * len(targets),
        2 * channels * wide * len(targets),
    )


def after(array, earlier):
    return lax.optimization_barrier((array, earlier))[0]


def per_device(token_ids, embed, norm_gain, w_in, filters, w_out, cache_rows, owner, lengths):
    steps, seqs = token_ids.shape
    vocab, channels = embed.shape
    rows = cache_rows.shape[0]
    tokens = steps * seqs
    owners = lax.axis_size("tensor")
    halves = lax.axis_size("batch")
    mine = lax.axis_index("tensor")
    half = lax.axis_index("batch")
    outer, inner, outer_size = mine // INNER, mine % INNER, owners // INNER

    onehot = token_ids.reshape(-1)[:, None] == jnp.arange(vocab, dtype=jnp.int32)[None, :]
    stream = jnp.dot(onehot.astype(jnp.bfloat16), embed, preferred_element_type=jnp.float32)
    tiny = jnp.concatenate([norm_gain.astype(jnp.float32), jnp.sum(stream * stream, axis=1)])
    tiny = tiny.reshape(-1, LANES)
    tiny = lax.all_to_all(
        jnp.broadcast_to(tiny[None], (owners, *tiny.shape)), "tensor", 0, 0, tiled=True
    )
    own_taps = filters.T
    lag_taps = spread(own_taps)
    streams = spread(after(stream.astype(jnp.bfloat16), own_taps))

    def spot_at(back):
        return jnp.stack([(outer + back) % outer_size, inner]).astype(jnp.int32)

    owner_grid = owner.reshape(owners, halves, rows)
    arrived = lax.dynamic_index_in_dim(owner_grid, half, 1, keepdims=False) - half * seqs
    seq_index = jnp.arange(seqs, dtype=jnp.int32)
    own = lax.dynamic_index_in_dim(arrived, mine, 0, keepdims=False)
    row_lengths = jnp.sum(jnp.where(own[:, None] == seq_index[None, :], lengths[None, :], 0), axis=1)
    row_lengths = jnp.broadcast_to(row_lengths[:, None], (rows, LANES))
    step_index = jnp.arange(steps, dtype=jnp.int32)
    place = (
        (step_index[:, None, None, None, None] == step_index[None, None, None, :, None])
        & (seq_index[None, :, None, None, None] == arrived[None, None, :, None, :])
    ).reshape(tokens, owners * steps * rows)
    place = place.astype(jnp.bfloat16)

    cache = cache_rows.transpose(1, 0, 2)
    first_terms = history_terms(cache, *lag_taps[0][1:], row_lengths, spot_at(0), steps, None)
    near_taps = filters[:, : 2 * steps].T.astype(jnp.float32)
    tiny = after(tiny, (first_terms, place, near_taps))
    gain_rows = channels // LANES
    gains = tiny[:, :gain_rows].reshape(owners, channels)
    inv_rms = lax.rsqrt(jnp.sum(tiny[:, gain_rows:], axis=0).reshape(tokens) / D + EPSILON)
    inv_rms = jnp.broadcast_to(inv_rms[:, None], (tokens, LANES))

    def owner_at(ahead, flip):
        return (outer + ahead) % outer_size * INNER + (inner + flip) % INNER

    order = sorted(range(outer_size), key=lambda ahead: (ahead == 0, -min(ahead, outer_size - ahead)))
    targets = [(owner_at(ahead, 1), jnp.bfloat16) for ahead in order]
    targets += [(owner_at(ahead, 0), jnp.float32) for ahead in order]
    terms, sums = first_terms, None
    parts = len(streams)
    for index, (back, near, far) in enumerate(lag_taps):
        if index:
            near = after(near, (sums, streams[-1][1]) if index == parts - 1 else sums)
            terms = history_terms(cache, near, far, row_lengths, spot_at(-back), steps, terms)
        if 2 * index < parts:
            at, *pair = streams[index]
            pair[0] = after(pair[0], terms)
            sums = projected(spot_at(-at), pair, gains, inv_rms, w_in, sums)
    terms = lax.all_to_all(terms, "tensor", 0, 0, tiled=True)
    terms = terms.reshape(owners * steps * rows, channels)
    for index in range((parts + 1) // 2, parts):
        at, *pair = streams[index]
        ends = None
        if index == parts - 1:
            ends = (steps, near_taps, place, terms, w_out, [which for which, _ in targets[:2]])
        sums = projected(spot_at(-at), pair, gains, inv_rms, w_in, sums, ends)
    gated, *shares = sums

    for start in range(2, outer_size, 2):
        shares += output_shares(targets[start : start + 2], gated, w_out, owners)
    across = [moved(share, 0, 1) for share in shares]
    shares += output_shares(targets[outer_size:], gated, w_out, owners)
    out = stream
    for ahead, own_share, arrived_share in zip(order, shares[outer_size:], across):
        share = own_share + arrived_share.astype(jnp.float32)
        if ahead:
            share = share.astype(jnp.bfloat16)
        out = out + (moved(share, ahead, 0) if ahead else share).astype(jnp.float32)
    return out.astype(jnp.bfloat16).reshape(steps, seqs, channels)


def solution(mesh):
    in_specs = (
        P(None, ("groups", "batch")),
        P(None, "tensor"),
        P("tensor"),
        P(None, "tensor"),
        P("tensor", None),
        P("tensor", None),
        P(("groups", "tensor", "batch"), None, None),
        P("groups"),
        P(("groups", "batch")),
    )
    out_specs = P(None, ("groups", "batch"), "tensor")
    return jax.shard_map(
        per_device, mesh=mesh, in_specs=in_specs, out_specs=out_specs, check_vma=False
    )
```
